256 devices in a mesh: dp: 8 (over x_hi, y), ctx: 32 (over z, x_lo, core).
Axes of the slice: x: 4 (x_hi: 2, x_lo: 2; x = x_hi * 2 + x_lo), y: 4, z: 8, core: 2. Of those that a mesh axis runs over, the one named last changes fastest.
Arguments:
- q_nope: bfloat16 [8, 4096, 8192], P('dp', 'ctx'), may hold values from -6 to 6
- q_rope: bfloat16 [8, 4096, 4096], P('dp', 'ctx'), may hold values from -6 to 6
- grad_out: bfloat16 [8, 4096, 8192], P('dp', 'ctx'), may hold values from -6 to 6
- log_total: float32 [8, 64, 4096], P('dp', None, 'ctx'), may hold values from 5 to 6.5
- kv_latent: bfloat16 [8, 4096, 320], P('dp', 'ctx'), may hold values from -6 to 6
- up_weight: bfloat16 [256, 16384], P('ctx'), may hold values from -0.375 to 0.375
- selected: int32 [8, 64, 3], P('dp', 'ctx'), may hold values from -1 to 62, as said below
- offered: int32 [8, 32, 4], P('dp'), may hold values from 0 to 1, as said below
Outputs:
- grad_q_nope: bfloat16 [8, 4096, 8192], P('dp', 'ctx')
- grad_q_rope: bfloat16 [8, 4096, 4096], P('dp', 'ctx')
- grad_latent: float32 [8, 4096, 320], P('dp', 'ctx')
- grad_weight: float32 [256, 16384], P('ctx')
The draws below stay inside these ranges and needn't reach their ends.
Inputs may be any that keep to these rules, and one draw needn't show every extreme that they name: offered[b, s, m] is a block number within group s's 128/64 blocks; in matching m group s offers it to group s + m + 1. `selected`: each list holds distinct global block ids, then -1 entries; every id is an earlier block of the query block's own group or a block offered to that group in one of the four matchings; a query block that is not the first of its group always lists the block just before it.
All inputs are finite; a program needn't handle non-finite values.
Results may differ from the reference program's by a relative error of at most 0.0028.
The reference program's roundings to bfloat16 on the way count: a program that leaves them out, or rounds other values in their place, can miss the bound.
Values may be sent and summed in bfloat16 or wider, within the bound.
A program may use at most 192 MiB of HBM per device.

```python
import jax
import jax.numpy as jnp
from jax import lax

H = 64
LAT = 256
ROPE = 64
NOPE = 128
VDIM = 128
BLOCK = 64
TOPK = 3
TOK_DEV = 128
LENGTH = 4096
BATCH = 8
NQB = 64
N_CTX = 32


partner_offsets = (1, 2, 3, 4)


def build_plan(key):
    per_block = TOK_DEV // BLOCK
    plan_key = jax.random.fold_in(key, 11)
    pick_key = jax.random.fold_in(key, 12)
    offered = jax.random.randint(plan_key, (BATCH, N_CTX, 4), 0, per_block, dtype=jnp.int32)
    offered = offered.at[:, 0, 0].set(0).at[:, 0, 1].set(per_block - 1)
    blocks = jnp.arange(NQB, dtype=jnp.int32)
    group_of = blocks // per_block
    within = blocks % per_block
    earlier = jnp.arange(per_block - 1, dtype=jnp.int32)
    own_ids = group_of[:, None] * per_block + earlier[None, :]
    own_valid = earlier[None, :] < within[:, None]
    own_first = earlier[None, :] == within[:, None] - 1
    offered_ids = []
    offered_valid = []
    for matching, offset in enumerate(partner_offsets):
        source = group_of - offset
        sender = jnp.maximum(source, 0)
        offered_ids.append(sender[None, :] * per_block + offered[:, sender, matching])
        offered_valid.append(jnp.broadcast_to((source >= 0)[None, :], (BATCH, NQB)))
    candidates = jnp.concatenate([jnp.broadcast_to(own_ids[None], (BATCH, NQB, per_block - 1)), jnp.stack(offered_ids, axis=-1)], axis=-1)
    usable = jnp.concatenate([jnp.broadcast_to(own_valid[None], (BATCH, NQB, per_block - 1)), jnp.stack(offered_valid, axis=-1)], axis=-1)
    leading = jnp.concatenate([jnp.broadcast_to(own_first[None], (BATCH, NQB, per_block - 1)), jnp.zeros((BATCH, NQB, 4), dtype=bool)], axis=-1)
    columns = candidates.shape[-1]
    noise_draw = jax.random.randint(pick_key, candidates.shape, 0, 1 << 20, dtype=jnp.int32)
    ranking_key = noise_draw * 64 + jnp.arange(columns, dtype=jnp.int32)
    ranking_key = jnp.where(leading, -1, jnp.where(usable, ranking_key, 1 << 30))
    ranking = jnp.argsort(ranking_key, axis=-1)[..., :TOPK]
    chosen = jnp.take_along_axis(candidates, ranking, axis=-1)
    chosen_valid = jnp.take_along_axis(usable, ranking, axis=-1)
    selected = jnp.where(chosen_valid, chosen, -1).astype(jnp.int32)
    return (offered, selected)


def draw_offered(key, part):
    return build_plan(key)[0]


def draw_selected(key, part):
    return build_plan(key)[1]


def block_levels(key, dims, cuts, low, top_value):
    loudness, own = 1.0, jax.random.fold_in(key, 6)
    for axis_at, shards_of in cuts:
        steps = jnp.exp(jax.random.uniform(jax.random.fold_in(own, axis_at), (shards_of,), jnp.float32, low / len(cuts), top_value / len(cuts)))
        loudness = loudness * jnp.repeat(steps, dims[axis_at] // shards_of).reshape([-1 if axis == axis_at else 1 for axis in range(len(dims))])
    return loudness


def scatter_about(key, shape, spread, limit, cuts=(), held_as=jnp.bfloat16):
    gain = block_levels(key, shape, cuts, -0.22, 0.18) if cuts else 1.0
    entries = jax.random.normal(key, shape, jnp.float32) * spread * gain
    return jnp.minimum(jnp.maximum(entries, -limit), limit).astype(held_as)


def setup_inputs(seed: int = 0) -> dict:
    splits = jax.random.split(jax.random.key(seed), 9)
    q_nope = scatter_about(splits[0], (BATCH, LENGTH, H * NOPE), 1.0, 6.0, ((0, 8), (1, 32)))
    q_rope = scatter_about(splits[1], (BATCH, LENGTH, H * ROPE), 1.0, 6.0, ((0, 8), (1, 32)))
    grad_out = scatter_about(splits[2], (BATCH, LENGTH, H * VDIM), 1.0, 6.0, ((0, 8), (1, 32)))
    log_total = jnp.clip(5.0 + 1.5 * jax.random.uniform(splits[3], (BATCH, H, LENGTH), jnp.float32) ** block_levels(splits[3], (BATCH, H, LENGTH), ((0, 8), (2, 32)), -0.2, 0.2), 5.0, 6.5)
    kv_latent = scatter_about(splits[4], (BATCH, LENGTH, LAT + ROPE), 1.0, 6.0, ((0, 8), (1, 32)))
    up_weight = scatter_about(splits[5], (LAT, H * (NOPE + VDIM)), LAT ** -0.5, 0.375, ((0, 32),))
    selected = draw_selected(jax.random.fold_in(splits[8], 71), 0)
    offered = draw_offered(jax.random.fold_in(splits[8], 71), 0)
    return {"q_nope": q_nope, "q_rope": q_rope, "grad_out": grad_out, "log_total": log_total, "kv_latent": kv_latent, "up_weight": up_weight, "selected": selected, "offered": offered}


partner_offsets = (1, 2, 3, 4)

def allowed_mask(selection, key_ids, first_query):
    query_ids = first_query + jnp.arange(selection.shape[0], dtype=jnp.int32)
    same_block = key_ids[None, :] == query_ids[:, None]
    picked = jnp.any(selection[:, :, None] == key_ids[None, None, :], axis=1) & (key_ids >= 0)[None, :]
    inner = jnp.arange(BLOCK, dtype=jnp.int32)
    causal = inner[:, None] >= inner[None, :]
    block_mask = picked[:, None, :, None] | same_block[:, None, :, None] & causal[None, :, None, :]
    return block_mask.reshape(selection.shape[0] * BLOCK, key_ids.shape[0] * BLOCK)

def head_backward(queries, rope_queries, out_grads, totals, key_part, value_part, rope_keys, allowed):
    softmax_scale = 1.0 / jnp.sqrt(jnp.float32(NOPE + ROPE))
    queries32 = queries.astype(jnp.float32)
    rope32 = rope_queries.astype(jnp.float32)
    grads32 = out_grads.astype(jnp.float32)
    keys32 = key_part.astype(jnp.float32)
    values32 = value_part.astype(jnp.float32)
    ropek32 = rope_keys.astype(jnp.float32)
    scores = (jnp.einsum('qhd,khd->hqk', queries32, keys32) + jnp.einsum('qhd,kd->hqk', rope32, ropek32)) * softmax_scale
    probabilities = jnp.where(allowed[None], jnp.exp(scores - totals[:, :, None]), jnp.float32(0.0))
    prob_grads = jnp.einsum('qhd,khd->hqk', grads32, values32)
    row_dot = lax.optimization_barrier(jnp.sum(probabilities * prob_grads, axis=2, keepdims=True))
    score_grads = (probabilities * (prob_grads - row_dot)).astype(jnp.bfloat16).astype(jnp.float32)
    probs_low = probabilities.astype(jnp.bfloat16).astype(jnp.float32)
    grad_nope = (jnp.einsum('hqk,khd->qhd', score_grads, keys32) * softmax_scale).astype(jnp.bfloat16)
    grad_rope = (jnp.einsum('hqk,kd->qhd', score_grads, ropek32) * softmax_scale).astype(jnp.bfloat16)
    key_grad = jnp.einsum('hqk,qhd->khd', score_grads, queries32) * softmax_scale
    value_grad = jnp.einsum('hqk,qhd->khd', probs_low, grads32)
    both_grads = jnp.concatenate([key_grad, value_grad], axis=2).astype(jnp.bfloat16)
    rope_grad = jnp.einsum('hqk,qhd->kd', score_grads, rope32) * softmax_scale
    return (grad_nope, grad_rope, both_grads, rope_grad)

def group_backward(queries, rope_queries, out_grads, totals, candidates, weight, allowed):
    latent_cols = candidates[:, :LAT]
    rope_keys = candidates[:, LAT:]
    expanded = jnp.dot(latent_cols, weight, preferred_element_type=jnp.float32).astype(jnp.bfloat16)
    query_len = queries.shape[0]
    key_len = candidates.shape[0]
    head_count = totals.shape[0]
    per_group = 8 if head_count % 8 == 0 else head_count
    groups = head_count // per_group

    def regroup(array, width, length):
        return array.reshape(length, groups, per_group, width).transpose(1, 0, 2, 3)
    both_parts = regroup(expanded, NOPE + VDIM, key_len)
    items = (regroup(queries, NOPE, query_len), regroup(rope_queries, ROPE, query_len), regroup(out_grads, VDIM, query_len), totals.reshape(groups, per_group, query_len), both_parts[..., :NOPE], both_parts[..., NOPE:])

    def one_heads(entry):
        return head_backward(entry[0], entry[1], entry[2], entry[3], entry[4], entry[5], rope_keys, allowed)
    results = lax.map(one_heads, items)
    grad_nope = results[0].transpose(1, 0, 2, 3).reshape(query_len, head_count * NOPE)
    grad_rope = results[1].transpose(1, 0, 2, 3).reshape(query_len, head_count * ROPE)
    key_grads = results[2].transpose(1, 0, 2, 3).reshape(key_len, head_count * (NOPE + VDIM))
    rope_part = lax.optimization_barrier(jnp.sum(results[3], axis=0))
    latent_grad = jnp.dot(key_grads, weight.T, preferred_element_type=jnp.float32)
    cand_grad = jnp.concatenate([latent_grad, rope_part], axis=1)
    return (grad_nope, grad_rope, key_grads, cand_grad)

def reference(q_nope, q_rope, grad_out, log_total, kv_latent, up_weight, selected, offered):
    per_block = TOK_DEV // BLOCK

    def one_sequence(weight_sum, inputs):
        queries, rope_queries, out_grads, totals, latent_rows, selection, offer_plan = inputs

        def one_group(state_pair, group_index):
            grad_rows, weight_acc = state_pair
            begin_row = (group_index * TOK_DEV).astype(jnp.int32)
            pieces = [lax.dynamic_slice_in_dim(latent_rows, begin_row, TOK_DEV, 0)]
            piece_ids = [group_index * per_block + jnp.arange(per_block, dtype=jnp.int32)]
            first_rows = []
            usable_list = []
            for matching, offset in enumerate(partner_offsets):
                source = group_index - offset
                usable = source >= 0
                sender = jnp.maximum(source, 0)
                block_index = offer_plan[sender, matching]
                first_row = (sender * TOK_DEV + block_index * BLOCK).astype(jnp.int32)
                block_rows = lax.dynamic_slice_in_dim(latent_rows, first_row, BLOCK, 0)
                pieces.append(jnp.where(usable, block_rows, jnp.zeros_like(block_rows)))
                piece_ids.append(jnp.where(usable, sender * per_block + block_index, -1).astype(jnp.int32)[None])
                first_rows.append(first_row)
                usable_list.append(usable)
            candidates = jnp.concatenate(pieces, axis=0)
            key_ids = jnp.concatenate(piece_ids, axis=0)
            own_selection = lax.dynamic_slice_in_dim(selection, (group_index * per_block).astype(jnp.int32), per_block, 0)
            allowed = allowed_mask(own_selection, key_ids, group_index * per_block)
            grad_nope, grad_rope, key_grads, cand_grad = group_backward(lax.dynamic_slice_in_dim(queries, begin_row, TOK_DEV, 0), lax.dynamic_slice_in_dim(rope_queries, begin_row, TOK_DEV, 0), lax.dynamic_slice_in_dim(out_grads, begin_row, TOK_DEV, 0), lax.dynamic_slice_in_dim(totals, begin_row, TOK_DEV, 1), candidates, up_weight, allowed)
            own_now = lax.dynamic_slice_in_dim(grad_rows, begin_row, TOK_DEV, 0)
            grad_rows = lax.dynamic_update_slice_in_dim(grad_rows, own_now + cand_grad[:TOK_DEV], begin_row, 0)
            for matching in range(4):
                returned = cand_grad[TOK_DEV + matching * BLOCK:TOK_DEV + (matching + 1) * BLOCK]
                returned = jnp.where(usable_list[matching], returned, jnp.zeros_like(returned))
                current = lax.dynamic_slice_in_dim(grad_rows, first_rows[matching], BLOCK, 0)
                grad_rows = lax.dynamic_update_slice_in_dim(grad_rows, current + returned, first_rows[matching], 0)
            weight_acc = weight_acc + lax.dot_general(candidates[:, :LAT], key_grads, (((0,), (0,)), ((), ())), preferred_element_type=jnp.float32)
            return ((grad_rows, weight_acc), (grad_nope, grad_rope))
        zero_rows = jnp.zeros((LENGTH, LAT + ROPE), jnp.float32)
        (grad_rows, weight_sum), (nope_parts, rope_parts) = lax.scan(one_group, (zero_rows, weight_sum), jnp.arange(N_CTX, dtype=jnp.int32))
        return (weight_sum, (nope_parts.reshape(LENGTH, H * NOPE), rope_parts.reshape(LENGTH, H * ROPE), grad_rows))
    weight_zero = jnp.zeros((LAT, H * (NOPE + VDIM)), jnp.float32)
    weight_sum, (grad_nope, grad_rope, grad_rows) = lax.scan(one_sequence, weight_zero, (q_nope, q_rope, grad_out, log_total, kv_latent, selected, offered))
    return (grad_nope, grad_rope, grad_rows, weight_sum)
```

```python
import functools

import jax
import jax.numpy as jnp
from jax import lax
from jax.experimental import pallas as pl
from jax.experimental.pallas import tpu as pltpu
from jax.sharding import PartitionSpec as P

LAT = 256
ROPE = 64
NOPE = 128
VDIM = 128
BLOCK = 64
HEADS = 64
HALF_HEADS = 32
CAND = 384
TOK = 128
HALF = 8192
SLAB = 1024

offsets = (1, 2, 3, 4)
MESH = pl.DeviceIdType.MESH
NT = (((1,), (1,)), ((), ()))
TN = (((0,), (0,)), ((), ()))
VMEM = pl.BlockSpec(memory_space=pltpu.VMEM)
ANY = pl.BlockSpec(memory_space=pl.ANY)


class Place:
    def __init__(self):
        self.dp = lax.axis_index("dp")
        self.ctx = lax.axis_index("ctx")
        self.xh = self.dp // 4
        self.y = self.dp % 4
        self.core = self.ctx % 2
        self.chip = self.ctx // 2
        self.xl = self.chip % 2

    def sibling(self):
        return (self.dp, self.ctx + 1 - 2 * self.core)

    def in_ctx(self, chip, core):
        return (self.dp, chip * 2 + core)

    def side(self):
        return (self.dp, self.ctx + 2 - 4 * self.xl)

    def cross(self):
        return ((1 - self.xh) * 4 + self.y, self.ctx + 2 - 4 * self.xl)

    def ring(self, step):
        return (self.xh * 4 + (self.y + step) % 4, self.ctx)


def rdma(src, dst, send, recv, device):
    return pltpu.make_async_remote_copy(
        src_ref=src, dst_ref=dst, send_sem=send, recv_sem=recv, device_id=device,
        device_id_type=MESH,
    )


def greet(devices):
    barrier = pltpu.get_barrier_semaphore()
    for device in devices:
        pl.semaphore_signal(barrier, inc=1, device_id=device, device_id_type=MESH)
    pl.semaphore_wait(barrier, len(devices))


def gather_kernel(
    qn, qr, go, lt, own, box, bias, upw,
    qn2, qr2, go2, lt2, cand, bias2, weight,
    sib_rows, row_blk,
    loc, sib_s, sib_r, off_s, off_r, z_s, z_r, y_s, y_r, f_s, f_r, x_s, x_r, n_s, n_r,
):
    me = Place()
    core, chip = me.core, me.chip
    sib = me.sibling()
    peers = [me.in_ctx((chip + o) % 16, core) for o in range(1, 16)]
    peers += [me.in_ctx((chip + o) % 16, 1 - core) for o in range(16)]
    peers += [me.ring(1), me.ring(3), me.cross()]
    greet(peers)

    slab_col = lambda dp: pl.ds(pl.multiple_of(dp * SLAB, SLAB), SLAB)
    half_col = lambda k: pl.ds(pl.multiple_of(k * HALF + me.dp * SLAB, SLAB), SLAB)
    first = rdma(upw.at[:, half_col(1 - core)], sib_rows, sib_s.at[0], sib_r.at[0], sib)
    first.start()

    sends = []
    for m, o in enumerate(offsets):
        target = (me.ctx + o) % 32
        rows = pl.ds(pl.multiple_of((target % 2) * CAND + TOK + m * BLOCK, 64), BLOCK)
        for t in range(2):
            device = (me.dp, (target // 2) * 2 + t)
            landing = off_r.at[m * 2 + target % 2]
            cp = rdma(box.at[m], cand.at[rows, :], off_s.at[m * 2 + t], landing, device)
            if m == 0 and t == 0:
                pl.when(core == 0)(
                    pltpu.make_async_copy(box.at[m], cand.at[rows, :], landing).start)
                pl.when(core == 1)(cp.start)
                to_next = cp
            else:
                cp.start()
                sends.append(cp)

    qrow = pl.ds(pl.multiple_of(core * TOK, TOK), TOK)
    crow = pl.ds(pl.multiple_of(core * CAND, TOK), TOK)
    brow = pl.ds(pl.multiple_of(core * CAND, TOK), CAND)

    def col(k, width):
        return pl.ds(pl.multiple_of(k * width, width), width)

    pairs = [
        (lambda k: qn.at[:, col(k, 4096)], qn2.at[qrow, :]),
        (lambda k: qr.at[:, col(k, 2048)], qr2.at[qrow, :]),
        (lambda k: go.at[:, col(k, 4096)], go2.at[qrow, :]),
        (lambda k: lt.at[col(k, 32), :], lt2.at[core]),
        (lambda k: own, cand.at[crow, :]),
        (lambda k: bias, bias2.at[brow, :]),
    ]
    locals_ = []
    for i, (src, dst) in enumerate(pairs):
        cp = rdma(src(1 - core), dst, sib_s.at[1 + i], sib_r.at[1 + i], sib)
        cp.start()
        sends.append(cp)
        lc = pltpu.make_async_copy(src(core), dst, loc.at[i])
        lc.start()
        locals_.append(lc)

    first.wait_recv()
    mine = upw[:, half_col(core)].astype(jnp.float32)
    other = sib_rows[...].astype(jnp.float32)
    top = jnp.where(core == 0, mine, other)
    bottom = jnp.where(core == 0, other, mine)
    row_blk[...] = jnp.concatenate([top, bottom], axis=0).astype(jnp.bfloat16)
    my_slab = slab_col(me.dp)

    def chip_rows(c):
        return pl.ds(pl.multiple_of(c * 16, 16), 16)

    lc = pltpu.make_async_copy(row_blk, weight.at[chip_rows(chip), my_slab], loc.at[6])
    lc.start()
    locals_.append(lc)
    zs = []
    for o in range(1, 16):
        cp = rdma(row_blk, weight.at[chip_rows(chip), my_slab], z_s.at[o], z_r.at[o],
                  me.in_ctx((chip + o) % 16, core))
        cp.start()
        zs.append(cp)
    for o in range(1, 16):
        zs[o - 1].wait_recv()
    locals_.pop().wait()

    lo, hi, whole = pl.ds(0, 128), pl.ds(128, 128), pl.ds(0, 256)
    sent_half = pl.ds(pl.multiple_of(me.xl * 128, 128), 128)
    got_half = pl.ds(pl.multiple_of((1 - me.xl) * 128, 128), 128)
    blk = lambda xh, step: slab_col(xh * 4 + (me.y + step) % 4)

    def go_copy(rows, cols, s, r, device):
        cp = rdma(weight.at[rows, cols], weight.at[rows, cols], s, r, device)
        cp.start()
        sends.append(cp)

    def await_block(rows, cols, s, r):
        rdma(weight.at[rows, cols], weight.at[rows, cols], s, r, sib).wait_recv()

    def cross(step):
        go_copy(sent_half, blk(me.xh, step), x_s.at[step], x_r.at[step], me.cross())

    def relay(step):
        cols = blk(1 - me.xh, step)
        await_block(got_half, cols, x_s.at[step], x_r.at[step])
        go_copy(got_half, cols, n_s.at[step], n_r.at[step], me.side())

    go_copy(whole, my_slab, y_s.at[0], y_r.at[0], me.ring(1))
    go_copy(whole, my_slab, y_s.at[1], y_r.at[1], me.ring(3))
    cross(0)
    await_block(whole, blk(me.xh, 3), y_s.at[0], y_r.at[0])
    go_copy(lo, blk(me.xh, 3), f_s.at[0], f_r.at[0], me.ring(1))
    cross(3)
    await_block(whole, blk(me.xh, 1), y_s.at[1], y_r.at[1])
    go_copy(hi, blk(me.xh, 1), f_s.at[1], f_r.at[1], me.ring(3))
    cross(1)
    relay(0)
    await_block(lo, blk(me.xh, 2), f_s.at[0], f_r.at[0])
    await_block(hi, blk(me.xh, 2), f_s.at[1], f_r.at[1])
    cross(2)
    relay(3)
    relay(1)
    relay(2)
    for step in (0, 3, 1, 2):
        await_block(sent_half, blk(1 - me.xh, step), n_s.at[step], n_r.at[step])

    for cp in locals_:
        cp.wait()
    orow = pl.ds(pl.multiple_of((1 - core) * TOK, TOK), TOK)
    ocrow = pl.ds(pl.multiple_of((1 - core) * CAND, TOK), TOK)
    obrow = pl.ds(pl.multiple_of((1 - core) * CAND, TOK), CAND)
    landed = [qn2.at[orow, :], qr2.at[orow, :], go2.at[orow, :], lt2.at[1 - core],
              cand.at[ocrow, :], bias2.at[obrow, :]]
    for i, dst in enumerate(landed):
        rdma(dst, dst, sib_s.at[1 + i], sib_r.at[1 + i], sib).wait_recv()
    for m in range(4):
        for g in range(2):
            dst = cand.at[pl.ds(g * CAND + TOK + m * BLOCK, BLOCK), :]
            rdma(dst, dst, off_s.at[0], off_r.at[m * 2 + g], sib).wait_recv()
    first.wait_send()
    pl.when(core == 1)(to_next.wait_send)
    for cp in zs + sends:
        cp.wait_send()


def gather_call(qn, qr, go, lt, own, box, bias, upw):
    bf = jnp.bfloat16
    dma = pltpu.SemaphoreType.DMA
    return pl.pallas_call(
        gather_kernel,
        out_shape=(
            jax.ShapeDtypeStruct((2 * TOK, 4096), bf),
            jax.ShapeDtypeStruct((2 * TOK, 2048), bf),
            jax.ShapeDtypeStruct((2 * TOK, 4096), bf),
            jax.ShapeDtypeStruct((2, HALF_HEADS, TOK), jnp.float32),
            jax.ShapeDtypeStruct((2 * CAND, LAT + ROPE), bf),
            jax.ShapeDtypeStruct((2 * CAND, TOK), bf),
            jax.ShapeDtypeStruct((LAT, HALF), bf),
        ),
        in_specs=[ANY] * 7 + [VMEM],
        out_specs=(ANY,) * 7,
        scratch_shapes=[
            pltpu.VMEM((8, SLAB), bf),
            pltpu.VMEM((16, SLAB), bf),
            dma((7,)), dma((7,)), dma((7,)), dma((8,)), dma((8,)),
            dma((16,)), dma((16,)), dma((2,)), dma((2,)), dma((2,)), dma((2,)),
            dma((4,)), dma((4,)), dma((4,)), dma((4,)),
        ],
        compiler_params=pltpu.CompilerParams(collective_id=0, has_side_effects=True),
        name="gather_inputs",
    )(qn, qr, go, lt, own, box, bias, upw)


def dg(a, b, dims):
    return lax.dot_general(a, b, dims, preferred_element_type=jnp.float32)


def mm(a, b):
    return jnp.dot(a, b, preferred_element_type=jnp.float32)


SCALE = 1.0 / float(NOPE + ROPE) ** 0.5


def heads_kernel(
    qn, qr, go, lt, c, bias, w, gqn, gqr, dw, cg, rope_a, rope_b, ct, lat, rope_acc
):
    bf = jnp.bfloat16
    zero = jnp.zeros((2 * CAND, ROPE), bf)
    rp = c[:, LAT:]
    rope_a[...] = jnp.concatenate([rp, zero], axis=1)
    rope_b[...] = jnp.concatenate([zero, rp], axis=1)
    ct[...] = c[:, :LAT].T
    lat[...] = jnp.zeros_like(lat)
    rope_acc[...] = jnp.zeros_like(rope_acc)
    lane = lax.broadcasted_iota(jnp.int32, (CAND, 128), 1)
    z128 = jnp.zeros((TOK, 128), bf)

    @pl.loop(0, HALF_HEADS // 2)
    def _(p):
        rcol = pl.ds(pl.multiple_of(p * 128, 128), 128)
        whs, kvs = [], []
        for e in range(2):
            wh = w[:, pl.ds(pl.multiple_of(p * 512 + e * 256, 256), 256)]
            whs.append(wh)
            kvs.append(mm(c[:, :LAT], wh).astype(bf))
        kgs = [[None, None], [None, None]]
        for g in range(2):
            rows = slice(g * CAND, (g + 1) * CAND)
            qrow = slice(g * TOK, (g + 1) * TOK)
            qrp = qr[qrow, rcol]
            hcol = [pl.ds(pl.multiple_of(p * 256 + e * 128, 128), 128) for e in range(2)]
            gos = [go[qrow, hcol[e]] for e in range(2)]
            bd = jnp.concatenate(
                [jnp.concatenate([gos[0], z128], axis=1),
                 jnp.concatenate([z128, gos[1]], axis=1)], axis=0)
            vals = jnp.concatenate([kvs[0][rows, 128:], kvs[1][rows, 128:]], axis=1)
            dp_t = dg(vals, bd, NT)
            gr, rk, lows = None, [], []
            for e in range(2):
                rope = (rope_a if e == 0 else rope_b)[rows, :]
                kcat = jnp.concatenate([kvs[e][rows, :128], rope], axis=1)
                qcat = jnp.concatenate([qn[qrow, hcol[e]], qrp], axis=1)
                s_t = dg(kcat, qcat, NT)
                shift = bias[rows, :].astype(jnp.float32) - lt[g, pl.ds(p * 2 + e, 1), :]
                p_t = jnp.exp(s_t * SCALE + shift)
                d = dp_t[:, e * 128:(e + 1) * 128]
                rd = jnp.sum(p_t * d, axis=0, keepdims=True)
                sg = (p_t * (d - rd)).astype(bf)
                lows.append(p_t.astype(bf))
                gq = dg(sg, kcat, TN) * SCALE
                gqn[qrow, hcol[e]] = gq[:, :128].astype(bf)
                gr = gq[:, 128:] if gr is None else gr + gq[:, 128:]
                kg = mm(sg, qcat) * SCALE
                rk.append(kg[:, 128:])
                kgs[e][g] = kg[:, :128].astype(bf)
            gqr[qrow, rcol] = gr.astype(bf)
            vg = mm(jnp.concatenate(lows, axis=1), bd).astype(bf)
            for e in range(2):
                kgs[e][g] = jnp.concatenate([kgs[e][g], vg[:, e * 128:(e + 1) * 128]], axis=1)
            rope_acc[rows, :] += jnp.where(lane < ROPE, rk[0], rk[1])
        tot = None
        for e in range(2):
            kga = jnp.concatenate(kgs[e], axis=0)
            dw[:, pl.ds(pl.multiple_of(p * 512 + e * 256, 256), 256)] = mm(ct[...], kga)
            t = dg(kga, whs[e], NT)
            tot = t if tot is None else tot + t
        lat[...] += tot

    ra = rope_acc[...]
    cg[...] = jnp.concatenate([lat[...], ra[:, :ROPE] + ra[:, ROPE:]], axis=1)


def heads_call(qn, qr, go, lt, c, bias, w):
    bf = jnp.bfloat16
    return pl.pallas_call(
        heads_kernel,
        out_shape=(
            jax.ShapeDtypeStruct((2 * TOK, 4096), bf),
            jax.ShapeDtypeStruct((2 * TOK, 2048), bf),
            jax.ShapeDtypeStruct((LAT, HALF), jnp.float32),
            jax.ShapeDtypeStruct((2 * CAND, LAT + ROPE), jnp.float32),
        ),
        in_specs=[VMEM] * 7,
        out_specs=(VMEM,) * 4,
        scratch_shapes=[
            pltpu.VMEM((2 * CAND, 128), bf),
            pltpu.VMEM((2 * CAND, 128), bf),
            pltpu.VMEM((LAT, 2 * CAND), bf),
            pltpu.VMEM((2 * CAND, LAT), jnp.float32),
            pltpu.VMEM((2 * CAND, 128), jnp.float32),
        ],
        compiler_params=pltpu.CompilerParams(vmem_limit_bytes=56 << 20),
        name="heads",
    )(qn, qr, go, lt, c, bias, w)


ORDER = (2, 1, 3, 0)


def reduce_kernel(
    gqn, gqr, dw, cg,
    out_n, out_r, got, own2, out_w,
    acc, xsend, xrecv, csend, crecv, y2s, y2r, y1s, y1r, zbuf, fin,
    ld, loc, sib_s, sib_r, off_s, off_r, x_s, x_r, c_s, c_r, y2_s, y2_r, y1_s, y1_r,
    z_s, z_r, w_s, w_r,
):
    bf = jnp.bfloat16
    me = Place()
    core, chip = me.core, me.chip
    sib = me.sibling()
    peers = [me.in_ctx((chip + o) % 16, core) for o in range(1, 16)]
    peers += [me.in_ctx((chip + o) % 16, 1 - core) for o in range(16)]
    peers += [(r, chip * 2 + c) for o in range(1, 8) for c in range(2) for r in [(me.dp + o) % 8]]
    peers += [me.cross()]
    blk = lambda xh, step: pl.ds(
        pl.multiple_of((xh * 4 + (me.y + step) % 4) * SLAB, SLAB), SLAB)
    lo, hi = pl.ds(0, 128), pl.ds(128, 128)
    keep_half = pl.ds(pl.multiple_of(me.xl * 128, 128), 128)
    give_half = pl.ds(pl.multiple_of((1 - me.xl) * 128, 128), 128)

    loads = []
    for side in range(2):
        for i, step in enumerate(ORDER):
            cols = blk(1 - me.xh if side == 0 else me.xh, step)
            cp = pltpu.make_async_copy(dw.at[:, cols], acc.at[side * 4 + i], ld.at[side * 4 + i])
            cp.start()
            loads.append(cp)
    greet(peers)

    sends = []
    locals_ = []

    def send(src, dst, s, r, device):
        cp = rdma(src, dst, s, r, device)
        cp.start()
        sends.append(cp)
        return cp

    for i in range(4):
        loads[i].wait()
        xsend[i] = acc[i, give_half, :].astype(bf)
        send(xsend.at[i], xrecv.at[i], x_s.at[i], x_r.at[i], me.side())

    qrow = pl.ds(pl.multiple_of((1 - core) * TOK, TOK), TOK)
    mrow = pl.ds(pl.multiple_of(core * TOK, TOK), TOK)
    ncol = pl.ds(pl.multiple_of(core * 4096, 4096), 4096)
    rcol = pl.ds(pl.multiple_of(core * 2048, 2048), 2048)
    orow = pl.ds(pl.multiple_of((1 - core) * CAND, TOK), TOK)
    moff = pl.ds(pl.multiple_of(core * CAND, TOK), TOK)
    back = [
        send(gqn.at[qrow, :], out_n.at[:, ncol], sib_s.at[0], sib_r.at[0], sib),
        send(gqr.at[qrow, :], out_r.at[:, rcol], sib_s.at[1], sib_r.at[1], sib),
        send(cg.at[orow, :], own2.at[1], sib_s.at[2], sib_r.at[2], sib),
    ]
    for i, (src, dst) in enumerate([(gqn.at[mrow, :], out_n.at[:, ncol]),
                                    (gqr.at[mrow, :], out_r.at[:, rcol]),
                                    (cg.at[moff, :], own2.at[0])]):
        cp = pltpu.make_async_copy(src, dst, loc.at[i])
        cp.start()
        locals_.append(cp)
    for m, o in enumerate(offsets):
        for g in range(2):
            target = (chip * 2 + g + 32 - o) % 32
            src = cg.at[pl.ds(g * CAND + TOK + m * BLOCK, BLOCK), :]
            dst, landing = got.at[m * 2 + core], off_r.at[m * 2 + core]
            if m == 0 and g == 1:
                to_last = rdma(src, dst, off_s.at[1], landing, (me.dp, target))
                pl.when(core == 0)(pltpu.make_async_copy(src, dst, landing).start)
                pl.when(core == 1)(to_last.start)
            else:
                send(src, dst, off_s.at[m * 2 + g], landing, (me.dp, target))

    for i in range(4):
        rdma(xrecv.at[i], xrecv.at[i], x_s.at[i], x_r.at[i], sib).wait_recv()
        csend[i] = (acc[i, keep_half, :] + xrecv[i].astype(jnp.float32)).astype(bf)
        send(csend.at[i], crecv.at[i], c_s.at[i], c_r.at[i], me.cross())

    def crossed(i):
        loads[4 + i].wait()
        rdma(crecv.at[i], crecv.at[i], c_s.at[i], c_r.at[i], sib).wait_recv()
        acc[4 + i, give_half, :] += crecv[i].astype(jnp.float32)

    crossed(0)
    y2s[0] = acc[4, 0:128, :].astype(bf)
    send(y2s.at[0], y2r.at[0], y2_s.at[0], y2_r.at[0], me.ring(1))
    y2s[1] = acc[4, 128:256, :].astype(bf)
    send(y2s.at[1], y2r.at[1], y2_s.at[1], y2_r.at[1], me.ring(3))
    crossed(1)
    rdma(y2r.at[0], y2r.at[0], y2_s.at[0], y2_r.at[0], sib).wait_recv()
    y1s[0, 0:128, :] = (acc[5, 0:128, :] + y2r[0].astype(jnp.float32)).astype(bf)
    y1s[0, 128:256, :] = acc[5, 128:256, :].astype(bf)
    send(y1s.at[0], y1r.at[0], y1_s.at[0], y1_r.at[0], me.ring(1))
    crossed(2)
    rdma(y2r.at[1], y2r.at[1], y2_s.at[1], y2_r.at[1], sib).wait_recv()
    y1s[1, 0:128, :] = acc[6, 0:128, :].astype(bf)
    y1s[1, 128:256, :] = (acc[6, 128:256, :] + y2r[1].astype(jnp.float32)).astype(bf)
    send(y1s.at[1], y1r.at[1], y1_s.at[1], y1_r.at[1], me.ring(3))
    crossed(3)
    rdma(y1r.at[0], y1r.at[0], y1_s.at[0], y1_r.at[0], sib).wait_recv()
    rdma(y1r.at[1], y1r.at[1], y1_s.at[1], y1_r.at[1], sib).wait_recv()
    acc[7] = acc[7] + (y1r[0].astype(jnp.float32) + y1r[1].astype(jnp.float32))

    for o in range(1, 16):
        to = (chip + o) % 16
        rows = pl.ds(pl.multiple_of(to * 16, 16), 16)
        send(acc.at[7, rows, :], zbuf.at[o], z_s.at[o], z_r.at[o], me.in_ctx(to, core))
    total = acc[7, pl.ds(pl.multiple_of(chip * 16, 16), 16), :]
    for o in range(1, 16):
        rdma(zbuf.at[o], zbuf.at[o], z_s.at[o], z_r.at[o], sib).wait_recv()
        total = total + zbuf[o]
    fin[...] = total

    cols = pl.ds(pl.multiple_of(core * HALF + me.dp * SLAB, SLAB), SLAB)
    for o in range(8):
        r = (me.dp + o) % 8
        for f in range(2):
            if o == 0 and f == 0:
                continue
            c = core if f == 0 else 1 - core
            rows = pl.ds(pl.multiple_of(c * 8, 8), 8)
            send(fin.at[rows, :], out_w.at[:, cols], w_s.at[o * 2 + f], w_r.at[o * 2 + f],
                 (r, chip * 2 + c))
    cp = pltpu.make_async_copy(
        fin.at[pl.ds(pl.multiple_of(core * 8, 8), 8), :], out_w.at[:, cols], loc.at[3])
    cp.start()
    locals_.append(cp)
    for o in range(8):
        r = (me.dp + 8 - o) % 8
        for f in range(2):
            if o == 0 and f == 0:
                continue
            c = core if f == 0 else 1 - core
            dst = out_w.at[:, pl.ds(pl.multiple_of(c * HALF + r * SLAB, SLAB), SLAB)]
            rdma(dst, dst, w_s.at[0], w_r.at[o * 2 + f], sib).wait_recv()

    for m in range(4):
        for c in range(2):
            dst = got.at[m * 2 + c]
            rdma(dst, dst, off_s.at[0], off_r.at[m * 2 + c], sib).wait_recv()
    dsts = [out_n.at[:, pl.ds(pl.multiple_of((1 - core) * 4096, 4096), 4096)],
            out_r.at[:, pl.ds(pl.multiple_of((1 - core) * 2048, 2048), 2048)],
            own2.at[1]]
    for i, dst in enumerate(dsts):
        rdma(dst, dst, sib_s.at[i], sib_r.at[i], sib).wait_recv()
    for cp in locals_:
        cp.wait()
    pl.when(core == 1)(to_last.wait_send)
    for cp in sends:
        cp.wait_send()


def reduce_call(gqn, gqr, dw, cg):
    bf, f32 = jnp.bfloat16, jnp.float32
    dma = pltpu.SemaphoreType.DMA
    return pl.pallas_call(
        reduce_kernel,
        out_shape=(
            jax.ShapeDtypeStruct((TOK, HEADS * NOPE), bf),
            jax.ShapeDtypeStruct((TOK, HEADS * ROPE), bf),
            jax.ShapeDtypeStruct((8, BLOCK, LAT + ROPE), f32),
            jax.ShapeDtypeStruct((2, TOK, LAT + ROPE), f32),
            jax.ShapeDtypeStruct((8, 2 * HALF), f32),
        ),
        in_specs=[ANY] * 4,
        out_specs=(ANY,) * 5,
        scratch_shapes=[
            pltpu.VMEM((8, LAT, SLAB), f32),
            pltpu.VMEM((4, 128, SLAB), bf), pltpu.VMEM((4, 128, SLAB), bf),
            pltpu.VMEM((4, 128, SLAB), bf), pltpu.VMEM((4, 128, SLAB), bf),
            pltpu.VMEM((2, 128, SLAB), bf), pltpu.VMEM((2, 128, SLAB), bf),
            pltpu.VMEM((2, 256, SLAB), bf), pltpu.VMEM((2, 256, SLAB), bf),
            pltpu.VMEM((16, 16, SLAB), f32),
            pltpu.VMEM((16, SLAB), f32),
            dma((8,)), dma((4,)), dma((3,)), dma((3,)), dma((8,)), dma((8,)),
            dma((4,)), dma((4,)), dma((4,)), dma((4,)),
            dma((2,)), dma((2,)), dma((2,)), dma((2,)),
            dma((16,)), dma((16,)), dma((16,)), dma((16,)),
        ],
        compiler_params=pltpu.CompilerParams(
            collective_id=1, has_side_effects=True, vmem_limit_bytes=40 << 20),
        name="reduce_grads",
    )(gqn, gqr, dw, cg)


def key_bias(selection, offer_plan, group):
    ids = [group * 2, group * 2 + 1]
    for m, o in enumerate(offsets):
        source = group - o
        sender = jnp.maximum(source, 0)
        ids.append(jnp.where(source >= 0, sender * 2 + offer_plan[sender, m], -1))
    key_ids = jnp.stack(ids)
    query_ids = group * 2 + jnp.arange(2, dtype=jnp.int32)
    same = key_ids[:, None] == query_ids[None, :]
    picked = jnp.any(selection[None, :, :] == key_ids[:, None, None], axis=2)
    picked = picked & (key_ids >= 0)[:, None]
    inner = jnp.arange(BLOCK, dtype=jnp.int32)
    causal = inner[None, :] >= inner[:, None]
    ok = picked[:, None, :, None] | same[:, None, :, None] & causal[None, :, None, :]
    return jnp.where(ok.reshape(CAND, TOK), 0.0, -1e30).astype(jnp.bfloat16)


def shards(q_nope, q_rope, grad_out, log_total, kv_latent, up_weight, selected, offered):
    group = lax.axis_index("ctx")
    own = kv_latent[0]
    offer = offered[0, group]
    bias = key_bias(selected[0], offered[0], group)
    pick = (offer == 0)[:, None, None]
    box = jnp.where(pick, own[None, :BLOCK], own[None, BLOCK:])
    qn2, qr2, go2, lt2, cand, bias2, weight = gather_call(
        q_nope[0], q_rope[0], grad_out[0], log_total[0], own, box, bias, up_weight)
    gqn, gqr, dw, cg = heads_call(qn2, qr2, go2, lt2, cand, bias2, weight)
    out_n, out_r, got, own2, out_w = reduce_call(gqn, gqr, dw, cg)
    returned = got.reshape(4, 2, BLOCK, LAT + ROPE).sum(axis=1)
    first = jnp.where(pick, returned, 0.0).sum(axis=0)
    second = jnp.where(pick, 0.0, returned).sum(axis=0)
    grad_rows = own2[0] + own2[1] + jnp.concatenate([first, second], axis=0)
    return (out_n[None], out_r[None], grad_rows[None], out_w)


def solution(mesh):
    in_specs = (
        P("dp", "ctx", None),
        P("dp", "ctx", None),
        P("dp", "ctx", None),
        P("dp", None, "ctx"),
        P("dp", "ctx", None),
        P("ctx", None),
        P("dp", "ctx", None),
        P("dp", None, None),
    )
    out_specs = (P("dp", "ctx", None), P("dp", "ctx", None), P("dp", "ctx", None), P("ctx", None))
    return jax.shard_map(shards, mesh=mesh, in_specs=in_specs, out_specs=out_specs, check_vma=False)
```

```python
import functools

import jax
import jax.numpy as jnp
from jax import lax
from jax.experimental import pallas as pl
from jax.experimental.pallas import tpu as pltpu
from jax.sharding import PartitionSpec as P

LAT = 256
ROPE = 64
NOPE = 128
VDIM = 128
BLOCK = 64
HEADS = 64
HALF_HEADS = 32
CAND = 384
TOK = 128
HALF = 8192
SLAB = 1024

offsets = (1, 2, 3, 4)
MESH = pl.DeviceIdType.MESH
NT = (((1,), (1,)), ((), ()))
TN = (((0,), (0,)), ((), ()))
VMEM = pl.BlockSpec(memory_space=pltpu.VMEM)
ANY = pl.BlockSpec(memory_space=pl.ANY)


class Place:
    def __init__(self):
        self.dp = lax.axis_index("dp")
        self.ctx = lax.axis_index("ctx")
        self.xh = self.dp // 4
        self.y = self.dp % 4
        self.core = self.ctx % 2
        self.chip = self.ctx // 2
        self.xl = self.chip % 2

    def sibling(self):
        return (self.dp, self.ctx + 1 - 2 * self.core)

    def in_ctx(self, chip, core):
        return (self.dp, chip * 2 + core)

    def side(self):
        return (self.dp, self.ctx + 2 - 4 * self.xl)

    def cross(self):
        return ((1 - self.xh) * 4 + self.y, self.ctx + 2 - 4 * self.xl)

    def ring(self, step):
        return (self.xh * 4 + (self.y + step) % 4, self.ctx)


def rdma(src, dst, send, recv, device):
    return pltpu.make_async_remote_copy(
        src_ref=src, dst_ref=dst, send_sem=send, recv_sem=recv, device_id=device,
        device_id_type=MESH,
    )


def greet(devices):
    barrier = pltpu.get_barrier_semaphore()
    for device in devices:
        pl.semaphore_signal(barrier, inc=1, device_id=device, device_id_type=MESH)
    pl.semaphore_wait(barrier, len(devices))


def dg(a, b, dims):
    return lax.dot_general(a, b, dims, preferred_element_type=jnp.float32)


def mm(a, b):
    return jnp.dot(a, b, preferred_element_type=jnp.float32)


SCALE = 1.0 / float(NOPE + ROPE) ** 0.5


UNITS = (
    ((0, 0), (0, 3), (0, 1), (1, 0), (0, 2), (1, 3), (1, 1), (1, 2)),
    ((1, 2), (1, 1), (1, 3), (1, 0), (0, 2), (0, 1), (0, 3), (0, 0)),
)
SLOT = {(f, u): f * 8 + i for f in range(2) for i, u in enumerate(UNITS[f])}
WIDE = SLAB // 2


class Sems:
    def __init__(self):
        self.at = {}
        self.count = 0

    def __call__(self, name, size=1):
        if name not in self.at:
            self.at[name] = self.count
            self.count += size
        return self.at[name]


NSEM = 256


def fused_kernel(
    qn, qr, go, lt, own, box, bias, upw,
    out_n, out_r, got, own2, out_w,
    qn2, qr2, go2, lt2, c, bias2, w, sib_rows, row_blk,
    gqn, gqr, cg, cgl, rope_a, rope_b, ct, lat, rope_acc,
    acc, xsend, xrecv, csend, crecv, y2s, y2r, y1s, y1r, zbuf, fin,
    ss, rs, ls,
):
    bf, f32 = jnp.bfloat16, jnp.float32
    me = Place()
    core, chip = me.core, me.chip
    sib = me.sibling()
    peers = [me.in_ctx((chip + o) % 16, core) for o in range(1, 16)]
    peers += [me.in_ctx((chip + o) % 16, 1 - core) for o in (0, 1, 2, 14, 15)]
    peers += [((me.dp + o) % 8, chip * 2 + k) for o in range(1, 8) for k in range(2)]
    peers += [me.cross()]

    chip_at = [(chip + o) % 16 for o in range(16)]
    y_at = [(me.y + o) % 4 for o in range(4)]

    sem = Sems()
    sends = []
    local = []

    def send(src, dst, name, device, land=None):
        at = sem(name)
        rdma(src(), dst(), ss.at[at], rs.at[at if land is None else land], device).start()
        sends.append((src, at))

    def got_it(ref, at):
        at = sem(at) if not isinstance(at, int) else at
        rdma(ref, ref, ss.at[at], rs.at[at], sib).wait_recv()

    def copy(src, dst):
        cp = pltpu.make_async_copy(src, dst, ls.at[len(local)])
        cp.start()
        local.append(cp)

    def rows_at(start, size, unit=8):
        return pl.ds(pl.multiple_of(start, unit), size)

    def col(k, width):
        return pl.ds(pl.multiple_of(k * width, width), width)

    def cols_of(f, side, step):
        xh = me.xh if side == 0 else 1 - me.xh
        return col((xh * 4 + y_at[step]) * 2 + f, WIDE)

    qrow, crow, brow = rows_at(core * TOK, TOK, TOK), rows_at(core * CAND, TOK, TOK), rows_at(
        core * CAND, CAND, TOK)
    pairs = [
        (lambda k: qn.at[:, col(k, 4096)], lambda k: qn2.at[rows_at(k * TOK, TOK, TOK), :]),
        (lambda k: qr.at[:, col(k, 2048)], lambda k: qr2.at[rows_at(k * TOK, TOK, TOK), :]),
        (lambda k: go.at[:, col(k, 4096)], lambda k: go2.at[rows_at(k * TOK, TOK, TOK), :]),
        (lambda k: lt.at[col(k, 32), :], lambda k: lt2.at[k]),
        (lambda k: own, lambda k: c.at[rows_at(k * CAND, TOK, TOK), :]),
        (lambda k: bias, lambda k: bias2.at[rows_at(k * CAND, CAND, TOK), :]),
    ]
    for src, dst in pairs:
        copy(src(core), dst(core))
    greet(peers)

    half_col = lambda k: pl.ds(pl.multiple_of(k * HALF + me.dp * SLAB, SLAB), SLAB)
    send(lambda: upw.at[:, half_col(1 - core)], lambda: sib_rows, "rows", sib)

    land0 = sem("offer_in", 8)
    for m, o in enumerate(offsets):
        target = (me.ctx + o) % 32
        place = rows_at((target % 2) * CAND + TOK + m * BLOCK, BLOCK, 64)
        for t in range(2):
            device = (me.dp, (target // 2) * 2 + t)
            land = land0 + m * 2 + target % 2
            if m == 0 and t == 0:
                at = sem("to_next")
                to_next = rdma(box.at[m], c.at[place, :], ss.at[at], rs.at[land], device)
                pl.when(core == 0)(
                    pltpu.make_async_copy(box.at[m], c.at[place, :], rs.at[land]).start)
                pl.when(core == 1)(to_next.start)
            else:
                send(lambda m=m: box.at[m], lambda place=place: c.at[place, :],
                     ("offer", m, t), device, land)
    for i, (src, dst) in enumerate(pairs):
        send(lambda src=src: src(1 - core), lambda dst=dst: dst(core), ("sib", i), sib)

    got_it(sib_rows, "rows")
    mine = upw[:, half_col(core)].astype(f32)
    other = sib_rows[...].astype(f32)
    top = jnp.where(core == 0, mine, other)
    bottom = jnp.where(core == 0, other, mine)
    row_blk[...] = jnp.concatenate([top, bottom], axis=0).astype(bf)
    my_rows = rows_at(chip * 16, 16, 16)
    for f in range(2):
        part = pl.ds(f * WIDE, WIDE)
        w[my_rows, cols_of(f, 0, 0)] = row_blk[:, part]
        for o in range(1, 16):
            send(lambda part=part: row_blk.at[:, part],
                 lambda f=f: w.at[my_rows, cols_of(f, 0, 0)],
                 ("z", f, o), me.in_ctx((chip + o) % 16, core))

    lo, hi, whole = pl.ds(0, 128), pl.ds(128, 128), pl.ds(0, 256)
    sent_half = rows_at(me.xl * 128, 128, 128)
    got_half = rows_at((1 - me.xl) * 128, 128, 128)

    def pass_on(rows, f, side, step, name, device):
        ref = lambda: w.at[rows, cols_of(f, side, step)]
        send(ref, ref, (name, f, step), device)

    def arrived(rows, f, side, step, name, as_step=None):
        got_it(w.at[rows, cols_of(f, side, step)], (name, f, step if as_step is None else as_step))

    def cross(f, step):
        pass_on(sent_half, f, 0, step, "cross", me.cross())

    def relay(f, step):
        arrived(got_half, f, 1, step, "cross")
        pass_on(got_half, f, 1, step, "side", me.side())

    def gather_a(f):
        for o in range(1, 16):
            ref = w.at[rows_at(chip_at[16 - o] * 16, 16, 16), cols_of(f, 0, 0)]
            got_it(ref, ("z", f, o))
        ref = lambda: w.at[whole, cols_of(f, 0, 0)]
        send(ref, ref, ("up", f), me.ring(1))
        send(ref, ref, ("down", f), me.ring(3))
        cross(f, 0)

    def gather_b(f):
        got_it(w.at[whole, cols_of(f, 0, 3)], ("up", f))
        ref3 = lambda: w.at[lo, cols_of(f, 0, 3)]
        send(ref3, ref3, ("up2", f), me.ring(1))
        cross(f, 3)
        got_it(w.at[whole, cols_of(f, 0, 1)], ("down", f))
        ref1 = lambda: w.at[hi, cols_of(f, 0, 1)]
        send(ref1, ref1, ("down2", f), me.ring(3))
        cross(f, 1)

    def gather_c(f):
        got_it(w.at[lo, cols_of(f, 0, 2)], ("up2", f))
        got_it(w.at[hi, cols_of(f, 0, 2)], ("down2", f))
        cross(f, 2)

    def side_done(f, step):
        arrived(sent_half, f, 1, step, "side")

    def reduce_x(f, step):
        at = f * 4 + step
        xsend[at] = acc[SLOT[f, (1, step)], sent_half, :].astype(bf)
        send(lambda: xsend.at[at], lambda: xrecv.at[at], ("rx", at), me.side())

    def reduce_cross(f, step):
        at = f * 4 + step
        got_it(xrecv.at[at], ("rx", at))
        csend[at] = (acc[SLOT[f, (1, step)], got_half, :] + xrecv[at].astype(f32)).astype(bf)
        send(lambda: csend.at[at], lambda: crecv.at[at], ("rc", at), me.cross())

    def crossed(f, step):
        at = f * 4 + step
        got_it(crecv.at[at], ("rc", at))
        acc[SLOT[f, (0, step)], sent_half, :] += crecv[at].astype(f32)

    def reduce_y2(f):
        crossed(f, 2)
        for i, step in enumerate((1, 3)):
            at = f * 2 + i
            y2s[at] = acc[SLOT[f, (0, 2)], i * 128:(i + 1) * 128, :].astype(bf)
            send(lambda at=at: y2s.at[at], lambda at=at: y2r.at[at], ("ry2", at), me.ring(step))

    def reduce_y1(f, i):
        step = (1, 3)[i]
        crossed(f, step)
        at = f * 2 + i
        got_it(y2r.at[at], ("ry2", at))
        slot = SLOT[f, (0, step)]
        near, far = slice(i * 128, (i + 1) * 128), slice((1 - i) * 128, (2 - i) * 128)
        y1s[at, near, :] = (acc[slot, near, :] + y2r[at].astype(f32)).astype(bf)
        y1s[at, far, :] = acc[slot, far, :].astype(bf)
        send(lambda: y1s.at[at], lambda: y1r.at[at], ("ry1", at), me.ring(step))

    def reduce_z(f):
        slot = SLOT[f, (0, 0)]
        crossed(f, 0)
        for i in range(2):
            got_it(y1r.at[f * 2 + i], ("ry1", f * 2 + i))
        acc[slot] = acc[slot] + (y1r[f * 2].astype(f32) + y1r[f * 2 + 1].astype(f32))
        for o in range(1, 16):
            send(lambda o=o: acc.at[slot, rows_at(chip_at[o] * 16, 16, 16), :],
                 lambda o=o: zbuf.at[f * 16 + o], ("rz", f, o), me.in_ctx(chip_at[o], core))

    def finish(f):
        total = acc[SLOT[f, (0, 0)], my_rows, :]
        for o in range(1, 16):
            got_it(zbuf.at[f * 16 + o], ("rz", f, o))
            total = total + zbuf[f * 16 + o]
        fin[f] = total
        for o in range(8):
            for k in range(2):
                if o == 0 and k == 0:
                    continue
                to = core if k == 0 else 1 - core
                send(lambda to=to: fin.at[f, rows_at(to * 8, 8), :], lambda: out_cols(f, core, me.dp),
                     ("w", f, o, k), ((me.dp + o) % 8, chip * 2 + to))

    def out_cols(f, k, r):
        return out_w.at[:, col((k * 8 + r) * 2 + f, WIDE)]

    before = {
        0: [lambda: gather_a(0)],
        1: [lambda: gather_b(0), lambda: relay(0, 0)],
        2: [lambda: gather_c(0), lambda: gather_a(1)],
        3: [lambda: relay(0, 3), lambda: side_done(0, 0)],
        4: [lambda: relay(0, 1), lambda: gather_b(1)],
        5: [lambda: reduce_x(0, 0), lambda: relay(0, 2), lambda: relay(1, 0),
            lambda: gather_c(1), lambda: side_done(0, 3)],
        6: [lambda: reduce_x(0, 3), lambda: reduce_cross(0, 0), lambda: relay(1, 3),
            lambda: side_done(0, 1)],
        7: [lambda: reduce_x(0, 1), lambda: relay(1, 1), lambda: relay(1, 2),
            lambda: side_done(0, 2)],
        8: [lambda: reduce_x(0, 2), lambda: reduce_cross(0, 3), lambda: side_done(1, 2)],
        9: [lambda: reduce_x(1, 2), lambda: reduce_cross(0, 1), lambda: side_done(1, 1)],
        10: [lambda: reduce_x(1, 1), lambda: reduce_cross(0, 2), lambda: side_done(1, 3)],
        11: [lambda: reduce_x(1, 3), lambda: reduce_cross(1, 2), lambda: side_done(1, 0)],
        12: [lambda: reduce_x(1, 0), lambda: reduce_cross(1, 1), lambda: reduce_y2(0)],
        13: [lambda: reduce_cross(1, 3), lambda: reduce_y2(1), lambda: reduce_y1(0, 0)],
        14: [lambda: reduce_cross(1, 0), lambda: reduce_y1(1, 0), lambda: reduce_y1(0, 1)],
        15: [lambda: reduce_y1(1, 1), lambda: reduce_z(0)],
    }

    for cp in local:
        cp.wait()
    for i, (_, dst) in enumerate(pairs):
        got_it(dst(1 - core), ("sib", i))
    for m in range(4):
        for g in range(2):
            got_it(c.at[pl.ds(g * CAND + TOK + m * BLOCK, BLOCK), :], land0 + m * 2 + g)
    zero = jnp.zeros((2 * CAND, ROPE), bf)
    rp = c[:, LAT:]
    rope_a[...] = jnp.concatenate([rp, zero], axis=1)
    rope_b[...] = jnp.concatenate([zero, rp], axis=1)
    ct[...] = c[:, :LAT].T
    lat[...] = jnp.zeros_like(lat)
    rope_acc[...] = jnp.zeros_like(rope_acc)
    lane = lax.broadcasted_iota(jnp.int32, (CAND, 128), 1)
    z128 = jnp.zeros((TOK, 128), bf)

    @pl.loop(0, 16)
    def _(s):
        for k, events in before.items():
            @pl.when(s == k)
            def _(events=events):
                for event in events:
                    event()
        side, step = [
            sum((s == SLOT[f, u]).astype(jnp.int32) * u[i] for f in range(2) for u in UNITS[f] if u[i])
            for i in range(2)]
        xh = me.xh + side - 2 * me.xh * side
        p = (xh * 4 + (me.y + step) % 4) * 2 + s // 8

        rcol = pl.ds(pl.multiple_of(p * 128, 128), 128)
        whs, kvs = [], []
        for e in range(2):
            wh = w[:, pl.ds(pl.multiple_of(p * 512 + e * 256, 256), 256)]
            whs.append(wh)
            kvs.append(mm(c[:, :LAT], wh).astype(bf))
        kgs = [[None, None], [None, None]]
        for g in range(2):
            rows = slice(g * CAND, (g + 1) * CAND)
            qs = slice(g * TOK, (g + 1) * TOK)
            qrp = qr2[qs, rcol]
            hcol = [pl.ds(pl.multiple_of(p * 256 + e * 128, 128), 128) for e in range(2)]
            gos = [go2[qs, hcol[e]] for e in range(2)]
            bd = jnp.concatenate(
                [jnp.concatenate([gos[0], z128], axis=1),
                 jnp.concatenate([z128, gos[1]], axis=1)], axis=0)
            vals = jnp.concatenate([kvs[0][rows, 128:], kvs[1][rows, 128:]], axis=1)
            dp_t = dg(vals, bd, NT)
            gr, rk, lows = None, [], []
            for e in range(2):
                rope = (rope_a if e == 0 else rope_b)[rows, :]
                kcat = jnp.concatenate([kvs[e][rows, :128], rope], axis=1)
                qcat = jnp.concatenate([qn2[qs, hcol[e]], qrp], axis=1)
                s_t = dg(kcat, qcat, NT)
                shift = bias2[rows, :].astype(f32) - lt2[g, pl.ds(p * 2 + e, 1), :]
                p_t = jnp.exp(s_t * SCALE + shift)
                d = dp_t[:, e * 128:(e + 1) * 128]
                rd = jnp.sum(p_t * d, axis=0, keepdims=True)
                sg = (p_t * (d - rd)).astype(bf)
                lows.append(p_t.astype(bf))
                gq = dg(sg, kcat, TN) * SCALE
                gqn[qs, hcol[e]] = gq[:, :128].astype(bf)
                gr = gq[:, 128:] if gr is None else gr + gq[:, 128:]
                kg = mm(sg, qcat) * SCALE
                rk.append(kg[:, 128:])
                kgs[e][g] = kg[:, :128].astype(bf)
            gqr[qs, rcol] = gr.astype(bf)
            vg = mm(jnp.concatenate(lows, axis=1), bd).astype(bf)
            for e in range(2):
                kgs[e][g] = jnp.concatenate([kgs[e][g], vg[:, e * 128:(e + 1) * 128]], axis=1)
            rope_acc[rows, :] += jnp.where(lane < ROPE, rk[0], rk[1])
        tot = None
        for e in range(2):
            kga = jnp.concatenate(kgs[e], axis=0)
            acc[s, :, e * 256:(e + 1) * 256] = mm(ct[...], kga)
            t = dg(kga, whs[e], NT)
            tot = t if tot is None else tot + t
        lat[...] += tot

    reduce_z(1)
    ra = rope_acc[...]
    full = jnp.concatenate([lat[...], ra[:, :ROPE] + ra[:, ROPE:]], axis=1)
    cg[...] = full
    cgl[...] = full.astype(bf)

    back0 = sem("back_in", 8)
    for m, o in enumerate(offsets):
        for g in range(2):
            target = (chip * 2 + g + 32 - o) % 32
            src = lambda m=m, g=g: cgl.at[pl.ds(g * CAND + TOK + m * BLOCK, BLOCK), :]
            dst = lambda m=m: got.at[m * 2 + core]
            land = back0 + m * 2 + core
            if m == 0 and g == 1:
                at = sem("to_last")
                to_last = rdma(src(), dst(), ss.at[at], rs.at[land], (me.dp, target))
                pl.when(core == 0)(pltpu.make_async_copy(src(), dst(), rs.at[land]).start)
                pl.when(core == 1)(to_last.start)
            else:
                send(src, dst, ("back", m, g), (me.dp, target), land)

    other_row = rows_at((1 - core) * TOK, TOK, TOK)
    ncol = lambda k: out_n.at[:, col(k, 4096)]
    rcol_ = lambda k: out_r.at[:, col(k, 2048)]
    send(lambda: gqn.at[other_row, :], lambda: ncol(core), "back_n", sib)
    send(lambda: gqr.at[other_row, :], lambda: rcol_(core), "back_r", sib)
    send(lambda: cg.at[rows_at((1 - core) * CAND, TOK, TOK), :], lambda: own2.at[1], "back_o", sib)
    first_late = len(local)
    copy(gqn.at[qrow, :], ncol(core))
    copy(gqr.at[qrow, :], rcol_(core))
    copy(cg.at[crow, :], own2.at[0])

    finish(0)
    finish(1)
    for f in range(2):
        copy(fin.at[f, rows_at(core * 8, 8), :], out_cols(f, core, me.dp))
    got_it(ncol(1 - core), "back_n")
    got_it(rcol_(1 - core), "back_r")
    got_it(own2.at[1], "back_o")
    for m in range(4):
        for k in range(2):
            got_it(got.at[m * 2 + k], back0 + m * 2 + k)
    for f in range(2):
        for o in range(8):
            for k in range(2):
                if o == 0 and k == 0:
                    continue
                who = core if k == 0 else 1 - core
                got_it(out_cols(f, who, (me.dp + 8 - o) % 8), ("w", f, o, k))
    for cp in local[first_late:]:
        cp.wait()
    pl.when(core == 1)(to_next.wait_send)
    pl.when(core == 1)(to_last.wait_send)
    for src, at in sends:
        rdma(src(), src(), ss.at[at], rs.at[at], sib).wait_send()
    assert sem.count <= NSEM, sem.count


def fused_call(qn, qr, go, lt, own, box, bias, upw):
    bf, f32 = jnp.bfloat16, jnp.float32
    dma = pltpu.SemaphoreType.DMA
    v = pltpu.VMEM
    return pl.pallas_call(
        fused_kernel,
        out_shape=(
            jax.ShapeDtypeStruct((TOK, HEADS * NOPE), bf),
            jax.ShapeDtypeStruct((TOK, HEADS * ROPE), bf),
            jax.ShapeDtypeStruct((8, BLOCK, LAT + ROPE), bf),
            jax.ShapeDtypeStruct((2, TOK, LAT + ROPE), f32),
            jax.ShapeDtypeStruct((8, 2 * HALF), f32),
        ),
        in_specs=[ANY] * 7 + [VMEM],
        out_specs=(ANY,) * 5,
        scratch_shapes=[
            v((2 * TOK, 4096), bf), v((2 * TOK, 2048), bf), v((2 * TOK, 4096), bf),
            v((2, HALF_HEADS, TOK), f32), v((2 * CAND, LAT + ROPE), bf), v((2 * CAND, TOK), bf),
            v((LAT, HALF), bf), v((8, SLAB), bf), v((16, SLAB), bf),
            v((2 * TOK, 4096), bf), v((2 * TOK, 2048), bf),
            v((2 * CAND, LAT + ROPE), f32), v((2 * CAND, LAT + ROPE), bf),
            v((2 * CAND, 128), bf), v((2 * CAND, 128), bf), v((LAT, 2 * CAND), bf),
            v((2 * CAND, LAT), f32), v((2 * CAND, 128), f32),
            v((16, LAT, WIDE), f32),
            v((8, 128, WIDE), bf), v((8, 128, WIDE), bf), v((8, 128, WIDE), bf),
            v((8, 128, WIDE), bf),
            v((4, 128, WIDE), bf), v((4, 128, WIDE), bf),
            v((4, 256, WIDE), bf), v((4, 256, WIDE), bf),
            v((32, 16, WIDE), f32), v((2, 16, WIDE), f32),
            dma((NSEM,)), dma((NSEM,)), dma((16,)),
        ],
        compiler_params=pltpu.CompilerParams(
            collective_id=0, has_side_effects=True, vmem_limit_bytes=56 << 20),
        name="fused_backward",
    )(qn, qr, go, lt, own, box, bias, upw)


def key_bias(selection, offer_plan, group):
    ids = [group * 2, group * 2 + 1]
    for m, o in enumerate(offsets):
        source = group - o
        sender = jnp.maximum(source, 0)
        ids.append(jnp.where(source >= 0, sender * 2 + offer_plan[sender, m], -1))
    key_ids = jnp.stack(ids)
    query_ids = group * 2 + jnp.arange(2, dtype=jnp.int32)
    same = key_ids[:, None] == query_ids[None, :]
    picked = jnp.any(selection[None, :, :] == key_ids[:, None, None], axis=2)
    picked = picked & (key_ids >= 0)[:, None]
    inner = jnp.arange(BLOCK, dtype=jnp.int32)
    causal = inner[None, :] >= inner[:, None]
    ok = picked[:, None, :, None] | same[:, None, :, None] & causal[None, :, None, :]
    return jnp.where(ok.reshape(CAND, TOK), 0.0, -1e30).astype(jnp.bfloat16)


def shards(q_nope, q_rope, grad_out, log_total, kv_latent, up_weight, selected, offered):
    group = lax.axis_index("ctx")
    own = kv_latent[0]
    offer = offered[0, group]
    bias = key_bias(selected[0], offered[0], group)
    pick = (offer == 0)[:, None, None]
    box = jnp.where(pick, own[None, :BLOCK], own[None, BLOCK:])
    out_n, out_r, got, own2, out_w = fused_call(
        q_nope[0], q_rope[0], grad_out[0], log_total[0], own, box, bias, up_weight)
    returned = got.astype(jnp.float32).reshape(4, 2, BLOCK, LAT + ROPE).sum(axis=1)
    first = jnp.where(pick, returned, 0.0).sum(axis=0)
    second = jnp.where(pick, 0.0, returned).sum(axis=0)
    grad_rows = own2[0] + own2[1] + jnp.concatenate([first, second], axis=0)
    return (out_n[None], out_r[None], grad_rows[None], out_w)


def solution(mesh):
    in_specs = (
        P("dp", "ctx", None),
        P("dp", "ctx", None),
        P("dp", "ctx", None),
        P("dp", None, "ctx"),
        P("dp", "ctx", None),
        P("ctx", None),
        P("dp", "ctx", None),
        P("dp", None, None),
    )
    out_specs = (P("dp", "ctx", None), P("dp", "ctx", None), P("dp", "ctx", None), P("ctx", None))
    return jax.shard_map(shards, mesh=mesh, in_specs=in_specs, out_specs=out_specs, check_vma=False)
```

```python
import functools

import jax
import jax.numpy as jnp
from jax import lax
from jax.experimental import pallas as pl
from jax.experimental.pallas import tpu as pltpu
from jax.sharding import PartitionSpec as P

LAT = 256
ROPE = 64
NOPE = 128
VDIM = 128
BLOCK = 64
HEADS = 64
HALF_HEADS = 32
CAND = 384
TOK = 128
HALF = 8192
SLAB = 1024

offsets = (1, 2, 3, 4)
MESH = pl.DeviceIdType.MESH
NT = (((1,), (1,)), ((), ()))
TN = (((0,), (0,)), ((), ()))
VMEM = pl.BlockSpec(memory_space=pltpu.VMEM)
ANY = pl.BlockSpec(memory_space=pl.ANY)


class Place:
    def __init__(self):
        self.dp = lax.axis_index("dp")
        self.ctx = lax.axis_index("ctx")
        self.xh = self.dp // 4
        self.y = self.dp % 4
        self.core = self.ctx % 2
        self.chip = self.ctx // 2
        self.xl = self.chip % 2
        self.z = self.chip // 2

    def sibling(self):
        return (self.dp, self.ctx + 1 - 2 * self.core)

    def in_ctx(self, chip, core):
        return (self.dp, chip * 2 + core)

    def side(self):
        return (self.dp, self.ctx + 2 - 4 * self.xl)

    def along_z(self, step):
        return (self.dp, (self.ctx + 4 * step) % 32)

    def cross(self):
        return ((1 - self.xh) * 4 + self.y, self.ctx + 2 - 4 * self.xl)

    def ring(self, step):
        return (self.xh * 4 + (self.y + step) % 4, self.ctx)


def rdma(src, dst, send, recv, device):
    return pltpu.make_async_remote_copy(
        src_ref=src, dst_ref=dst, send_sem=send, recv_sem=recv, device_id=device,
        device_id_type=MESH,
    )


def signal_peers(devices):
    barrier = pltpu.get_barrier_semaphore()
    for device in devices:
        pl.semaphore_signal(barrier, inc=1, device_id=device, device_id_type=MESH)
    return barrier


def dg(a, b, dims):
    return lax.dot_general(a, b, dims, preferred_element_type=jnp.float32)


def mm(a, b):
    return jnp.dot(a, b, preferred_element_type=jnp.float32)


SCALE = 1.0 / float(NOPE + ROPE) ** 0.5


PLAN = (
    ("cross", 0, 0), ("along_y", 0), ("unit", 0, 0, 0), ("along_z", 1, 2), ("relay", 0, 0),
    ("up", 0), ("cross", 0, 1), ("down", 0), ("cross", 0, 3), ("unit", 0, 0, 3),
    ("unit", 0, 0, 1), ("cross", 0, 2), ("relay", 0, 1), ("along_z", 1, 3), ("unit", 0, 0, 2),
    ("relay", 0, 3), ("unit", 0, 1, 0), ("relay", 0, 2), ("unit", 0, 1, 1), ("along_z", 1, 4),
    ("unit", 0, 1, 3), ("add_x", 0, 3), ("unit", 0, 1, 2), ("add_x", 0, 2), ("add_x", 0, 1),
    ("unit", 1, 1, 2), ("unit", 1, 1, 0), ("add_cross", 0, 2), ("add_x", 1, 2), ("unit", 1, 1, 3),
    ("add_cross", 0, 3), ("add_cross", 0, 1), ("add_x", 1, 3), ("add_x", 0, 0), ("add_y2", 0),
    ("add_cross", 1, 2), ("unit", 1, 0, 2), ("unit", 1, 1, 1), ("add_y1", 0, 1), ("add_y1", 0, 0),
    ("add_x", 1, 1), ("add_cross", 0, 0), ("add_x", 1, 0), ("add_cross", 1, 3), ("unit", 1, 0, 1),
    ("add_y2", 1), ("add_cross", 1, 1), ("unit", 1, 0, 3), ("add_z", 0), ("add_y1", 1, 1),
    ("add_y1", 1, 0), ("add_cross", 1, 0), ("unit", 1, 0, 0), ("add_z", 1), ("add_side", 0),
    ("finish", 0), ("add_side", 1), ("finish", 1),
)
UNITS = [op[1:] for op in PLAN if op[0] == "unit"]
SLOT = {u: i for i, u in enumerate(UNITS)}
WIDE = SLAB // 2
LONG = HALF // 2


class Sems:
    def __init__(self):
        self.at = {}
        self.count = 0

    def __call__(self, name, size=1):
        if name not in self.at:
            self.at[name] = self.count
            self.count += size
        return self.at[name]


NSEM = 256


def fused_kernel(
    selected, offered, qn, qr, go, lt, own_t, upw,
    out_n, out_r, out_l, out_w,
    own, box, qn2, qr2, go2, lt2, c, bias2, w, in_slab, in_long, stage,
    gqn, gqr, cg, cgl, got, own2, rope_a, rope_b, ct, lat, rope_acc,
    acc, xsend, xrecv, csend, crecv, y2s, y2r, y1s, y1r, zbuf, part, side_in, fin,
    ss, rs, ls,
):
    bf, f32 = jnp.bfloat16, jnp.float32
    me = Place()
    core, chip = me.core, me.chip
    sib = me.sibling()
    chip_at = [(chip + o) % 16 for o in range(16)]
    y_at = [(me.y + o) % 4 for o in range(4)]
    z_at = [(me.z + o) % 8 for o in range(8)]
    peers = [sib] + [me.in_ctx(chip_at[o], k) for o in (1, 2, 14, 15) for k in range(2)]
    peers += [(me.dp, (z_at[o] * 2 + me.xl) * 2 + core) for o in range(2, 7)]
    peers += [((me.dp + o) % 8, chip * 2 + k) for o in range(1, 8) for k in range(2)]
    peers += [me.cross()]
    barrier = signal_peers(peers)

    sem = Sems()
    sends = []
    local = []
    seen = set()

    def send(src, dst, name, device, land=None):
        at = sem(name)
        rdma(src(), dst(), ss.at[at], rs.at[at if land is None else land], device).start()
        sends.append((src, at))

    def got_it(ref, name):
        if name not in seen:
            seen.add(name)
            at = name if isinstance(name, int) else sem(name)
            rdma(ref, ref, ss.at[at], rs.at[at], sib).wait_recv()

    def copy(src, dst):
        cp = pltpu.make_async_copy(src, dst, ls.at[len(local)])
        cp.start()
        local.append(cp)

    def rows_at(start, size, unit=8):
        return pl.ds(pl.multiple_of(start, unit), size)

    def col(k, width):
        return pl.ds(pl.multiple_of(k * width, width), width)

    def cols_of(f, side, step):
        xh = me.xh if side == 0 else 1 - me.xh
        return col(f * 8 + xh * 4 + y_at[step], WIDE)

    def rows_of(k):
        return rows_at(k * TOK, TOK, TOK)

    def crows_of(k, size):
        return rows_at(k * CAND, size, TOK)

    qrow, crow = rows_of(core), crows_of(core, TOK)
    pairs = [
        (lambda k: qn.at[:, col(k, 4096)], lambda k: qn2.at[rows_of(k), :]),
        (lambda k: qr.at[:, col(k, 2048)], lambda k: qr2.at[rows_of(k), :]),
        (lambda k: go.at[:, col(k, 4096)], lambda k: go2.at[rows_of(k), :]),
        (lambda k: lt.at[col(k, 32), :], lambda k: lt2.at[k]),
    ]
    for src, dst in pairs:
        copy(src(core), dst(core))

    group = me.ctx
    latent = own_t[...].astype(f32).T
    own[...] = latent.astype(bf)
    c[crow, :] = latent.astype(bf)
    offer = [offered[group, m] for m in range(4)]
    for m in range(4):
        box[m] = jnp.where(offer[m] == 0, latent[:BLOCK], latent[BLOCK:]).astype(bf)
    ids = [group * 2, group * 2 + 1]
    for m, o in enumerate(offsets):
        source = group - o
        sender = jnp.maximum(source, 0)
        ids.append(jnp.where(source >= 0, sender * 2 + offered[sender, m], -1))
    lane64 = lax.broadcasted_iota(jnp.int32, (BLOCK, TOK), 1)
    inner = lax.broadcasted_iota(jnp.int32, (BLOCK, TOK), 0)
    for k in range(6):
        cols = []
        for q in range(2):
            hit = (selected[q, 0] == ids[k]) | (selected[q, 1] == ids[k]) | (selected[q, 2] == ids[k])
            off = jnp.where(hit & (ids[k] >= 0), 0.0, -1e30).astype(f32)
            if k == q:
                place = lane64 - q * BLOCK
                cols.append(jnp.where(place >= inner, 0.0, jnp.broadcast_to(off, (BLOCK, TOK))))
            else:
                cols.append(jnp.broadcast_to(off, (BLOCK, TOK)))
        bias2[rows_at(core * CAND + k * BLOCK, BLOCK, 64), :] = jnp.where(
            lane64 < BLOCK, cols[0], cols[1]).astype(bf)
    pl.semaphore_wait(barrier, len(peers))

    near = [sib, me.side(), (me.dp, me.ctx + 2 - 4 * me.xl + 1 - 2 * core)]
    near_core = [1 - core, core, 1 - core]
    near_at = [me.xl * 2 + 1 - core, (1 - me.xl) * 2 + core, (1 - me.xl) * 2 + 1 - core]

    def slab_in(k):
        return upw.at[:, col(k * 16 + me.dp, WIDE)]

    def long_in(k):
        return upw.at[:, col(k * 2 + 1, LONG)]

    for i in range(3):
        send(lambda i=i: slab_in(near_core[i]), lambda i=i: in_slab.at[i], ("slab", i), near[i])
    for i in range(3):
        send(lambda i=i: long_in(near_core[i]), lambda i=i: in_long.at[i], ("long", i), near[i])

    land0 = sem("offer_in", 8)
    for m, o in enumerate(offsets):
        target = (me.ctx + o) % 32
        place = rows_at((target % 2) * CAND + TOK + m * BLOCK, BLOCK, 64)
        for t in range(2):
            device = (me.dp, (target // 2) * 2 + t)
            land = land0 + m * 2 + target % 2
            if m == 0 and t == 0:
                at = sem("to_next")
                to_next = rdma(box.at[m], c.at[place, :], ss.at[at], rs.at[land], device)
                pl.when(core == 0)(
                    pltpu.make_async_copy(box.at[m], c.at[place, :], rs.at[land]).start)
                pl.when(core == 1)(to_next.start)
            else:
                send(lambda m=m: box.at[m], lambda place=place: c.at[place, :],
                     ("offer", m, t), device, land)
    shared = [(lambda k: own, lambda k: c.at[crows_of(k, TOK), :]),
              (lambda k: bias2.at[crows_of(1 - k, CAND), :], lambda k: bias2.at[crows_of(k, CAND), :])]
    for i, (src, dst) in enumerate(pairs + shared):
        send(lambda src=src: src(1 - core), lambda dst=dst: dst(core), ("sib", i), sib)

    my_rows = rows_at(me.z * 32, 32, 32)
    zrows = lambda o: rows_at(z_at[o % 8] * 32, 32, 32)
    at_z = lambda o: (me.dp, (z_at[o % 8] * 2 + me.xl) * 2 + core)

    def assemble(arrived, mine, width, name):
        stage[rows_at((me.xl * 2 + core) * 8, 8), 0:width] = mine.astype(f32)
        for i in range(3):
            got_it(arrived.at[i], (name, i))
            stage[rows_at(near_at[i] * 8, 8), 0:width] = arrived[i].astype(f32)
        return stage[:, 0:width].astype(bf)

    w[my_rows, cols_of(0, 0, 0)] = assemble(
        in_slab, upw[:, col(core * 16 + me.dp, WIDE)], WIDE, "slab")
    for o in range(1, 8):
        ref = lambda: w.at[my_rows, cols_of(0, 0, 0)]
        send(ref, ref, ("z", o), at_z(o))
    w[my_rows, LONG:] = assemble(in_long, upw[:, col(core * 2 + 1, LONG)], LONG, "long")

    lo, hi, whole = pl.ds(0, 128), pl.ds(128, 128), pl.ds(0, 256)
    sent_half = rows_at(me.xl * 128, 128, 128)
    got_half = rows_at((1 - me.xl) * 128, 128, 128)
    full_long = pl.ds(LONG, LONG)
    quarters = [pl.ds(LONG, LONG // 2), pl.ds(LONG + LONG // 2, LONG // 2)]

    def ring_ref(n, way):
        rows = zrows(8 - (n - 1) if way == 0 else n - 1)
        return w.at[rows, full_long if n < 4 else quarters[way]]

    def ring_in(n, way):
        rows = zrows(8 - n if way == 0 else n)
        return w.at[rows, full_long if n < 4 else quarters[way]]

    def along_z(f, n):
        for way in range(2):
            if n > 1:
                got_it(ring_in(n - 1, way), ("ring", n - 1, way))
            ref = lambda way=way: ring_ref(n, way)
            send(ref, ref, ("ring", n, way), at_z(1 if way == 0 else 7))

    along_z(1, 1)

    def weight_part(rows, side, step, name):
        got_it(w.at[rows, cols_of(0, side, step)], name)

    def need_block(f, side, step):
        if f == 1:
            for n in range(1, 5):
                for way in range(2):
                    got_it(ring_in(n, way), ("ring", n, way))
        elif side == 1:
            weight_part(got_half, 1, step, ("cross", step))
            weight_part(sent_half, 1, step, ("side", step))
        elif step == 0:
            for o in range(1, 8):
                got_it(w.at[zrows(8 - o), cols_of(0, 0, 0)], ("z", o))
        elif step == 2:
            weight_part(lo, 0, 2, "up2")
            weight_part(hi, 0, 2, "down2")
        else:
            weight_part(whole, 0, step, "up" if step == 3 else "down")

    def pass_on(rows, side, step, name, device):
        ref = lambda: w.at[rows, cols_of(0, side, step)]
        send(ref, ref, name, device)

    def along_y(f):
        need_block(0, 0, 0)
        pass_on(whole, 0, 0, "up", me.ring(1))
        pass_on(whole, 0, 0, "down", me.ring(3))

    def cross(f, step):
        need_block(0, 0, step)
        pass_on(sent_half, 0, step, ("cross", step), me.cross())

    def up(f):
        need_block(0, 0, 3)
        pass_on(lo, 0, 3, "up2", me.ring(1))

    def down(f):
        need_block(0, 0, 1)
        pass_on(hi, 0, 1, "down2", me.ring(3))

    def relay(f, step):
        weight_part(got_half, 1, step, ("cross", step))
        pass_on(got_half, 1, step, ("side", step), me.side())

    def add_x(f, step):
        at = f * 4 + step
        xsend[at] = acc[SLOT[f, 1, step], sent_half, :].astype(bf)
        send(lambda: xsend.at[at], lambda: xrecv.at[at], ("rx", at), me.side())

    def add_cross(f, step):
        at = f * 4 + step
        got_it(xrecv.at[at], ("rx", at))
        csend[at] = (acc[SLOT[f, 1, step], got_half, :] + xrecv[at].astype(f32)).astype(bf)
        send(lambda: csend.at[at], lambda: crecv.at[at], ("rc", at), me.cross())

    def crossed(f, step):
        at = f * 4 + step
        got_it(crecv.at[at], ("rc", at))
        acc[SLOT[f, 0, step], sent_half, :] += crecv[at].astype(f32)

    def add_y2(f):
        crossed(f, 2)
        for i, step in enumerate((1, 3)):
            at = f * 2 + i
            y2s[at] = acc[SLOT[f, 0, 2], i * 128:(i + 1) * 128, :].astype(bf)
            send(lambda at=at: y2s.at[at], lambda at=at: y2r.at[at], ("ry2", at), me.ring(step))

    def add_y1(f, i):
        step = (1, 3)[i]
        crossed(f, step)
        at = f * 2 + i
        got_it(y2r.at[at], ("ry2", at))
        slot = SLOT[f, 0, step]
        near_half, far = slice(i * 128, (i + 1) * 128), slice((1 - i) * 128, (2 - i) * 128)
        y1s[at, near_half, :] = (acc[slot, near_half, :] + y2r[at].astype(f32)).astype(bf)
        y1s[at, far, :] = acc[slot, far, :].astype(bf)
        send(lambda: y1s.at[at], lambda: y1r.at[at], ("ry1", at), me.ring(step))

    def add_z(f):
        slot = SLOT[f, 0, 0]
        crossed(f, 0)
        for i in range(2):
            got_it(y1r.at[f * 2 + i], ("ry1", f * 2 + i))
        acc[slot] = acc[slot] + (y1r[f * 2].astype(f32) + y1r[f * 2 + 1].astype(f32))
        for o in range(1, 8):
            send(lambda o=o: acc.at[slot, zrows(o), :], lambda o=o: zbuf.at[f * 8 + o],
                 ("rz", f, o), at_z(o))

    def add_side(f):
        total = acc[SLOT[f, 0, 0], my_rows, :]
        for o in range(1, 8):
            got_it(zbuf.at[f * 8 + o], ("rz", f, o))
            total = total + zbuf[f * 8 + o]
        part[f] = total
        send(lambda: part.at[f, rows_at((1 - me.xl) * 16, 16, 16), :], lambda: side_in.at[f],
             ("pair", f), me.side())

    def finish(f):
        got_it(side_in.at[f], ("pair", f))
        fin[f] = part[f, rows_at(me.xl * 16, 16, 16), :] + side_in[f]
        for o in range(8):
            for k in range(2):
                if o == 0 and k == 0:
                    continue
                to = core if k == 0 else 1 - core
                send(lambda to=to: fin.at[f, rows_at(to * 8, 8), :], lambda: out_cols(f, core, me.dp),
                     ("w", f, o, k), ((me.dp + o) % 8, chip * 2 + to))

    def out_cols(f, k, r):
        return out_w.at[:, col(k * 16 + f * 8 + r, WIDE)]

    actions = dict(
        along_y=along_y, along_z=along_z, cross=cross, up=up, down=down, relay=relay, add_x=add_x,
        add_cross=add_cross, add_y2=add_y2, add_y1=add_y1, add_z=add_z, add_side=add_side,
        finish=finish, unit=need_block)
    before, events = [], []
    for op in PLAN:
        events.append(op)
        if op[0] == "unit":
            before.append(events)
            events = []
    after = events

    def act(ops):
        for name, *where in ops:
            actions[name](*where)

    for cp in local:
        cp.wait()
    for i, (_, dst) in enumerate(pairs + shared):
        got_it(dst(1 - core), ("sib", i))
    for m in range(4):
        for g in range(2):
            got_it(c.at[pl.ds(g * CAND + TOK + m * BLOCK, BLOCK), :], land0 + m * 2 + g)
    zero = jnp.zeros((2 * CAND, ROPE), bf)
    rp = c[:, LAT:]
    rope_a[...] = jnp.concatenate([rp, zero], axis=1)
    rope_b[...] = jnp.concatenate([zero, rp], axis=1)
    ct[...] = c[:, :LAT].T
    lat[...] = jnp.zeros_like(lat)
    rope_acc[...] = jnp.zeros_like(rope_acc)
    lane = lax.broadcasted_iota(jnp.int32, (CAND, 128), 1)
    z128 = jnp.zeros((TOK, 128), bf)

    @pl.loop(0, 16)
    def _(s):
        for k, ops in enumerate(before):
            @pl.when(s == k)
            def _(ops=ops):
                act(ops)
        half, side, step = [
            sum((s == k).astype(jnp.int32) * u[i] for k, u in enumerate(UNITS) if u[i])
            for i in range(3)]
        xh = me.xh + side - 2 * me.xh * side
        p = half * 8 + xh * 4 + (me.y + step) % 4

        rcol = pl.ds(pl.multiple_of(p * 128, 128), 128)
        whs, kvs = [], []
        for e in range(2):
            wh = w[:, pl.ds(pl.multiple_of(p * 512 + e * 256, 256), 256)]
            whs.append(wh)
            kvs.append(mm(c[:, :LAT], wh).astype(bf))
        kgs = [[None, None], [None, None]]
        for g in range(2):
            rows = slice(g * CAND, (g + 1) * CAND)
            qs = slice(g * TOK, (g + 1) * TOK)
            qrp = qr2[qs, rcol]
            hcol = [pl.ds(pl.multiple_of(p * 256 + e * 128, 128), 128) for e in range(2)]
            gos = [go2[qs, hcol[e]] for e in range(2)]
            bd = jnp.concatenate(
                [jnp.concatenate([gos[0], z128], axis=1),
                 jnp.concatenate([z128, gos[1]], axis=1)], axis=0)
            vals = jnp.concatenate([kvs[0][rows, 128:], kvs[1][rows, 128:]], axis=1)
            dp_t = dg(vals, bd, NT)
            gr, rk, lows = None, [], []
            for e in range(2):
                rope = (rope_a if e == 0 else rope_b)[rows, :]
                kcat = jnp.concatenate([kvs[e][rows, :128], rope], axis=1)
                qcat = jnp.concatenate([qn2[qs, hcol[e]], qrp], axis=1)
                s_t = dg(kcat, qcat, NT)
                shift = bias2[rows, :].astype(f32) - lt2[g, pl.ds(p * 2 + e, 1), :]
                p_t = jnp.exp(s_t * SCALE + shift)
                d = dp_t[:, e * 128:(e + 1) * 128]
                rd = jnp.sum(p_t * d, axis=0, keepdims=True)
                sg = (p_t * (d - rd)).astype(bf)
                lows.append(p_t.astype(bf))
                gq = dg(sg, kcat, TN) * SCALE
                gqn[qs, hcol[e]] = gq[:, :128].astype(bf)
                gr = gq[:, 128:] if gr is None else gr + gq[:, 128:]
                kg = mm(sg, qcat) * SCALE
                rk.append(kg[:, 128:])
                kgs[e][g] = kg[:, :128].astype(bf)
            gqr[qs, rcol] = gr.astype(bf)
            vg = mm(jnp.concatenate(lows, axis=1), bd).astype(bf)
            for e in range(2):
                kgs[e][g] = jnp.concatenate([kgs[e][g], vg[:, e * 128:(e + 1) * 128]], axis=1)
            rope_acc[rows, :] += jnp.where(lane < ROPE, rk[0], rk[1])
        tot = None
        for e in range(2):
            kga = jnp.concatenate(kgs[e], axis=0)
            acc[s, :, e * 256:(e + 1) * 256] = mm(ct[...], kga)
            t = dg(kga, whs[e], NT)
            tot = t if tot is None else tot + t
        lat[...] += tot

    last = after.index(("add_z", 1)) + 1
    act(after[:last])
    ra = rope_acc[...]
    full = jnp.concatenate([lat[...], ra[:, :ROPE] + ra[:, ROPE:]], axis=1)
    cg[...] = full
    cgl[...] = full.astype(bf)

    back0 = sem("back_in", 8)
    for m, o in enumerate(offsets):
        for g in range(2):
            target = (chip * 2 + g + 32 - o) % 32
            src = lambda m=m, g=g: cgl.at[pl.ds(g * CAND + TOK + m * BLOCK, BLOCK), :]
            dst = lambda m=m: got.at[m * 2 + core]
            land = back0 + m * 2 + core
            if m == 0 and g == 1:
                at = sem("to_last")
                to_last = rdma(src(), dst(), ss.at[at], rs.at[land], (me.dp, target))
                pl.when(core == 0)(pltpu.make_async_copy(src(), dst(), rs.at[land]).start)
                pl.when(core == 1)(to_last.start)
            else:
                send(src, dst, ("back", m, g), (me.dp, target), land)

    ncol = lambda k: out_n.at[:, col(k, 4096)]
    rcol_ = lambda k: out_r.at[:, col(k, 2048)]
    send(lambda: cg.at[crows_of(1 - core, TOK), :], lambda: own2, "back_o", sib)
    send(lambda: gqn.at[rows_of(1 - core), :], lambda: ncol(core), "back_n", sib)
    send(lambda: gqr.at[rows_of(1 - core), :], lambda: rcol_(core), "back_r", sib)
    first_late = len(local)
    copy(gqn.at[qrow, :], ncol(core))
    copy(gqr.at[qrow, :], rcol_(core))

    act(after[last:-2])

    got_it(own2, "back_o")
    total = cg[crow, :] + own2[...]
    first, second = total[:BLOCK], total[BLOCK:]
    for m in range(4):
        for k in range(2):
            got_it(got.at[m * 2 + k], back0 + m * 2 + k)
        rows = got[m * 2].astype(f32) + got[m * 2 + 1].astype(f32)
        nil = jnp.zeros_like(rows)
        first = first + jnp.where(offer[m] == 0, rows, nil)
        second = second + jnp.where(offer[m] == 0, nil, rows)
    out_l[0:BLOCK, :] = first
    out_l[BLOCK:TOK, :] = second

    act(after[-2:])
    for f in range(2):
        copy(fin.at[f, rows_at(core * 8, 8), :], out_cols(f, core, me.dp))
    got_it(ncol(1 - core), "back_n")
    got_it(rcol_(1 - core), "back_r")
    for f in range(2):
        for o in range(8):
            for k in range(2):
                if o == 0 and k == 0:
                    continue
                who = core if k == 0 else 1 - core
                got_it(out_cols(f, who, (me.dp + 8 - o) % 8), ("w", f, o, k))
    for cp in local[first_late:]:
        cp.wait()
    pl.when(core == 1)(to_next.wait_send)
    pl.when(core == 1)(to_last.wait_send)
    for src, at in sends:
        rdma(src(), src(), ss.at[at], rs.at[at], sib).wait_send()
    assert sem.count <= NSEM, sem.count


def fused_call(selected, offered, qn, qr, go, lt, own_t, upw):
    bf, f32 = jnp.bfloat16, jnp.float32
    dma = pltpu.SemaphoreType.DMA
    v = pltpu.VMEM
    smem = pl.BlockSpec(memory_space=pltpu.SMEM)
    return pl.pallas_call(
        fused_kernel,
        out_shape=(
            jax.ShapeDtypeStruct((TOK, HEADS * NOPE), bf),
            jax.ShapeDtypeStruct((TOK, HEADS * ROPE), bf),
            jax.ShapeDtypeStruct((TOK, LAT + ROPE), f32),
            jax.ShapeDtypeStruct((8, 2 * HALF), f32),
        ),
        in_specs=[smem, smem] + [ANY] * 4 + [VMEM, VMEM],
        out_specs=(ANY, ANY, VMEM, ANY),
        scratch_shapes=[
            v((TOK, LAT + ROPE), bf), v((4, BLOCK, LAT + ROPE), bf),
            v((2 * TOK, 4096), bf), v((2 * TOK, 2048), bf), v((2 * TOK, 4096), bf),
            v((2, HALF_HEADS, TOK), f32), v((2 * CAND, LAT + ROPE), bf), v((2 * CAND, TOK), bf),
            v((LAT, HALF), bf), v((3, 8, WIDE), bf), v((3, 8, LONG), bf), v((32, LONG), f32),
            v((2 * TOK, 4096), bf), v((2 * TOK, 2048), bf),
            v((2 * CAND, LAT + ROPE), f32), v((2 * CAND, LAT + ROPE), bf),
            v((8, BLOCK, LAT + ROPE), bf), v((TOK, LAT + ROPE), f32),
            v((2 * CAND, 128), bf), v((2 * CAND, 128), bf), v((LAT, 2 * CAND), bf),
            v((2 * CAND, LAT), f32), v((2 * CAND, 128), f32),
            v((16, LAT, WIDE), f32),
            v((8, 128, WIDE), bf), v((8, 128, WIDE), bf), v((8, 128, WIDE), bf),
            v((8, 128, WIDE), bf),
            v((4, 128, WIDE), bf), v((4, 128, WIDE), bf),
            v((4, 256, WIDE), bf), v((4, 256, WIDE), bf),
            v((16, 32, WIDE), f32), v((2, 32, WIDE), f32), v((2, 16, WIDE), f32),
            v((2, 16, WIDE), f32),
            dma((NSEM,)), dma((NSEM,)), dma((16,)),
        ],
        compiler_params=pltpu.CompilerParams(
            collective_id=0, has_side_effects=True, vmem_limit_bytes=56 << 20),
        name="fused_backward",
    )(selected, offered, qn, qr, go, lt, own_t, upw)


def shards(q_nope, q_rope, grad_out, log_total, kv_latent, up_weight, selected, offered):
    out_n, out_r, out_l, out_w = fused_call(
        selected[0], offered[0], q_nope[0], q_rope[0], grad_out[0], log_total[0], kv_latent[0].T,
        up_weight)
    return (out_n[None], out_r[None], out_l[None], out_w)


def solution(mesh):
    in_specs = (
        P("dp", "ctx", None),
        P("dp", "ctx", None),
        P("dp", "ctx", None),
        P("dp", None, "ctx"),
        P("dp", "ctx", None),
        P("ctx", None),
        P("dp", "ctx", None),
        P("dp", None, None),
    )
    out_specs = (P("dp", "ctx", None), P("dp", "ctx", None), P("dp", "ctx", None), P("ctx", None))
    return jax.shard_map(shards, mesh=mesh, in_specs=in_specs, out_specs=out_specs, check_vma=False)
```

```python
import functools

import jax
import jax.numpy as jnp
from jax import lax
from jax.experimental import pallas as pl
from jax.experimental.pallas import tpu as pltpu
from jax.sharding import PartitionSpec as P

LAT = 256
ROPE = 64
NOPE = 128
VDIM = 128
BLOCK = 64
HEADS = 64
HALF_HEADS = 32
CAND = 384
TOK = 128
HALF = 8192
SLAB = 1024

offsets = (1, 2, 3, 4)
MESH = pl.DeviceIdType.MESH
NT = (((1,), (1,)), ((), ()))
TN = (((0,), (0,)), ((), ()))
VMEM = pl.BlockSpec(memory_space=pltpu.VMEM)
ANY = pl.BlockSpec(memory_space=pl.ANY)


class Place:
    def __init__(self):
        self.dp = lax.axis_index("dp")
        self.ctx = lax.axis_index("ctx")
        self.xh = self.dp // 4
        self.y = self.dp % 4
        self.core = self.ctx % 2
        self.chip = self.ctx // 2
        self.xl = self.chip % 2
        self.z = self.chip // 2

    def sibling(self):
        return (self.dp, self.ctx + 1 - 2 * self.core)

    def in_ctx(self, chip, core):
        return (self.dp, chip * 2 + core)

    def side(self):
        return (self.dp, self.ctx + 2 - 4 * self.xl)

    def along_z(self, step):
        return (self.dp, (self.ctx + 4 * step) % 32)

    def cross(self):
        return ((1 - self.xh) * 4 + self.y, self.ctx + 2 - 4 * self.xl)

    def ring(self, step):
        return (self.xh * 4 + (self.y + step) % 4, self.ctx)


def rdma(src, dst, send, recv, device):
    return pltpu.make_async_remote_copy(
        src_ref=src, dst_ref=dst, send_sem=send, recv_sem=recv, device_id=device,
        device_id_type=MESH,
    )


def signal_peers(devices):
    barrier = pltpu.get_barrier_semaphore()
    for device in devices:
        pl.semaphore_signal(barrier, inc=1, device_id=device, device_id_type=MESH)
    return barrier


def dg(a, b, dims):
    return lax.dot_general(a, b, dims, preferred_element_type=jnp.float32)


def mm(a, b):
    return jnp.dot(a, b, preferred_element_type=jnp.float32)


SCALE = 1.0 / float(NOPE + ROPE) ** 0.5


PLAN = (
    ("cross", 0, 0), ("along_y", 0), ("relay", 0, 0), ("unit", 0, 0, 0), ("cross", 0, 1),
    ("cross", 0, 3), ("down", 0), ("up", 0), ("along_z", 1, 2), ("unit", 0, 0, 1),
    ("unit", 0, 0, 3), ("cross", 0, 2), ("relay", 0, 1), ("unit", 0, 1, 0), ("relay", 0, 3),
    ("along_z", 1, 3), ("unit", 0, 0, 2), ("relay", 0, 2), ("unit", 0, 1, 1), ("add_x", 0, 1),
    ("unit", 0, 1, 3), ("along_z", 1, 4), ("unit", 0, 1, 2), ("add_x", 0, 2), ("add_x", 0, 3),
    ("add_cross", 0, 1), ("add_x", 0, 0), ("unit", 1, 1, 2), ("add_x", 1, 2), ("add_cross", 0, 2),
    ("unit", 1, 1, 1), ("unit", 1, 1, 0), ("add_y2", 0), ("add_cross", 0, 3), ("add_cross", 0, 0),
    ("unit", 1, 1, 3), ("add_x", 1, 1), ("add_x", 1, 3), ("add_x", 1, 0), ("add_cross", 1, 2),
    ("add_y1", 0, 0), ("add_y1", 0, 1), ("unit", 1, 0, 2), ("add_cross", 1, 1), ("unit", 1, 0, 1),
    ("add_cross", 1, 3), ("add_y2", 1), ("unit", 1, 0, 3), ("add_z", 0), ("add_cross", 1, 0),
    ("add_y1", 1, 0), ("add_y1", 1, 1), ("unit", 1, 0, 0), ("add_z", 1), ("add_side", 0),
    ("finish", 0), ("add_side", 1), ("finish", 1),
)
UNITS = [op[1:] for op in PLAN if op[0] == "unit"]
SLOT = {u: i for i, u in enumerate(UNITS)}
WIDE = SLAB // 2
LONG = HALF // 2


class Sems:
    def __init__(self):
        self.at = {}
        self.count = 0

    def __call__(self, name, size=1):
        if name not in self.at:
            self.at[name] = self.count
            self.count += size
        return self.at[name]


NSEM = 256


def fused_kernel(
    selected, offered, qn, qr, go, lt, own_t, upw,
    out_n, out_r, out_l, out_w,
    own, box, qn2, qr2, go2, lt2, c, bias2, w, in_slab, in_long, stage,
    gqn, gqr, cg, cgl, got, own2, rope_a, rope_b, ct, lat, rope_acc,
    acc, xsend, xrecv, csend, crecv, y2s, y2r, y1s, y1r, zbuf, part, side_in, low, low_in, fin,
    ss, rs, ls,
):
    bf, f32 = jnp.bfloat16, jnp.float32
    me = Place()
    core, chip = me.core, me.chip
    sib = me.sibling()
    chip_at = [(chip + o) % 16 for o in range(16)]
    y_at = [(me.y + o) % 4 for o in range(4)]
    z_at = [(me.z + o) % 8 for o in range(8)]
    peers = [(me.dp, (me.ctx + o) % 32) for o in (1, 2, 3, 4, 28, 29, 30, 31)]
    peers += [me.in_ctx(chip_at[o], core) for o in range(3, 14)]
    peers += [((me.dp + o) % 8, chip * 2 + k) for o in range(1, 8) for k in range(2)]
    peers += [me.cross()]
    barrier = signal_peers(peers)

    sem = Sems()
    sends = []
    local = []
    seen = set()

    def send(src, dst, name, device):
        at = sem(name)
        rdma(src(), dst(), ss.at[at], rs.at[at], device).start()
        sends.append((src, at))

    def got_it(ref, name):
        if name not in seen:
            seen.add(name)
            at = sem(name)
            rdma(ref, ref, ss.at[at], rs.at[at], sib).wait_recv()

    def copy(src, dst):
        cp = pltpu.make_async_copy(src, dst, ls.at[len(local)])
        cp.start()
        local.append(cp)

    def rows_at(start, size, unit=8):
        return pl.ds(pl.multiple_of(start, unit), size)

    def col(k, width):
        return pl.ds(pl.multiple_of(k * width, width), width)

    def cols_of(f, side, step):
        xh = me.xh if side == 0 else 1 - me.xh
        return col(f * 8 + xh * 4 + y_at[step], WIDE)

    def rows_of(k):
        return rows_at(k * TOK, TOK, TOK)

    def crows_of(k, size):
        return rows_at(k * CAND, size, TOK)

    qrow, crow = rows_of(core), crows_of(core, TOK)
    pairs = [
        (lambda k: qn.at[:, col(k, 4096)], lambda k: qn2.at[rows_of(k), :]),
        (lambda k: qr.at[:, col(k, 2048)], lambda k: qr2.at[rows_of(k), :]),
        (lambda k: go.at[:, col(k, 4096)], lambda k: go2.at[rows_of(k), :]),
        (lambda k: lt.at[col(k, 32), :], lambda k: lt2.at[k]),
    ]
    for src, dst in pairs:
        copy(src(core), dst(core))

    group = me.ctx
    latent = own_t[...].astype(f32).T
    own[...] = latent.astype(bf)
    c[crow, :] = latent.astype(bf)
    offer = [offered[m, group] for m in range(4)]
    for m in range(4):
        box[m] = jnp.where(offer[m] == 0, latent[:BLOCK], latent[BLOCK:]).astype(bf)
    ids = [group * 2, group * 2 + 1]
    for m, o in enumerate(offsets):
        source = group - o
        sender = jnp.maximum(source, 0)
        ids.append(jnp.where(source >= 0, sender * 2 + offered[m, sender], -1))
    lane64 = lax.broadcasted_iota(jnp.int32, (BLOCK, TOK), 1)
    inner = lax.broadcasted_iota(jnp.int32, (BLOCK, TOK), 0)
    for k in range(6):
        cols = []
        for q in range(2):
            hit = (selected[q, 0] == ids[k]) | (selected[q, 1] == ids[k]) | (selected[q, 2] == ids[k])
            off = jnp.where(hit & (ids[k] >= 0), 0.0, -1e30).astype(f32)
            if k == q:
                place = lane64 - q * BLOCK
                cols.append(jnp.where(place >= inner, 0.0, jnp.broadcast_to(off, (BLOCK, TOK))))
            else:
                cols.append(jnp.broadcast_to(off, (BLOCK, TOK)))
        bias2[rows_at(core * CAND + k * BLOCK, BLOCK, 64), :] = jnp.where(
            lane64 < BLOCK, cols[0], cols[1]).astype(bf)
    pl.semaphore_wait(barrier, len(peers))

    near = [sib, me.side(), (me.dp, me.ctx + 2 - 4 * me.xl + 1 - 2 * core)]
    near_core = [1 - core, core, 1 - core]
    near_at = [me.xl * 2 + 1 - core, (1 - me.xl) * 2 + core, (1 - me.xl) * 2 + 1 - core]

    def slab_in(k):
        return upw.at[:, col(k * 16 + me.dp, WIDE)]

    def long_in(k):
        return upw.at[:, col(k * 2 + 1, LONG)]

    for i in range(3):
        send(lambda i=i: slab_in(near_core[i]), lambda i=i: in_slab.at[i], ("slab", i), near[i])
    for i in range(3):
        send(lambda i=i: long_in(near_core[i]), lambda i=i: in_long.at[i], ("long", i), near[i])

    for m, o in enumerate(offsets):
        to = (me.ctx + o) % 32
        place = rows_at((to % 2) * CAND + TOK + m * BLOCK, BLOCK, 64)
        send(lambda m=m: box.at[m], lambda place=place: c.at[place, :], ("offer", m), (me.dp, to))
    shared = [(lambda k: own, lambda k: c.at[crows_of(k, TOK), :]),
              (lambda k: bias2.at[crows_of(1 - k, CAND), :], lambda k: bias2.at[crows_of(k, CAND), :])]
    for i, (src, dst) in enumerate(pairs + shared):
        send(lambda src=src: src(1 - core), lambda dst=dst: dst(core), ("sib", i), sib)

    def offered_rows(k):
        return c.at[rows_at(k * CAND + TOK, 4 * BLOCK, TOK), :]

    my_rows = rows_at(me.z * 32, 32, 32)
    zrows = lambda o: rows_at(z_at[o % 8] * 32, 32, 32)
    at_z = lambda o: (me.dp, (z_at[o % 8] * 2 + me.xl) * 2 + core)

    def assemble(arrived, mine, width, name):
        stage[rows_at((me.xl * 2 + core) * 8, 8), 0:width] = mine.astype(f32)
        for i in range(3):
            got_it(arrived.at[i], (name, i))
            stage[rows_at(near_at[i] * 8, 8), 0:width] = arrived[i].astype(f32)
        return stage[:, 0:width].astype(bf)

    w[my_rows, cols_of(0, 0, 0)] = assemble(
        in_slab, upw[:, col(core * 16 + me.dp, WIDE)], WIDE, "slab")
    for o in range(1, 8):
        ref = lambda: w.at[my_rows, cols_of(0, 0, 0)]
        send(ref, ref, ("z", o), at_z(o))
    w[my_rows, LONG:] = assemble(in_long, upw[:, col(core * 2 + 1, LONG)], LONG, "long")

    lo, hi, whole = pl.ds(0, 128), pl.ds(128, 128), pl.ds(0, 256)
    sent_half = rows_at(me.xl * 128, 128, 128)
    got_half = rows_at((1 - me.xl) * 128, 128, 128)
    full_long = pl.ds(LONG, LONG)
    quarters = [pl.ds(LONG, LONG // 2), pl.ds(LONG + LONG // 2, LONG // 2)]

    def ring_ref(n, way):
        rows = zrows(8 - (n - 1) if way == 0 else n - 1)
        return w.at[rows, full_long if n < 4 else quarters[way]]

    def ring_in(n, way):
        rows = zrows(8 - n if way == 0 else n)
        return w.at[rows, full_long if n < 4 else quarters[way]]

    def along_z(f, n):
        for way in range(2):
            if n > 1:
                got_it(ring_in(n - 1, way), ("ring", n - 1, way))
            ref = lambda way=way: ring_ref(n, way)
            send(ref, ref, ("ring", n, way), at_z(1 if way == 0 else 7))

    along_z(1, 1)
    for m in range(4):
        got_it(c.at[rows_at(core * CAND + TOK + m * BLOCK, BLOCK, 64), :], ("offer", m))
    send(lambda: offered_rows(core), lambda: offered_rows(core), "offer_on", sib)

    def weight_part(rows, side, step, name):
        got_it(w.at[rows, cols_of(0, side, step)], name)

    def need_block(f, side, step):
        if f == 1:
            for n in range(1, 5):
                for way in range(2):
                    got_it(ring_in(n, way), ("ring", n, way))
        elif side == 1:
            weight_part(got_half, 1, step, ("cross", step))
            weight_part(sent_half, 1, step, ("side", step))
        elif step == 0:
            for o in range(1, 8):
                got_it(w.at[zrows(8 - o), cols_of(0, 0, 0)], ("z", o))
        elif step == 2:
            weight_part(lo, 0, 2, "up2")
            weight_part(hi, 0, 2, "down2")
        else:
            weight_part(whole, 0, step, "up" if step == 3 else "down")

    def pass_on(rows, side, step, name, device):
        ref = lambda: w.at[rows, cols_of(0, side, step)]
        send(ref, ref, name, device)

    def along_y(f):
        need_block(0, 0, 0)
        pass_on(whole, 0, 0, "up", me.ring(1))
        pass_on(whole, 0, 0, "down", me.ring(3))

    def cross(f, step):
        need_block(0, 0, step)
        pass_on(sent_half, 0, step, ("cross", step), me.cross())

    def up(f):
        need_block(0, 0, 3)
        pass_on(lo, 0, 3, "up2", me.ring(1))

    def down(f):
        need_block(0, 0, 1)
        pass_on(hi, 0, 1, "down2", me.ring(3))

    def relay(f, step):
        weight_part(got_half, 1, step, ("cross", step))
        pass_on(got_half, 1, step, ("side", step), me.side())

    def add_x(f, step):
        at = f * 4 + step
        xsend[at] = acc[SLOT[f, 1, step], sent_half, :].astype(bf)
        send(lambda: xsend.at[at], lambda: xrecv.at[at], ("rx", at), me.side())

    def add_cross(f, step):
        at = f * 4 + step
        got_it(xrecv.at[at], ("rx", at))
        csend[at] = (acc[SLOT[f, 1, step], got_half, :] + xrecv[at].astype(f32)).astype(bf)
        send(lambda: csend.at[at], lambda: crecv.at[at], ("rc", at), me.cross())

    def crossed(f, step):
        at = f * 4 + step
        got_it(crecv.at[at], ("rc", at))
        acc[SLOT[f, 0, step], sent_half, :] += crecv[at].astype(f32)

    def add_y2(f):
        crossed(f, 2)
        for i, step in enumerate((1, 3)):
            at = f * 2 + i
            y2s[at] = acc[SLOT[f, 0, 2], i * 128:(i + 1) * 128, :].astype(bf)
            send(lambda at=at: y2s.at[at], lambda at=at: y2r.at[at], ("ry2", at), me.ring(step))

    def add_y1(f, i):
        step = (1, 3)[i]
        crossed(f, step)
        at = f * 2 + i
        got_it(y2r.at[at], ("ry2", at))
        slot = SLOT[f, 0, step]
        near_half, far = slice(i * 128, (i + 1) * 128), slice((1 - i) * 128, (2 - i) * 128)
        y1s[at, near_half, :] = (acc[slot, near_half, :] + y2r[at].astype(f32)).astype(bf)
        y1s[at, far, :] = acc[slot, far, :].astype(bf)
        send(lambda: y1s.at[at], lambda: y1r.at[at], ("ry1", at), me.ring(step))

    def add_z(f):
        slot = SLOT[f, 0, 0]
        crossed(f, 0)
        for i in range(2):
            got_it(y1r.at[f * 2 + i], ("ry1", f * 2 + i))
        acc[slot] = acc[slot] + (y1r[f * 2].astype(f32) + y1r[f * 2 + 1].astype(f32))
        if f == 1:
            low[...] = acc[slot].astype(bf)
            for o in range(1, 16):
                send(lambda o=o: low.at[rows_at(chip_at[o] * 16, 16, 16), :], lambda o=o: low_in.at[o],
                     ("rz", f, o), me.in_ctx(chip_at[o], core))
            return
        for o in range(1, 8):
            send(lambda o=o: acc.at[slot, zrows(o), :], lambda o=o: zbuf.at[o], ("rz", f, o), at_z(o))

    def add_side(f):
        if f == 1:
            total = acc[SLOT[f, 0, 0], rows_at(chip * 16, 16, 16), :]
            for o in range(1, 16):
                got_it(low_in.at[o], ("rz", f, o))
                total = total + low_in[o].astype(f32)
            fin[f] = total
            return
        total = acc[SLOT[f, 0, 0], my_rows, :]
        for o in range(1, 8):
            got_it(zbuf.at[o], ("rz", f, o))
            total = total + zbuf[o]
        part[...] = total
        send(lambda: part.at[rows_at((1 - me.xl) * 16, 16, 16), :], lambda: side_in, "pair", me.side())

    def finish(f):
        if f == 0:
            got_it(side_in, "pair")
            fin[f] = part[rows_at(me.xl * 16, 16, 16), :] + side_in[...]
        for o in range(8):
            for k in range(2):
                if o == 0 and k == 0:
                    continue
                to = core if k == 0 else 1 - core
                send(lambda to=to: fin.at[f, rows_at(to * 8, 8), :], lambda: out_cols(f, core, me.dp),
                     ("w", f, o, k), ((me.dp + o) % 8, chip * 2 + to))

    def out_cols(f, k, r):
        return out_w.at[:, col(k * 16 + f * 8 + r, WIDE)]

    actions = dict(
        along_y=along_y, along_z=along_z, cross=cross, up=up, down=down, relay=relay, add_x=add_x,
        add_cross=add_cross, add_y2=add_y2, add_y1=add_y1, add_z=add_z, add_side=add_side,
        finish=finish, unit=need_block)
    before, events = [], []
    for op in PLAN:
        events.append(op)
        if op[0] == "unit":
            before.append(events)
            events = []
    after = events

    def act(ops):
        for name, *where in ops:
            actions[name](*where)

    for cp in local:
        cp.wait()
    for i, (_, dst) in enumerate(pairs + shared):
        got_it(dst(1 - core), ("sib", i))
    got_it(offered_rows(1 - core), "offer_on")
    zero = jnp.zeros((2 * CAND, ROPE), bf)
    rp = c[:, LAT:]
    rope_a[...] = jnp.concatenate([rp, zero], axis=1)
    rope_b[...] = jnp.concatenate([zero, rp], axis=1)
    ct[...] = c[:, :LAT].T
    lat[...] = jnp.zeros_like(lat)
    rope_acc[...] = jnp.zeros_like(rope_acc)
    lane = lax.broadcasted_iota(jnp.int32, (CAND, 128), 1)
    z128 = jnp.zeros((TOK, 128), bf)

    @pl.loop(0, 16)
    def _(s):
        for k, ops in enumerate(before):
            @pl.when(s == k)
            def _(ops=ops):
                act(ops)
        half, side, step = [
            sum((s == k).astype(jnp.int32) * u[i] for k, u in enumerate(UNITS) if u[i])
            for i in range(3)]
        xh = me.xh + side - 2 * me.xh * side
        p = half * 8 + xh * 4 + (me.y + step) % 4

        rcol = pl.ds(pl.multiple_of(p * 128, 128), 128)
        whs, kvs = [], []
        for e in range(2):
            wh = w[:, pl.ds(pl.multiple_of(p * 512 + e * 256, 256), 256)]
            whs.append(wh)
            kvs.append(mm(c[:, :LAT], wh).astype(bf))
        kgs = [[None, None], [None, None]]
        for g in range(2):
            rows = slice(g * CAND, (g + 1) * CAND)
            qs = slice(g * TOK, (g + 1) * TOK)
            qrp = qr2[qs, rcol]
            hcol = [pl.ds(pl.multiple_of(p * 256 + e * 128, 128), 128) for e in range(2)]
            gos = [go2[qs, hcol[e]] for e in range(2)]
            bd = jnp.concatenate(
                [jnp.concatenate([gos[0], z128], axis=1),
                 jnp.concatenate([z128, gos[1]], axis=1)], axis=0)
            vals = jnp.concatenate([kvs[0][rows, 128:], kvs[1][rows, 128:]], axis=1)
            dp_t = dg(vals, bd, NT)
            gr, rk, lows = None, [], []
            for e in range(2):
                rope = (rope_a if e == 0 else rope_b)[rows, :]
                kcat = jnp.concatenate([kvs[e][rows, :128], rope], axis=1)
                qcat = jnp.concatenate([qn2[qs, hcol[e]], qrp], axis=1)
                s_t = dg(kcat, qcat, NT)
                shift = bias2[rows, :].astype(f32) - lt2[g, pl.ds(p * 2 + e, 1), :]
                p_t = jnp.exp(s_t * SCALE + shift)
                d = dp_t[:, e * 128:(e + 1) * 128]
                rd = jnp.sum(p_t * d, axis=0, keepdims=True)
                sg = (p_t * (d - rd)).astype(bf)
                lows.append(p_t.astype(bf))
                gq = dg(sg, kcat, TN) * SCALE
                gqn[qs, hcol[e]] = gq[:, :128].astype(bf)
                gr = gq[:, 128:] if gr is None else gr + gq[:, 128:]
                kg = mm(sg, qcat) * SCALE
                rk.append(kg[:, 128:])
                kgs[e][g] = kg[:, :128].astype(bf)
            gqr[qs, rcol] = gr.astype(bf)
            vg = mm(jnp.concatenate(lows, axis=1), bd).astype(bf)
            for e in range(2):
                kgs[e][g] = jnp.concatenate([kgs[e][g], vg[:, e * 128:(e + 1) * 128]], axis=1)
            rope_acc[rows, :] += jnp.where(lane < ROPE, rk[0], rk[1])
        tot = None
        for e in range(2):
            kga = jnp.concatenate(kgs[e], axis=0)
            acc[s, :, e * 256:(e + 1) * 256] = mm(ct[...], kga)
            t = dg(kga, whs[e], NT)
            tot = t if tot is None else tot + t
        lat[...] += tot

    last = after.index(("add_z", 1)) + 1
    act(after[:last])
    late = [op for op in after[last:] if op[1] == 1]
    ra = rope_acc[...]
    cg[...] = jnp.concatenate([lat[...], ra[:, :ROPE] + ra[:, ROPE:]], axis=1)
    send(lambda: cg.at[crows_of(1 - core, CAND), :], lambda: own2, "back_o", sib)
    act(op for op in after[last:] if op[1] == 0)

    got_it(own2, "back_o")
    mine = cg[crows_of(core, CAND), :] + own2[...]
    for m, o in enumerate(offsets):
        cgl[m] = mine[TOK + m * BLOCK:TOK + (m + 1) * BLOCK].astype(bf)
        send(lambda m=m: cgl.at[m], lambda m=m: got.at[m], ("back", m), (me.dp, (me.ctx + 32 - o) % 32))

    ncol = lambda k: out_n.at[:, col(k, 4096)]
    rcol_ = lambda k: out_r.at[:, col(k, 2048)]
    send(lambda: gqn.at[rows_of(1 - core), :], lambda: ncol(core), "back_n", sib)
    send(lambda: gqr.at[rows_of(1 - core), :], lambda: rcol_(core), "back_r", sib)
    first_late = len(local)
    copy(gqn.at[qrow, :], ncol(core))
    copy(gqr.at[qrow, :], rcol_(core))

    act(late)

    first, second = mine[:BLOCK], mine[BLOCK:TOK]
    for m in range(4):
        got_it(got.at[m], ("back", m))
        rows = got[m].astype(f32)
        nil = jnp.zeros_like(rows)
        first = first + jnp.where(offer[m] == 0, rows, nil)
        second = second + jnp.where(offer[m] == 0, nil, rows)
    out_l[...] = jnp.concatenate([first, second], axis=0).T
    for f in range(2):
        copy(fin.at[f, rows_at(core * 8, 8), :], out_cols(f, core, me.dp))
    got_it(ncol(1 - core), "back_n")
    got_it(rcol_(1 - core), "back_r")
    for f in range(2):
        for o in range(8):
            for k in range(2):
                if o == 0 and k == 0:
                    continue
                who = core if k == 0 else 1 - core
                got_it(out_cols(f, who, (me.dp + 8 - o) % 8), ("w", f, o, k))
    for cp in local[first_late:]:
        cp.wait()
    for src, at in sends:
        rdma(src(), src(), ss.at[at], rs.at[at], sib).wait_send()
    assert sem.count <= NSEM, sem.count


def fused_call(selected, offered, qn, qr, go, lt, own_t, upw):
    bf, f32 = jnp.bfloat16, jnp.float32
    dma = pltpu.SemaphoreType.DMA
    v = pltpu.VMEM
    smem = pl.BlockSpec(memory_space=pltpu.SMEM)
    return pl.pallas_call(
        fused_kernel,
        out_shape=(
            jax.ShapeDtypeStruct((TOK, HEADS * NOPE), bf),
            jax.ShapeDtypeStruct((TOK, HEADS * ROPE), bf),
            jax.ShapeDtypeStruct((LAT + ROPE, TOK), f32),
            jax.ShapeDtypeStruct((8, 2 * HALF), f32),
        ),
        in_specs=[smem, smem] + [ANY] * 4 + [VMEM, VMEM],
        out_specs=(ANY, ANY, VMEM, ANY),
        scratch_shapes=[
            v((TOK, LAT + ROPE), bf), v((4, BLOCK, LAT + ROPE), bf),
            v((2 * TOK, 4096), bf), v((2 * TOK, 2048), bf), v((2 * TOK, 4096), bf),
            v((2, HALF_HEADS, TOK), f32), v((2 * CAND, LAT + ROPE), bf), v((2 * CAND, TOK), bf),
            v((LAT, HALF), bf), v((3, 8, WIDE), bf), v((3, 8, LONG), bf), v((32, LONG), f32),
            v((2 * TOK, 4096), bf), v((2 * TOK, 2048), bf),
            v((2 * CAND, LAT + ROPE), f32), v((4, BLOCK, LAT + ROPE), bf),
            v((4, BLOCK, LAT + ROPE), bf), v((CAND, LAT + ROPE), f32),
            v((2 * CAND, 128), bf), v((2 * CAND, 128), bf), v((LAT, 2 * CAND), bf),
            v((2 * CAND, LAT), f32), v((2 * CAND, 128), f32),
            v((16, LAT, WIDE), f32),
            v((8, 128, WIDE), bf), v((8, 128, WIDE), bf), v((8, 128, WIDE), bf),
            v((8, 128, WIDE), bf),
            v((4, 128, WIDE), bf), v((4, 128, WIDE), bf),
            v((4, 256, WIDE), bf), v((4, 256, WIDE), bf),
            v((8, 32, WIDE), f32), v((32, WIDE), f32), v((16, WIDE), f32),
            v((LAT, WIDE), bf), v((16, 16, WIDE), bf), v((2, 16, WIDE), f32),
            dma((NSEM,)), dma((NSEM,)), dma((16,)),
        ],
        compiler_params=pltpu.CompilerParams(
            collective_id=0, has_side_effects=True, vmem_limit_bytes=56 << 20),
        name="fused_backward",
    )(selected, offered, qn, qr, go, lt, own_t, upw)


def hand_over_kernel(a, b, c, d, out_a, out_b, out_c, out_d):
    out_a[...] = a[...]
    out_b[...] = b[...]
    out_c[...] = c[...]
    out_d[...] = d[...]


def hand_over(*arrays):
    steps = 8
    specs = []
    for a in arrays:
        if a.shape[0] == 8:
            specs.append(pl.BlockSpec((8, a.shape[1] // steps), lambda i: (0, i)))
        else:
            specs.append(pl.BlockSpec((a.shape[0] // steps, a.shape[1]), lambda i: (i, 0)))
    return pl.pallas_call(
        hand_over_kernel,
        grid=(steps,),
        out_shape=tuple(jax.ShapeDtypeStruct(a.shape, a.dtype) for a in arrays),
        in_specs=specs,
        out_specs=tuple(specs),
        compiler_params=pltpu.CompilerParams(vmem_limit_bytes=60 << 20),
        name="hand_over",
    )(*arrays)


def shards(q_nope, q_rope, grad_out, log_total, kv_latent, up_weight, selected, offered):
    out_n, out_r, out_l, out_w = hand_over(*fused_call(
        selected[0], offered[0].T, q_nope[0], q_rope[0], grad_out[0], log_total[0], kv_latent[0].T,
        up_weight))
    return (out_n[None], out_r[None], out_l.T[None], out_w)


def solution(mesh):
    in_specs = (
        P("dp", "ctx", None),
        P("dp", "ctx", None),
        P("dp", "ctx", None),
        P("dp", None, "ctx"),
        P("dp", "ctx", None),
        P("ctx", None),
        P("dp", "ctx", None),
        P("dp", None, None),
    )
    out_specs = (P("dp", "ctx", None), P("dp", "ctx", None), P("dp", "ctx", None), P("ctx", None))
    return jax.shard_map(shards, mesh=mesh, in_specs=in_specs, out_specs=out_specs, check_vma=False)
```

```python
import functools

import jax
import jax.numpy as jnp
from jax import lax
from jax.experimental import pallas as pl
from jax.experimental.pallas import tpu as pltpu
from jax.sharding import PartitionSpec as P

LAT = 256
ROPE = 64
NOPE = 128
VDIM = 128
BLOCK = 64
HEADS = 64
HALF_HEADS = 32
CAND = 384
TOK = 128
HALF = 8192
SLAB = 1024

offsets = (1, 2, 3, 4)
MESH = pl.DeviceIdType.MESH
NT = (((1,), (1,)), ((), ()))
VMEM = pl.BlockSpec(memory_space=pltpu.VMEM)
ANY = pl.BlockSpec(memory_space=pl.ANY)


class Place:
    def __init__(self):
        self.dp = lax.axis_index("dp")
        self.ctx = lax.axis_index("ctx")
        self.xh = self.dp // 4
        self.y = self.dp % 4
        self.core = self.ctx % 2
        self.chip = self.ctx // 2
        self.xl = self.chip % 2
        self.z = self.chip // 2

    def sibling(self):
        return (self.dp, self.ctx + 1 - 2 * self.core)

    def in_ctx(self, chip, core):
        return (self.dp, chip * 2 + core)

    def side(self):
        return (self.dp, self.ctx + 2 - 4 * self.xl)

    def along_z(self, step):
        return (self.dp, (self.ctx + 4 * step) % 32)

    def cross(self):
        return ((1 - self.xh) * 4 + self.y, self.ctx + 2 - 4 * self.xl)

    def ring(self, step):
        return (self.xh * 4 + (self.y + step) % 4, self.ctx)


def rdma(src, dst, send, recv, device):
    return pltpu.make_async_remote_copy(
        src_ref=src, dst_ref=dst, send_sem=send, recv_sem=recv, device_id=device,
        device_id_type=MESH,
    )


def signal_peers(devices):
    barrier = pltpu.get_barrier_semaphore()
    for device in devices:
        pl.semaphore_signal(barrier, inc=1, device_id=device, device_id_type=MESH)
    return barrier


def dg(a, b, dims):
    return lax.dot_general(a, b, dims, preferred_element_type=jnp.float32)


def mm(a, b):
    return jnp.dot(a, b, preferred_element_type=jnp.float32)


SCALE = 1.0 / float(NOPE + ROPE) ** 0.5


PLAN = (
    ("along_y", 0), ("unit", 0, 0, 0), ("cross", 0, 0), ("cross", 0, 3), ("up", 0),
    ("cross", 0, 1), ("relay", 0, 0), ("down", 0), ("unit", 0, 0, 3), ("along_z", 1, 2),
    ("relay", 0, 3), ("cross", 0, 2), ("unit", 0, 0, 2), ("relay", 0, 1), ("unit", 0, 1, 0),
    ("along_z", 1, 3), ("relay", 0, 2), ("unit", 0, 1, 3), ("add_x", 0, 3), ("unit", 0, 1, 1),
    ("unit", 0, 1, 2), ("add_x", 0, 2), ("along_z", 1, 4), ("add_x", 0, 1), ("add_cross", 0, 3),
    ("add_x", 0, 0), ("unit", 0, 0, 1), ("add_cross", 0, 2), ("unit", 1, 1, 2), ("unit", 1, 1, 3),
    ("add_x", 1, 2), ("add_cross", 0, 1), ("add_x", 1, 3), ("add_y2", 0), ("unit", 1, 1, 1),
    ("add_cross", 0, 0), ("unit", 1, 1, 0), ("add_x", 1, 1), ("add_cross", 1, 2),
    ("add_y1", 0, 0), ("add_y1", 0, 1), ("unit", 1, 0, 3), ("add_cross", 1, 3), ("unit", 1, 0, 2),
    ("add_x", 1, 0), ("add_cross", 1, 1), ("add_y2", 1), ("unit", 1, 0, 1), ("add_z", 0),
    ("add_cross", 1, 0), ("add_y1", 1, 0), ("add_y1", 1, 1), ("unit", 1, 0, 0), ("add_z", 1),
    ("add_side", 0), ("finish", 0), ("add_side", 1), ("finish", 1),
)
UNITS = [op[1:] for op in PLAN if op[0] == "unit"]
SLOT = {u: i for i, u in enumerate(UNITS)}
WIDE = SLAB // 2
LONG = HALF // 2


class Sems:
    def __init__(self):
        self.at = {}
        self.count = 0

    def __call__(self, name, size=1):
        if name not in self.at:
            self.at[name] = self.count
            self.count += size
        return self.at[name]


NSEM = 256


def fused_kernel(
    selected, offered, qn, qr, go, lt, own_t, upw,
    out_n, out_r, out_l, out_w,
    own, box, qn2, qr2, go2, lt2, c, bias2, w, in_slab, in_long, stage,
    gqn, gqr, cg, cgl, got, own2, rope_a, rope_b, ct, lat, rope_acc,
    acc, xsend, xrecv, csend, crecv, y2s, y2r, y1s, y1r, zbuf, part, side_in, low, low_in, fin,
    ss, rs, ls,
):
    bf, f32 = jnp.bfloat16, jnp.float32
    me = Place()
    core, chip = me.core, me.chip
    sib = me.sibling()
    chip_at = [(chip + o) % 16 for o in range(16)]
    y_at = [(me.y + o) % 4 for o in range(4)]
    z_at = [(me.z + o) % 8 for o in range(8)]
    peers = [(me.dp, (me.ctx + o) % 32) for o in (1, 2, 3, 4, 28, 29, 30, 31)]
    peers += [me.in_ctx(chip_at[o], core) for o in range(3, 14)]
    peers += [((me.dp + o) % 8, chip * 2 + k) for o in range(1, 8) for k in range(2)]
    peers += [me.cross()]
    barrier = signal_peers(peers)

    sem = Sems()
    sends = []
    local = []
    seen = set()

    def send(src, dst, name, device):
        at = sem(name)
        rdma(src(), dst(), ss.at[at], rs.at[at], device).start()
        sends.append((src, at))

    def got_it(ref, name):
        if name not in seen:
            seen.add(name)
            at = sem(name)
            rdma(ref, ref, ss.at[at], rs.at[at], sib).wait_recv()

    def copy(src, dst):
        cp = pltpu.make_async_copy(src, dst, ls.at[len(local)])
        cp.start()
        local.append(cp)

    def rows_at(start, size, unit=8):
        return pl.ds(pl.multiple_of(start, unit), size)

    def col(k, width):
        return pl.ds(pl.multiple_of(k * width, width), width)

    def cols_of(f, side, step):
        xh = me.xh if side == 0 else 1 - me.xh
        return col(f * 8 + xh * 4 + y_at[step], WIDE)

    def rows_of(k):
        return rows_at(k * TOK, TOK, TOK)

    def crows_of(k, size):
        return rows_at(k * CAND, size, TOK)

    qrow, crow = rows_of(core), crows_of(core, TOK)
    pairs = [
        (lambda k: qn.at[:, col(k, 4096)], lambda k: qn2.at[rows_of(k), :]),
        (lambda k: qr.at[:, col(k, 2048)], lambda k: qr2.at[rows_of(k), :]),
        (lambda k: go.at[:, col(k, 4096)], lambda k: go2.at[rows_of(k), :]),
        (lambda k: lt.at[col(k, 32), :], lambda k: lt2.at[k]),
    ]
    for src, dst in pairs:
        copy(src(core), dst(core))

    group = me.ctx
    latent = own_t[...].astype(f32).T
    own[...] = latent.astype(bf)
    c[crow, :] = latent.astype(bf)
    offer = [offered[m, group] for m in range(4)]
    for m in range(4):
        box[m] = jnp.where(offer[m] == 0, latent[:BLOCK], latent[BLOCK:]).astype(bf)
    ids = [group * 2, group * 2 + 1]
    for m, o in enumerate(offsets):
        source = group - o
        sender = jnp.maximum(source, 0)
        ids.append(jnp.where(source >= 0, sender * 2 + offered[m, sender], -1))
    lane64 = lax.broadcasted_iota(jnp.int32, (BLOCK, TOK), 1)
    inner = lax.broadcasted_iota(jnp.int32, (BLOCK, TOK), 0)
    for k in range(6):
        cols = []
        for q in range(2):
            hit = (selected[q, 0] == ids[k]) | (selected[q, 1] == ids[k]) | (selected[q, 2] == ids[k])
            off = jnp.where(hit & (ids[k] >= 0), 0.0, -1e30).astype(f32)
            if k == q:
                place = lane64 - q * BLOCK
                cols.append(jnp.where(place >= inner, 0.0, jnp.broadcast_to(off, (BLOCK, TOK))))
            else:
                cols.append(jnp.broadcast_to(off, (BLOCK, TOK)))
        bias2[rows_at(core * CAND + k * BLOCK, BLOCK, 64), :] = jnp.where(
            lane64 < BLOCK, cols[0], cols[1]).astype(bf)
    pl.semaphore_wait(barrier, len(peers))

    near = [sib, me.side(), (me.dp, me.ctx + 2 - 4 * me.xl + 1 - 2 * core)]
    near_core = [1 - core, core, 1 - core]
    near_at = [me.xl * 2 + 1 - core, (1 - me.xl) * 2 + core, (1 - me.xl) * 2 + 1 - core]

    def slab_in(k):
        return upw.at[:, col(k * 16 + me.dp, WIDE)]

    def long_in(k):
        return upw.at[:, col(k * 2 + 1, LONG)]

    for i in range(3):
        send(lambda i=i: slab_in(near_core[i]), lambda i=i: in_slab.at[i], ("slab", i), near[i])
    for i in range(3):
        send(lambda i=i: long_in(near_core[i]), lambda i=i: in_long.at[i], ("long", i), near[i])

    for m, o in enumerate(offsets):
        to = (me.ctx + o) % 32
        place = rows_at((to % 2) * CAND + TOK + m * BLOCK, BLOCK, 64)
        send(lambda m=m: box.at[m], lambda place=place: c.at[place, :], ("offer", m), (me.dp, to))
    shared = [(lambda k: own, lambda k: c.at[crows_of(k, TOK), :]),
              (lambda k: bias2.at[crows_of(1 - k, CAND), :], lambda k: bias2.at[crows_of(k, CAND), :])]
    for i, (src, dst) in enumerate(pairs + shared):
        send(lambda src=src: src(1 - core), lambda dst=dst: dst(core), ("sib", i), sib)

    def offered_rows(k):
        return c.at[rows_at(k * CAND + TOK, 4 * BLOCK, TOK), :]

    my_rows = rows_at(me.z * 32, 32, 32)
    zrows = lambda o: rows_at(z_at[o % 8] * 32, 32, 32)
    at_z = lambda o: (me.dp, (z_at[o % 8] * 2 + me.xl) * 2 + core)

    def assemble(arrived, mine, width, name):
        stage[rows_at((me.xl * 2 + core) * 8, 8), 0:width] = mine.astype(f32)
        for i in range(3):
            got_it(arrived.at[i], (name, i))
            stage[rows_at(near_at[i] * 8, 8), 0:width] = arrived[i].astype(f32)
        return stage[:, 0:width].astype(bf)

    w[my_rows, cols_of(0, 0, 0)] = assemble(
        in_slab, upw[:, col(core * 16 + me.dp, WIDE)], WIDE, "slab")
    for o in range(1, 8):
        ref = lambda: w.at[my_rows, cols_of(0, 0, 0)]
        send(ref, ref, ("z", o), at_z(o))
    w[my_rows, LONG:] = assemble(in_long, upw[:, col(core * 2 + 1, LONG)], LONG, "long")

    lo, hi, whole = pl.ds(0, 128), pl.ds(128, 128), pl.ds(0, 256)
    sent_half = rows_at(me.xl * 128, 128, 128)
    got_half = rows_at((1 - me.xl) * 128, 128, 128)
    full_long = pl.ds(LONG, LONG)
    quarters = [pl.ds(LONG, LONG // 2), pl.ds(LONG + LONG // 2, LONG // 2)]

    def ring_ref(n, way):
        rows = zrows(8 - (n - 1) if way == 0 else n - 1)
        return w.at[rows, full_long if n < 4 else quarters[way]]

    def ring_in(n, way):
        rows = zrows(8 - n if way == 0 else n)
        return w.at[rows, full_long if n < 4 else quarters[way]]

    def along_z(f, n):
        for way in range(2):
            if n > 1:
                got_it(ring_in(n - 1, way), ("ring", n - 1, way))
            ref = lambda way=way: ring_ref(n, way)
            send(ref, ref, ("ring", n, way), at_z(1 if way == 0 else 7))

    along_z(1, 1)
    for m in range(4):
        got_it(c.at[rows_at(core * CAND + TOK + m * BLOCK, BLOCK, 64), :], ("offer", m))
    send(lambda: offered_rows(core), lambda: offered_rows(core), "offer_on", sib)

    def weight_part(rows, side, step, name):
        got_it(w.at[rows, cols_of(0, side, step)], name)

    def need_block(f, side, step):
        if f == 1:
            for n in range(1, 5):
                for way in range(2):
                    got_it(ring_in(n, way), ("ring", n, way))
        elif side == 1:
            weight_part(got_half, 1, step, ("cross", step))
            weight_part(sent_half, 1, step, ("side", step))
        elif step == 0:
            for o in range(1, 8):
                got_it(w.at[zrows(8 - o), cols_of(0, 0, 0)], ("z", o))
        elif step == 2:
            weight_part(lo, 0, 2, "up2")
            weight_part(hi, 0, 2, "down2")
        else:
            weight_part(whole, 0, step, "up" if step == 3 else "down")

    def pass_on(rows, side, step, name, device):
        ref = lambda: w.at[rows, cols_of(0, side, step)]
        send(ref, ref, name, device)

    def along_y(f):
        need_block(0, 0, 0)
        pass_on(whole, 0, 0, "up", me.ring(1))
        pass_on(whole, 0, 0, "down", me.ring(3))

    def cross(f, step):
        need_block(0, 0, step)
        pass_on(sent_half, 0, step, ("cross", step), me.cross())

    def up(f):
        need_block(0, 0, 3)
        pass_on(lo, 0, 3, "up2", me.ring(1))

    def down(f):
        need_block(0, 0, 1)
        pass_on(hi, 0, 1, "down2", me.ring(3))

    def relay(f, step):
        weight_part(got_half, 1, step, ("cross", step))
        pass_on(got_half, 1, step, ("side", step), me.side())

    def add_x(f, step):
        at = f * 4 + step
        xsend[at] = acc[SLOT[f, 1, step], sent_half, :].astype(bf)
        send(lambda: xsend.at[at], lambda: xrecv.at[at], ("rx", at), me.side())

    def add_cross(f, step):
        at = f * 4 + step
        got_it(xrecv.at[at], ("rx", at))
        csend[at] = (acc[SLOT[f, 1, step], got_half, :] + xrecv[at].astype(f32)).astype(bf)
        send(lambda: csend.at[at], lambda: crecv.at[at], ("rc", at), me.cross())

    def crossed(f, step):
        at = f * 4 + step
        got_it(crecv.at[at], ("rc", at))
        acc[SLOT[f, 0, step], sent_half, :] += crecv[at].astype(f32)

    def add_y2(f):
        crossed(f, 2)
        for i, step in enumerate((1, 3)):
            at = f * 2 + i
            y2s[at] = acc[SLOT[f, 0, 2], i * 128:(i + 1) * 128, :].astype(bf)
            send(lambda at=at: y2s.at[at], lambda at=at: y2r.at[at], ("ry2", at), me.ring(step))

    def add_y1(f, i):
        step = (1, 3)[i]
        crossed(f, step)
        at = f * 2 + i
        got_it(y2r.at[at], ("ry2", at))
        slot = SLOT[f, 0, step]
        near_half, far = slice(i * 128, (i + 1) * 128), slice((1 - i) * 128, (2 - i) * 128)
        y1s[at, near_half, :] = (acc[slot, near_half, :] + y2r[at].astype(f32)).astype(bf)
        y1s[at, far, :] = acc[slot, far, :].astype(bf)
        send(lambda: y1s.at[at], lambda: y1r.at[at], ("ry1", at), me.ring(step))

    def add_z(f):
        slot = SLOT[f, 0, 0]
        crossed(f, 0)
        for i in range(2):
            got_it(y1r.at[f * 2 + i], ("ry1", f * 2 + i))
        acc[slot] = acc[slot] + (y1r[f * 2].astype(f32) + y1r[f * 2 + 1].astype(f32))
        if f == 1:
            low[...] = acc[slot].astype(bf)
            for o in range(1, 16):
                send(lambda o=o: low.at[rows_at(chip_at[o] * 16, 16, 16), :], lambda o=o: low_in.at[o],
                     ("rz", f, o), me.in_ctx(chip_at[o], core))
            return
        for o in range(1, 8):
            send(lambda o=o: acc.at[slot, zrows(o), :], lambda o=o: zbuf.at[o], ("rz", f, o), at_z(o))

    def add_side(f):
        if f == 1:
            total = acc[SLOT[f, 0, 0], rows_at(chip * 16, 16, 16), :]
            for o in range(1, 16):
                got_it(low_in.at[o], ("rz", f, o))
                total = total + low_in[o].astype(f32)
            fin[f] = total
            return
        total = acc[SLOT[f, 0, 0], my_rows, :]
        for o in range(1, 8):
            got_it(zbuf.at[o], ("rz", f, o))
            total = total + zbuf[o]
        part[...] = total
        send(lambda: part.at[rows_at((1 - me.xl) * 16, 16, 16), :], lambda: side_in, "pair", me.side())

    def finish(f):
        if f == 0:
            got_it(side_in, "pair")
            fin[f] = part[rows_at(me.xl * 16, 16, 16), :] + side_in[...]
        for o in range(8):
            for k in range(2):
                if o == 0 and k == 0:
                    continue
                to = core if k == 0 else 1 - core
                send(lambda to=to: fin.at[f, rows_at(to * 8, 8), :], lambda: out_cols(f, core, me.dp),
                     ("w", f, o, k), ((me.dp + o) % 8, chip * 2 + to))

    def out_cols(f, k, r):
        return out_w.at[:, col(k * 16 + f * 8 + r, WIDE)]

    actions = dict(
        along_y=along_y, along_z=along_z, cross=cross, up=up, down=down, relay=relay, add_x=add_x,
        add_cross=add_cross, add_y2=add_y2, add_y1=add_y1, add_z=add_z, add_side=add_side,
        finish=finish, unit=need_block)
    before, events = [], []
    for op in PLAN:
        events.append(op)
        if op[0] == "unit":
            before.append(events)
            events = []
    after = events

    def act(ops):
        for name, *where in ops:
            actions[name](*where)

    for cp in local:
        cp.wait()
    for i, (_, dst) in enumerate(pairs + shared):
        got_it(dst(1 - core), ("sib", i))
    got_it(offered_rows(1 - core), "offer_on")
    zero = jnp.zeros((2 * CAND, ROPE), bf)
    rp = c[:, LAT:]
    rope_a[...] = jnp.concatenate([rp, zero], axis=1)
    rope_b[...] = jnp.concatenate([zero, rp], axis=1)
    ct[...] = c[:, :LAT].T
    lat[...] = jnp.zeros_like(lat)
    rope_acc[...] = jnp.zeros_like(rope_acc)
    lane = lax.broadcasted_iota(jnp.int32, (CAND, 128), 1)
    z128 = jnp.zeros((TOK, 128), bf)

    @pl.loop(0, 16)
    def _(s):
        for k, ops in enumerate(before):
            @pl.when(s == k)
            def _(ops=ops):
                act(ops)
        half, side, step = [
            sum((s == k).astype(jnp.int32) * u[i] for k, u in enumerate(UNITS) if u[i])
            for i in range(3)]
        xh = me.xh + side - 2 * me.xh * side
        p = half * 8 + xh * 4 + (me.y + step) % 4

        rcol = col(p, 128)
        pair = col(p, 512)
        hcol = [col(p * 2 + e, 128) for e in range(2)]
        keys = [slice(g * CAND, (g + 1) * CAND) for g in range(2)]
        qs = [slice(g * TOK, (g + 1) * TOK) for g in range(2)]
        expanded = mm(c[:, :LAT], w[:, pair]).astype(bf)
        kvs = [expanded[:, :256], expanded[:, 256:]]

        def kcat(g, e):
            rope = rope_a if e == 0 else rope_b
            return jnp.concatenate([kvs[e][keys[g], :128], rope[keys[g], :]], axis=1)

        def qcat(g, e):
            return jnp.concatenate([qn2[qs[g], hcol[e]], qr2[qs[g], rcol]], axis=1)

        both = []
        for g in range(2):
            gos = [go2[qs[g], hcol[e]] for e in range(2)]
            both.append(jnp.concatenate(
                [jnp.concatenate([gos[0], z128], axis=1),
                 jnp.concatenate([z128, gos[1]], axis=1)], axis=0))
        sg, low_p = {}, {}
        for g in range(2):
            vals = jnp.concatenate([kvs[0][keys[g], 128:], kvs[1][keys[g], 128:]], axis=1)
            dp_t = dg(vals, both[g], NT)
            scores = [dg(kcat(g, e), qcat(g, e), NT) for e in range(2)]
            for e in range(2):
                shift = bias2[keys[g], :].astype(f32) - lt2[g, pl.ds(p * 2 + e, 1), :]
                p_t = jnp.exp(scores[e] * SCALE + shift)
                d = dp_t[:, e * 128:(e + 1) * 128]
                rd = jnp.sum(p_t * d, axis=0, keepdims=True)
                sg[g, e] = (p_t * (d - rd)).astype(bf)
                low_p[g, e] = p_t.astype(bf)
        kgs = [[None, None], [None, None]]
        for g in range(2):
            vg = mm(jnp.concatenate([low_p[g, 0], low_p[g, 1]], axis=1), both[g]).astype(bf)
            rk = []
            for e in range(2):
                kg = mm(sg[g, e], qcat(g, e)) * SCALE
                rk.append(kg[:, 128:])
                kgs[e][g] = jnp.concatenate(
                    [kg[:, :128].astype(bf), vg[:, e * 128:(e + 1) * 128]], axis=1)
            rope_acc[keys[g], :] += jnp.where(lane < ROPE, rk[0], rk[1])
            turned = jnp.concatenate([sg[g, 0], sg[g, 1]], axis=1).T
            gr = None
            for e in range(2):
                gq = mm(turned[e * 128:(e + 1) * 128], kcat(g, e)) * SCALE
                gqn[qs[g], hcol[e]] = gq[:, :128].astype(bf)
                gr = gq[:, 128:] if gr is None else gr + gq[:, 128:]
            gqr[qs[g], rcol] = gr.astype(bf)
        kga = jnp.concatenate([jnp.concatenate(kgs[e], axis=0) for e in range(2)], axis=1)
        acc[s] = mm(ct[...], kga)
        for g in range(2):
            lat[keys[g], :] += dg(kga[keys[g]], w[:, pair], NT)

    last = after.index(("add_z", 1)) + 1
    act(after[:last])
    late = [op for op in after[last:] if op[1] == 1]
    ra = rope_acc[...]
    cg[...] = jnp.concatenate([lat[...], ra[:, :ROPE] + ra[:, ROPE:]], axis=1)
    send(lambda: cg.at[crows_of(1 - core, CAND), :], lambda: own2, "back_o", sib)
    act(op for op in after[last:] if op[1] == 0)

    got_it(own2, "back_o")
    mine = cg[crows_of(core, CAND), :] + own2[...]
    for m, o in enumerate(offsets):
        cgl[m] = mine[TOK + m * BLOCK:TOK + (m + 1) * BLOCK].astype(bf)
        send(lambda m=m: cgl.at[m], lambda m=m: got.at[m], ("back", m), (me.dp, (me.ctx + 32 - o) % 32))

    ncol = lambda k: out_n.at[:, col(k, 4096)]
    rcol_ = lambda k: out_r.at[:, col(k, 2048)]
    send(lambda: gqn.at[rows_of(1 - core), :], lambda: ncol(core), "back_n", sib)
    send(lambda: gqr.at[rows_of(1 - core), :], lambda: rcol_(core), "back_r", sib)
    first_late = len(local)
    copy(gqn.at[qrow, :], ncol(core))
    copy(gqr.at[qrow, :], rcol_(core))

    act(late)

    first, second = mine[:BLOCK], mine[BLOCK:TOK]
    for m in range(4):
        got_it(got.at[m], ("back", m))
        rows = got[m].astype(f32)
        nil = jnp.zeros_like(rows)
        first = first + jnp.where(offer[m] == 0, rows, nil)
        second = second + jnp.where(offer[m] == 0, nil, rows)
    out_l[...] = jnp.concatenate([first, second], axis=0).T
    for f in range(2):
        copy(fin.at[f, rows_at(core * 8, 8), :], out_cols(f, core, me.dp))
    got_it(ncol(1 - core), "back_n")
    got_it(rcol_(1 - core), "back_r")
    for f in range(2):
        for o in range(8):
            for k in range(2):
                if o == 0 and k == 0:
                    continue
                who = core if k == 0 else 1 - core
                got_it(out_cols(f, who, (me.dp + 8 - o) % 8), ("w", f, o, k))
    for cp in local[first_late:]:
        cp.wait()
    for src, at in sends:
        rdma(src(), src(), ss.at[at], rs.at[at], sib).wait_send()
    assert sem.count <= NSEM, sem.count


def fused_call(selected, offered, qn, qr, go, lt, own_t, upw):
    bf, f32 = jnp.bfloat16, jnp.float32
    dma = pltpu.SemaphoreType.DMA
    v = pltpu.VMEM
    smem = pl.BlockSpec(memory_space=pltpu.SMEM)
    return pl.pallas_call(
        fused_kernel,
        out_shape=(
            jax.ShapeDtypeStruct((TOK, HEADS * NOPE), bf),
            jax.ShapeDtypeStruct((TOK, HEADS * ROPE), bf),
            jax.ShapeDtypeStruct((LAT + ROPE, TOK), f32),
            jax.ShapeDtypeStruct((8, 2 * HALF), f32),
        ),
        in_specs=[smem, smem] + [ANY] * 4 + [VMEM, VMEM],
        out_specs=(ANY, ANY, VMEM, ANY),
        scratch_shapes=[
            v((TOK, LAT + ROPE), bf), v((4, BLOCK, LAT + ROPE), bf),
            v((2 * TOK, 4096), bf), v((2 * TOK, 2048), bf), v((2 * TOK, 4096), bf),
            v((2, HALF_HEADS, TOK), f32), v((2 * CAND, LAT + ROPE), bf), v((2 * CAND, TOK), bf),
            v((LAT, HALF), bf), v((3, 8, WIDE), bf), v((3, 8, LONG), bf), v((32, LONG), f32),
            v((2 * TOK, 4096), bf), v((2 * TOK, 2048), bf),
            v((2 * CAND, LAT + ROPE), f32), v((4, BLOCK, LAT + ROPE), bf),
            v((4, BLOCK, LAT + ROPE), bf), v((CAND, LAT + ROPE), f32),
            v((2 * CAND, 128), bf), v((2 * CAND, 128), bf), v((LAT, 2 * CAND), bf),
            v((2 * CAND, LAT), f32), v((2 * CAND, 128), f32),
            v((16, LAT, WIDE), f32),
            v((8, 128, WIDE), bf), v((8, 128, WIDE), bf), v((8, 128, WIDE), bf),
            v((8, 128, WIDE), bf),
            v((4, 128, WIDE), bf), v((4, 128, WIDE), bf),
            v((4, 256, WIDE), bf), v((4, 256, WIDE), bf),
            v((8, 32, WIDE), f32), v((32, WIDE), f32), v((16, WIDE), f32),
            v((LAT, WIDE), bf), v((16, 16, WIDE), bf), v((2, 16, WIDE), f32),
            dma((NSEM,)), dma((NSEM,)), dma((16,)),
        ],
        compiler_params=pltpu.CompilerParams(
            collective_id=0, has_side_effects=True, vmem_limit_bytes=56 << 20),
        name="fused_backward",
    )(selected, offered, qn, qr, go, lt, own_t, upw)


def hand_over_kernel(*refs):
    count = (len(refs) - 2) // 3
    sources, results, held = refs[:count], refs[count:2 * count], refs[2 * count:3 * count]
    sem_in, sem_out = refs[3 * count:]
    parts = []
    for src, dst, buf in zip(sources, results, held):
        pieces = src.shape[0] // 32 if src.shape[0] == TOK else 1
        size = src.shape[0] // pieces
        for i in range(pieces):
            rows = pl.ds(i * size, size)
            at = len(parts)
            parts.append((
                pltpu.make_async_copy(src.at[rows, :], buf.at[rows, :], sem_in.at[at]),
                pltpu.make_async_copy(buf.at[rows, :], dst.at[rows, :], sem_out.at[at])))
    for into, _ in parts:
        into.start()
    for into, out in parts:
        into.wait()
        out.start()
    for _, out in parts:
        out.wait()


def hand_over(*arrays):
    dma = pltpu.SemaphoreType.DMA
    return pl.pallas_call(
        hand_over_kernel,
        out_shape=tuple(jax.ShapeDtypeStruct(a.shape, a.dtype) for a in arrays),
        in_specs=[ANY] * len(arrays),
        out_specs=(ANY,) * len(arrays),
        scratch_shapes=[pltpu.VMEM(a.shape, a.dtype) for a in arrays] + [dma((16,)), dma((16,))],
        compiler_params=pltpu.CompilerParams(vmem_limit_bytes=60 << 20),
        name="hand_over",
    )(*arrays)


def shards(q_nope, q_rope, grad_out, log_total, kv_latent, up_weight, selected, offered):
    out_n, out_r, out_l, out_w = hand_over(*fused_call(
        selected[0], offered[0].T, q_nope[0], q_rope[0], grad_out[0], log_total[0], kv_latent[0].T,
        up_weight))
    return (out_n[None], out_r[None], out_l.T[None], out_w)


def solution(mesh):
    in_specs = (
        P("dp", "ctx", None),
        P("dp", "ctx", None),
        P("dp", "ctx", None),
        P("dp", None, "ctx"),
        P("dp", "ctx", None),
        P("ctx", None),
        P("dp", "ctx", None),
        P("dp", None, None),
    )
    out_specs = (P("dp", "ctx", None), P("dp", "ctx", None), P("dp", "ctx", None), P("ctx", None))
    return jax.shard_map(shards, mesh=mesh, in_specs=in_specs, out_specs=out_specs, check_vma=False)
```

```python
import functools

import jax
import jax.numpy as jnp
from jax import lax
from jax.experimental import pallas as pl
from jax.experimental.pallas import tpu as pltpu
from jax.sharding import PartitionSpec as P

LAT = 256
ROPE = 64
NOPE = 128
VDIM = 128
BLOCK = 64
HEADS = 64
HALF_HEADS = 32
CAND = 384
TOK = 128
HALF = 8192
SLAB = 1024

offsets = (1, 2, 3, 4)
MESH = pl.DeviceIdType.MESH
NT = (((1,), (1,)), ((), ()))
VMEM = pl.BlockSpec(memory_space=pltpu.VMEM)
ANY = pl.BlockSpec(memory_space=pl.ANY)


class Place:
    def __init__(self):
        self.dp = lax.axis_index("dp")
        self.ctx = lax.axis_index("ctx")
        self.xh = self.dp // 4
        self.y = self.dp % 4
        self.core = self.ctx % 2
        self.chip = self.ctx // 2
        self.xl = self.chip % 2
        self.z = self.chip // 2

    def sibling(self):
        return (self.dp, self.ctx + 1 - 2 * self.core)

    def in_ctx(self, chip, core):
        return (self.dp, chip * 2 + core)

    def side(self):
        return (self.dp, self.ctx + 2 - 4 * self.xl)

    def along_z(self, step):
        return (self.dp, (self.ctx + 4 * step) % 32)

    def cross(self):
        return ((1 - self.xh) * 4 + self.y, self.ctx + 2 - 4 * self.xl)

    def ring(self, step):
        return (self.xh * 4 + (self.y + step) % 4, self.ctx)


def rdma(src, dst, send, recv, device):
    return pltpu.make_async_remote_copy(
        src_ref=src, dst_ref=dst, send_sem=send, recv_sem=recv, device_id=device,
        device_id_type=MESH,
    )


def signal_peers(devices):
    barrier = pltpu.get_barrier_semaphore()
    for device in devices:
        pl.semaphore_signal(barrier, inc=1, device_id=device, device_id_type=MESH)
    return barrier


def dg(a, b, dims):
    return lax.dot_general(a, b, dims, preferred_element_type=jnp.float32)


def mm(a, b):
    return jnp.dot(a, b, preferred_element_type=jnp.float32)


SCALE = 1.0 / float(NOPE + ROPE) ** 0.5


PLAN = (
    ("along_y", 0), ("cross", 0, 0), ("along_z", 1, 1), ("unit", 0, 0, 0), ("cross", 0, 3),
    ("down", 0), ("cross", 0, 1), ("relay", 0, 0), ("up", 0), ("along_z", 1, 2),
    ("unit", 0, 0, 3), ("relay", 0, 3), ("cross", 0, 2), ("relay", 0, 1), ("unit", 0, 1, 0),
    ("along_z", 1, 3), ("relay", 0, 2), ("unit", 0, 1, 3), ("add_x", 0, 3), ("unit", 0, 0, 1),
    ("unit", 0, 1, 2), ("add_x", 0, 2), ("along_z", 1, 4), ("unit", 0, 1, 1), ("add_x", 0, 1),
    ("add_x", 0, 0), ("add_cross", 0, 3), ("unit", 0, 0, 2), ("add_cross", 0, 2),
    ("unit", 1, 1, 1), ("unit", 1, 1, 2), ("add_cross", 0, 1), ("add_x", 1, 2), ("unit", 1, 0, 1),
    ("add_cross", 0, 0), ("add_x", 1, 1), ("add_y2", 0), ("unit", 1, 1, 3), ("add_y1_far", 0, 0),
    ("add_y1_far", 0, 1), ("add_cross", 1, 2), ("add_x", 1, 3), ("unit", 1, 0, 2),
    ("add_cross", 1, 1), ("add_y1", 0, 1), ("add_y1", 0, 0), ("unit", 1, 1, 0), ("add_x", 1, 0),
    ("add_cross", 1, 3), ("unit", 1, 0, 3), ("add_y2", 1), ("add_y1_far", 1, 0), ("add_z", 0),
    ("add_y1_far", 1, 1), ("add_y1", 1, 0), ("add_cross", 1, 0), ("add_y1", 1, 1),
    ("unit", 1, 0, 0), ("add_z", 1), ("add_side", 0), ("finish", 0), ("add_side", 1),
    ("finish", 1),
)
UNITS = [op[1:] for op in PLAN if op[0] == "unit"]
SLOT = {u: i for i, u in enumerate(UNITS)}
WIDE = SLAB // 2
LONG = HALF // 2


class Sems:
    def __init__(self):
        self.at = {}
        self.count = 0

    def __call__(self, name, size=1):
        if name not in self.at:
            self.at[name] = self.count
            self.count += size
        return self.at[name]


ARRIVALS = 132
SENDS = 48


def fused_kernel(
    selected, offered, qn, qr, go, lt, own_t, upw,
    out_n, out_r, out_l, out_w,
    own, box, qn2, qr2, go2, lt2, c, bias2, w, in_slab, in_long, stage,
    gqn, gqr, cg, cgl, got, own2, rope_a, rope_b, ct, lat, rope_acc,
    acc, xsend, xrecv, csend, crecv, y2s, y2r, y1s, y1r, zbuf, part, side_in, low, low_in, fin,
    ss, rs, ls,
):
    bf, f32 = jnp.bfloat16, jnp.float32
    me = Place()
    core, chip = me.core, me.chip
    sib = me.sibling()
    chip_at = [(chip + o) % 16 for o in range(16)]
    y_at = [(me.y + o) % 4 for o in range(4)]
    z_at = [(me.z + o) % 8 for o in range(8)]
    peers = [(me.dp, (me.ctx + o) % 32) for o in (1, 2, 3, 4, 28, 29, 30, 31)]
    peers += [me.in_ctx(chip_at[o], core) for o in range(3, 14)]
    peers += [((me.dp + o) % 8, chip * 2 + k) for o in range(1, 8) for k in range(2)]
    peers += [me.cross()]
    barrier = signal_peers(peers)

    sem = Sems()
    sends = []
    local = []
    seen = set()

    def send(src, dst, name, device):
        if len(sends) < SENDS:
            at = len(sends)
        else:
            old, at = sends.pop(0)
            rdma(old(), old(), ss.at[at], rs.at[0], sib).wait_send()
        rdma(src(), dst(), ss.at[at], rs.at[sem(name)], device).start()
        sends.append((src, at))

    def got_it(ref, name):
        if name not in seen:
            seen.add(name)
            at = sem(name)
            rdma(ref, ref, ss.at[0], rs.at[at], sib).wait_recv()

    def copy(src, dst):
        cp = pltpu.make_async_copy(src, dst, ls.at[len(local)])
        cp.start()
        local.append(cp)

    def rows_at(start, size, unit=8):
        return pl.ds(pl.multiple_of(start, unit), size)

    def col(k, width):
        return pl.ds(pl.multiple_of(k * width, width), width)

    def cols_of(f, side, step):
        xh = me.xh if side == 0 else 1 - me.xh
        return col(f * 8 + xh * 4 + y_at[step], WIDE)

    def rows_of(k):
        return rows_at(k * TOK, TOK, TOK)

    def crows_of(k, size):
        return rows_at(k * CAND, size, TOK)

    qrow, crow = rows_of(core), crows_of(core, TOK)
    pairs = [
        (lambda k: qn.at[:, col(k, 4096)], lambda k: qn2.at[rows_of(k), :]),
        (lambda k: qr.at[:, col(k, 2048)], lambda k: qr2.at[rows_of(k), :]),
        (lambda k: go.at[:, col(k, 4096)], lambda k: go2.at[rows_of(k), :]),
        (lambda k: lt.at[col(k, 32), :], lambda k: lt2.at[k]),
    ]
    for src, dst in pairs:
        copy(src(core), dst(core))

    group = me.ctx
    latent = own_t[...].astype(f32).T
    own[...] = latent.astype(bf)
    c[crow, :] = latent.astype(bf)
    offer = [offered[m, group] for m in range(4)]
    for m in range(4):
        box[m] = jnp.where(offer[m] == 0, latent[:BLOCK], latent[BLOCK:]).astype(bf)
    ids = [group * 2, group * 2 + 1]
    for m, o in enumerate(offsets):
        source = group - o
        sender = jnp.maximum(source, 0)
        ids.append(jnp.where(source >= 0, sender * 2 + offered[m, sender], -1))
    lane64 = lax.broadcasted_iota(jnp.int32, (BLOCK, TOK), 1)
    inner = lax.broadcasted_iota(jnp.int32, (BLOCK, TOK), 0)
    for k in range(6):
        cols = []
        for q in range(2):
            hit = (selected[q, 0] == ids[k]) | (selected[q, 1] == ids[k]) | (selected[q, 2] == ids[k])
            off = jnp.where(hit & (ids[k] >= 0), 0.0, -1e30).astype(f32)
            if k == q:
                place = lane64 - q * BLOCK
                cols.append(jnp.where(place >= inner, 0.0, jnp.broadcast_to(off, (BLOCK, TOK))))
            else:
                cols.append(jnp.broadcast_to(off, (BLOCK, TOK)))
        bias2[rows_at(core * CAND + k * BLOCK, BLOCK, 64), :] = jnp.where(
            lane64 < BLOCK, cols[0], cols[1]).astype(bf)
    pl.semaphore_wait(barrier, len(peers))

    near = [sib, me.side(), (me.dp, me.ctx + 2 - 4 * me.xl + 1 - 2 * core)]
    near_core = [1 - core, core, 1 - core]
    near_at = [me.xl * 2 + 1 - core, (1 - me.xl) * 2 + core, (1 - me.xl) * 2 + 1 - core]

    def slab_in(k):
        return upw.at[:, col(k * 16 + me.dp, WIDE)]

    def long_in(k):
        return upw.at[:, col(k * 2 + 1, LONG)]

    for i in range(3):
        send(lambda i=i: slab_in(near_core[i]), lambda i=i: in_slab.at[i], ("slab", i), near[i])
    for i in range(3):
        send(lambda i=i: long_in(near_core[i]), lambda i=i: in_long.at[i], ("long", i), near[i])

    for m, o in enumerate(offsets):
        to = (me.ctx + o) % 32
        place = rows_at((to % 2) * CAND + TOK + m * BLOCK, BLOCK, 64)
        send(lambda m=m: box.at[m], lambda place=place: c.at[place, :], ("offer", m), (me.dp, to))
    shared = [(lambda k: own, lambda k: c.at[crows_of(k, TOK), :]),
              (lambda k: bias2.at[crows_of(1 - k, CAND), :], lambda k: bias2.at[crows_of(k, CAND), :])]
    for i, (src, dst) in enumerate(pairs + shared):
        send(lambda src=src: src(1 - core), lambda dst=dst: dst(core), ("sib", i), sib)

    def offered_rows(k):
        return c.at[rows_at(k * CAND + TOK, 4 * BLOCK, TOK), :]

    my_rows = rows_at(me.z * 32, 32, 32)
    zrows = lambda o: rows_at(z_at[o % 8] * 32, 32, 32)
    at_z = lambda o: (me.dp, (z_at[o % 8] * 2 + me.xl) * 2 + core)

    def assemble(arrived, mine, width, name):
        stage[rows_at((me.xl * 2 + core) * 8, 8), 0:width] = mine.astype(f32)
        for i in range(3):
            got_it(arrived.at[i], (name, i))
            stage[rows_at(near_at[i] * 8, 8), 0:width] = arrived[i].astype(f32)
        return stage[:, 0:width].astype(bf)

    w[my_rows, cols_of(0, 0, 0)] = assemble(
        in_slab, upw[:, col(core * 16 + me.dp, WIDE)], WIDE, "slab")
    for o in range(1, 8):
        ref = lambda: w.at[my_rows, cols_of(0, 0, 0)]
        send(ref, ref, ("z", o), at_z(o))
    w[my_rows, LONG:] = assemble(in_long, upw[:, col(core * 2 + 1, LONG)], LONG, "long")

    lo, hi, whole = pl.ds(0, 128), pl.ds(128, 128), pl.ds(0, 256)
    sent_half = rows_at(me.xl * 128, 128, 128)
    got_half = rows_at((1 - me.xl) * 128, 128, 128)
    full_long = pl.ds(LONG, LONG)
    quarters = [pl.ds(LONG, LONG // 2), pl.ds(LONG + LONG // 2, LONG // 2)]

    def ring_ref(n, way):
        rows = zrows(8 - (n - 1) if way == 0 else n - 1)
        return w.at[rows, full_long if n < 4 else quarters[way]]

    def ring_in(n, way):
        rows = zrows(8 - n if way == 0 else n)
        return w.at[rows, full_long if n < 4 else quarters[way]]

    def along_z(f, n):
        if n == 1:
            need_block(0, 0, 0)
        for way in range(2):
            if n > 1:
                got_it(ring_in(n - 1, way), ("ring", n - 1, way))
            ref = lambda way=way: ring_ref(n, way)
            send(ref, ref, ("ring", n, way), at_z(1 if way == 0 else 7))

    for m in range(4):
        got_it(c.at[rows_at(core * CAND + TOK + m * BLOCK, BLOCK, 64), :], ("offer", m))
    send(lambda: offered_rows(core), lambda: offered_rows(core), "offer_on", sib)

    def weight_part(rows, side, step, name):
        got_it(w.at[rows, cols_of(0, side, step)], name)

    def need_block(f, side, step):
        if f == 1:
            for n in range(1, 5):
                for way in range(2):
                    got_it(ring_in(n, way), ("ring", n, way))
        elif side == 1:
            weight_part(got_half, 1, step, ("cross", step))
            weight_part(sent_half, 1, step, ("side", step))
        elif step == 0:
            for o in range(1, 8):
                got_it(w.at[zrows(8 - o), cols_of(0, 0, 0)], ("z", o))
        elif step == 2:
            weight_part(lo, 0, 2, "up2")
            weight_part(hi, 0, 2, "down2")
        else:
            weight_part(whole, 0, step, "up" if step == 3 else "down")

    def pass_on(rows, side, step, name, device):
        ref = lambda: w.at[rows, cols_of(0, side, step)]
        send(ref, ref, name, device)

    def along_y(f):
        need_block(0, 0, 0)
        pass_on(whole, 0, 0, "up", me.ring(1))
        pass_on(whole, 0, 0, "down", me.ring(3))

    def cross(f, step):
        need_block(0, 0, step)
        pass_on(sent_half, 0, step, ("cross", step), me.cross())

    def up(f):
        need_block(0, 0, 3)
        pass_on(lo, 0, 3, "up2", me.ring(1))

    def down(f):
        need_block(0, 0, 1)
        pass_on(hi, 0, 1, "down2", me.ring(3))

    def relay(f, step):
        weight_part(got_half, 1, step, ("cross", step))
        pass_on(got_half, 1, step, ("side", step), me.side())

    def add_x(f, step):
        at = f * 4 + step
        xsend[at] = acc[SLOT[f, 1, step], sent_half, :].astype(bf)
        send(lambda: xsend.at[at], lambda: xrecv.at[at], ("rx", at), me.side())

    def add_cross(f, step):
        at = f * 4 + step
        got_it(xrecv.at[at], ("rx", at))
        csend[at] = (acc[SLOT[f, 1, step], got_half, :] + xrecv[at].astype(f32)).astype(bf)
        send(lambda: csend.at[at], lambda: crecv.at[at], ("rc", at), me.cross())

    def crossed(f, step):
        at = f * 4 + step
        got_it(crecv.at[at], ("rc", at))
        acc[SLOT[f, 0, step], sent_half, :] += crecv[at].astype(f32)

    def add_y2(f):
        crossed(f, 2)
        for i, step in enumerate((1, 3)):
            at = f * 2 + i
            y2s[at] = acc[SLOT[f, 0, 2], i * 128:(i + 1) * 128, :].astype(bf)
            send(lambda at=at: y2s.at[at], lambda at=at: y2r.at[at], ("ry2", at), me.ring(step))

    def add_y1_far(f, i):
        step = (1, 3)[i]
        crossed(f, step)
        at = f * 4 + i * 2
        far = slice((1 - i) * 128, (2 - i) * 128)
        y1s[at] = acc[SLOT[f, 0, step], far, :].astype(bf)
        send(lambda: y1s.at[at], lambda: y1r.at[at], ("ry1", at), me.ring(step))

    def add_y1(f, i):
        step = (1, 3)[i]
        got_it(y2r.at[f * 2 + i], ("ry2", f * 2 + i))
        at = f * 4 + i * 2 + 1
        near_half = slice(i * 128, (i + 1) * 128)
        y1s[at] = (acc[SLOT[f, 0, step], near_half, :] + y2r[f * 2 + i].astype(f32)).astype(bf)
        send(lambda: y1s.at[at], lambda: y1r.at[at], ("ry1", at), me.ring(step))

    def add_z(f):
        slot = SLOT[f, 0, 0]
        crossed(f, 0)
        for at in range(f * 4, f * 4 + 4):
            got_it(y1r.at[at], ("ry1", at))
        for i in range(2):
            rows = slice(i * 128, (i + 1) * 128)
            near_in, far_in = f * 4 + i * 2 + 1, f * 4 + (1 - i) * 2
            acc[slot, rows, :] += y1r[near_in].astype(f32) + y1r[far_in].astype(f32)
        if f == 1:
            low[...] = acc[slot].astype(bf)
            for o in range(1, 16):
                send(lambda o=o: low.at[rows_at(chip_at[o] * 16, 16, 16), :], lambda o=o: low_in.at[o],
                     ("rz", f, o), me.in_ctx(chip_at[o], core))
            return
        for o in range(1, 8):
            send(lambda o=o: acc.at[slot, zrows(o), :], lambda o=o: zbuf.at[o], ("rz", f, o), at_z(o))

    def add_side(f):
        if f == 1:
            total = acc[SLOT[f, 0, 0], rows_at(chip * 16, 16, 16), :]
            for o in range(1, 16):
                got_it(low_in.at[o], ("rz", f, o))
                total = total + low_in[o].astype(f32)
            fin[f] = total
            return
        total = acc[SLOT[f, 0, 0], my_rows, :]
        for o in range(1, 8):
            got_it(zbuf.at[o], ("rz", f, o))
            total = total + zbuf[o]
        part[...] = total
        send(lambda: part.at[rows_at((1 - me.xl) * 16, 16, 16), :], lambda: side_in, "pair", me.side())

    def finish(f):
        if f == 0:
            got_it(side_in, "pair")
            fin[f] = part[rows_at(me.xl * 16, 16, 16), :] + side_in[...]
        for o in range(8):
            for k in range(2):
                if o == 0 and k == 0:
                    continue
                to = core if k == 0 else 1 - core
                send(lambda to=to: fin.at[f, rows_at(to * 8, 8), :], lambda: out_cols(f, core, me.dp),
                     ("w", f, o, k), ((me.dp + o) % 8, chip * 2 + to))

    def out_cols(f, k, r):
        return out_w.at[:, col(k * 16 + f * 8 + r, WIDE)]

    actions = dict(
        along_y=along_y, along_z=along_z, cross=cross, up=up, down=down, relay=relay, add_x=add_x,
        add_cross=add_cross, add_y2=add_y2, add_y1=add_y1,
        add_y1_far=add_y1_far, add_z=add_z, add_side=add_side,
        finish=finish, unit=need_block)
    before, events = [], []
    for op in PLAN:
        events.append(op)
        if op[0] == "unit":
            before.append(events)
            events = []
    after = events

    def act(ops):
        for name, *where in ops:
            actions[name](*where)

    for cp in local:
        cp.wait()
    for i, (_, dst) in enumerate(pairs + shared):
        got_it(dst(1 - core), ("sib", i))
    got_it(offered_rows(1 - core), "offer_on")
    zero = jnp.zeros((2 * CAND, ROPE), bf)
    rp = c[:, LAT:]
    rope_a[...] = jnp.concatenate([rp, zero], axis=1)
    rope_b[...] = jnp.concatenate([zero, rp], axis=1)
    ct[...] = c[:, :LAT].T
    lat[...] = jnp.zeros_like(lat)
    rope_acc[...] = jnp.zeros_like(rope_acc)
    lane = lax.broadcasted_iota(jnp.int32, (CAND, 128), 1)
    z128 = jnp.zeros((TOK, 128), bf)

    @pl.loop(0, 16)
    def _(s):
        for k, ops in enumerate(before):
            @pl.when(s == k)
            def _(ops=ops):
                act(ops)
        half, side, step = [
            sum((s == k).astype(jnp.int32) * u[i] for k, u in enumerate(UNITS) if u[i])
            for i in range(3)]
        xh = me.xh + side - 2 * me.xh * side
        p = half * 8 + xh * 4 + (me.y + step) % 4

        rcol = col(p, 128)
        pair = col(p, 512)
        hcol = [col(p * 2 + e, 128) for e in range(2)]
        keys = [slice(g * CAND, (g + 1) * CAND) for g in range(2)]
        qs = [slice(g * TOK, (g + 1) * TOK) for g in range(2)]
        expanded = mm(c[:, :LAT], w[:, pair]).astype(bf)
        kvs = [expanded[:, :256], expanded[:, 256:]]

        def kcat(g, e):
            rope = rope_a if e == 0 else rope_b
            return jnp.concatenate([kvs[e][keys[g], :128], rope[keys[g], :]], axis=1)

        def qcat(g, e):
            return jnp.concatenate([qn2[qs[g], hcol[e]], qr2[qs[g], rcol]], axis=1)

        both = []
        for g in range(2):
            gos = [go2[qs[g], hcol[e]] for e in range(2)]
            both.append(jnp.concatenate(
                [jnp.concatenate([gos[0], z128], axis=1),
                 jnp.concatenate([z128, gos[1]], axis=1)], axis=0))
        sg, low_p = {}, {}
        for g in range(2):
            vals = jnp.concatenate([kvs[0][keys[g], 128:], kvs[1][keys[g], 128:]], axis=1)
            dp_t = dg(vals, both[g], NT)
            scores = [dg(kcat(g, e), qcat(g, e), NT) for e in range(2)]
            for e in range(2):
                shift = bias2[keys[g], :].astype(f32) - lt2[g, pl.ds(p * 2 + e, 1), :]
                p_t = jnp.exp(scores[e] * SCALE + shift)
                d = dp_t[:, e * 128:(e + 1) * 128]
                rd = jnp.sum(p_t * d, axis=0, keepdims=True)
                sg[g, e] = (p_t * (d - rd)).astype(bf)
                low_p[g, e] = p_t.astype(bf)
        kgs = [[None, None], [None, None]]
        for g in range(2):
            vg = mm(jnp.concatenate([low_p[g, 0], low_p[g, 1]], axis=1), both[g]).astype(bf)
            rk = []
            for e in range(2):
                kg = mm(sg[g, e], qcat(g, e)) * SCALE
                rk.append(kg[:, 128:])
                kgs[e][g] = jnp.concatenate(
                    [kg[:, :128].astype(bf), vg[:, e * 128:(e + 1) * 128]], axis=1)
            rope_acc[keys[g], :] += jnp.where(lane < ROPE, rk[0], rk[1])
            turned = jnp.concatenate([sg[g, 0], sg[g, 1]], axis=1).T
            gr = None
            for e in range(2):
                gq = mm(turned[e * 128:(e + 1) * 128], kcat(g, e)) * SCALE
                gqn[qs[g], hcol[e]] = gq[:, :128].astype(bf)
                gr = gq[:, 128:] if gr is None else gr + gq[:, 128:]
            gqr[qs[g], rcol] = gr.astype(bf)
        kga = jnp.concatenate([jnp.concatenate(kgs[e], axis=0) for e in range(2)], axis=1)
        acc[s] = mm(ct[...], kga)
        for g in range(2):
            lat[keys[g], :] += dg(kga[keys[g]], w[:, pair], NT)

    last = after.index(("add_z", 1)) + 1
    act(after[:last])
    late = [op for op in after[last:] if op[1] == 1]
    ra = rope_acc[...]
    cg[...] = jnp.concatenate([lat[...], ra[:, :ROPE] + ra[:, ROPE:]], axis=1)
    send(lambda: cg.at[crows_of(1 - core, CAND), :], lambda: own2, "back_o", sib)
    act(op for op in after[last:] if op[1] == 0)

    got_it(own2, "back_o")
    mine = cg[crows_of(core, CAND), :] + own2[...]
    for m in range(4):
        cgl[m] = mine[TOK + m * BLOCK:TOK + (m + 1) * BLOCK].astype(bf)

    ncol = lambda k: out_n.at[:, col(k, 4096)]
    rcol_ = lambda k: out_r.at[:, col(k, 2048)]
    send(lambda: gqn.at[rows_of(1 - core), :], lambda: ncol(core), "back_n", sib)
    send(lambda: gqr.at[rows_of(1 - core), :], lambda: rcol_(core), "back_r", sib)
    first_late = len(local)
    copy(gqn.at[qrow, :], ncol(core))
    copy(gqr.at[qrow, :], rcol_(core))

    act(late)
    for m, o in enumerate(offsets):
        send(lambda m=m: cgl.at[m], lambda m=m: got.at[m], ("back", m), (me.dp, (me.ctx + 32 - o) % 32))

    first, second = mine[:BLOCK], mine[BLOCK:TOK]
    for m in range(4):
        got_it(got.at[m], ("back", m))
        rows = got[m].astype(f32)
        nil = jnp.zeros_like(rows)
        first = first + jnp.where(offer[m] == 0, rows, nil)
        second = second + jnp.where(offer[m] == 0, nil, rows)
    out_l[...] = jnp.concatenate([first, second], axis=0).T
    for f in range(2):
        copy(fin.at[f, rows_at(core * 8, 8), :], out_cols(f, core, me.dp))
    got_it(ncol(1 - core), "back_n")
    got_it(rcol_(1 - core), "back_r")
    for f in range(2):
        for o in range(8):
            for k in range(2):
                if o == 0 and k == 0:
                    continue
                who = core if k == 0 else 1 - core
                got_it(out_cols(f, who, (me.dp + 8 - o) % 8), ("w", f, o, k))
    for cp in local[first_late:]:
        cp.wait()
    for src, at in sends:
        rdma(src(), src(), ss.at[at], rs.at[0], sib).wait_send()
    assert sem.count == ARRIVALS, sem.count


def fused_call(selected, offered, qn, qr, go, lt, own_t, upw):
    bf, f32 = jnp.bfloat16, jnp.float32
    dma = pltpu.SemaphoreType.DMA
    v = pltpu.VMEM
    smem = pl.BlockSpec(memory_space=pltpu.SMEM)
    return pl.pallas_call(
        fused_kernel,
        out_shape=(
            jax.ShapeDtypeStruct((TOK, HEADS * NOPE), bf),
            jax.ShapeDtypeStruct((TOK, HEADS * ROPE), bf),
            jax.ShapeDtypeStruct((LAT + ROPE, TOK), f32),
            jax.ShapeDtypeStruct((8, 2 * HALF), f32),
        ),
        in_specs=[smem, smem] + [ANY] * 4 + [VMEM, VMEM],
        out_specs=(ANY, ANY, VMEM, ANY),
        scratch_shapes=[
            v((TOK, LAT + ROPE), bf), v((4, BLOCK, LAT + ROPE), bf),
            v((2 * TOK, 4096), bf), v((2 * TOK, 2048), bf), v((2 * TOK, 4096), bf),
            v((2, HALF_HEADS, TOK), f32), v((2 * CAND, LAT + ROPE), bf), v((2 * CAND, TOK), bf),
            v((LAT, HALF), bf), v((3, 8, WIDE), bf), v((3, 8, LONG), bf), v((32, LONG), f32),
            v((2 * TOK, 4096), bf), v((2 * TOK, 2048), bf),
            v((2 * CAND, LAT + ROPE), f32), v((4, BLOCK, LAT + ROPE), bf),
            v((4, BLOCK, LAT + ROPE), bf), v((CAND, LAT + ROPE), f32),
            v((2 * CAND, 128), bf), v((2 * CAND, 128), bf), v((LAT, 2 * CAND), bf),
            v((2 * CAND, LAT), f32), v((2 * CAND, 128), f32),
            v((16, LAT, WIDE), f32),
            v((8, 128, WIDE), bf), v((8, 128, WIDE), bf), v((8, 128, WIDE), bf),
            v((8, 128, WIDE), bf),
            v((4, 128, WIDE), bf), v((4, 128, WIDE), bf),
            v((8, 128, WIDE), bf), v((8, 128, WIDE), bf),
            v((8, 32, WIDE), f32), v((32, WIDE), f32), v((16, WIDE), f32),
            v((LAT, WIDE), bf), v((16, 16, WIDE), bf), v((2, 16, WIDE), f32),
            dma((SENDS,)), dma((ARRIVALS,)), dma((8,)),
        ],
        compiler_params=pltpu.CompilerParams(
            collective_id=0, has_side_effects=True, vmem_limit_bytes=56 << 20),
        name="fused_backward",
    )(selected, offered, qn, qr, go, lt, own_t, upw)


def hand_over_kernel(*refs):
    count = (len(refs) - 2) // 3
    sources, results, held = refs[:count], refs[count:2 * count], refs[2 * count:3 * count]
    sem_in, sem_out = refs[3 * count:]
    parts = []
    for src, dst, buf in zip(sources, results, held):
        pieces = src.shape[0] // 32 if src.shape[0] == TOK else 1
        size = src.shape[0] // pieces
        for i in range(pieces):
            rows = pl.ds(i * size, size)
            at = len(parts)
            parts.append((
                pltpu.make_async_copy(src.at[rows, :], buf.at[rows, :], sem_in.at[at]),
                pltpu.make_async_copy(buf.at[rows, :], dst.at[rows, :], sem_out.at[at])))
    for into, _ in parts:
        into.start()
    for into, out in parts:
        into.wait()
        out.start()
    for _, out in parts:
        out.wait()


def hand_over(*arrays):
    dma = pltpu.SemaphoreType.DMA
    return pl.pallas_call(
        hand_over_kernel,
        out_shape=tuple(jax.ShapeDtypeStruct(a.shape, a.dtype) for a in arrays),
        in_specs=[ANY] * len(arrays),
        out_specs=(ANY,) * len(arrays),
        scratch_shapes=[pltpu.VMEM(a.shape, a.dtype) for a in arrays] + [dma((10,)), dma((10,))],
        compiler_params=pltpu.CompilerParams(vmem_limit_bytes=60 << 20),
        name="hand_over",
    )(*arrays)


def shards(q_nope, q_rope, grad_out, log_total, kv_latent, up_weight, selected, offered):
    out_n, out_r, out_l, out_w = hand_over(*fused_call(
        selected[0], offered[0].T, q_nope[0], q_rope[0], grad_out[0], log_total[0], kv_latent[0].T,
        up_weight))
    return (out_n[None], out_r[None], out_l.T[None], out_w)


def solution(mesh):
    in_specs = (
        P("dp", "ctx", None),
        P("dp", "ctx", None),
        P("dp", "ctx", None),
        P("dp", None, "ctx"),
        P("dp", "ctx", None),
        P("ctx", None),
        P("dp", "ctx", None),
        P("dp", None, None),
    )
    out_specs = (P("dp", "ctx", None), P("dp", "ctx", None), P("dp", "ctx", None), P("ctx", None))
    return jax.shard_map(shards, mesh=mesh, in_specs=in_specs, out_specs=out_specs, check_vma=False)
```

```python
import functools

import jax
import jax.numpy as jnp
from jax import lax
from jax.experimental import pallas as pl
from jax.experimental.pallas import tpu as pltpu
from jax.sharding import PartitionSpec as P

LAT = 256
ROPE = 64
NOPE = 128
VDIM = 128
BLOCK = 64
HEADS = 64
HALF_HEADS = 32
CAND = 384
TOK = 128
HALF = 8192
SLAB = 1024

offsets = (1, 2, 3, 4)
MESH = pl.DeviceIdType.MESH
NT = (((1,), (1,)), ((), ()))
VMEM = pl.BlockSpec(memory_space=pltpu.VMEM)
ANY = pl.BlockSpec(memory_space=pl.ANY)


class Place:
    def __init__(self):
        self.dp = lax.axis_index("dp")
        self.ctx = lax.axis_index("ctx")
        self.xh = self.dp // 4
        self.y = self.dp % 4
        self.core = self.ctx % 2
        self.chip = self.ctx // 2
        self.xl = self.chip % 2
        self.z = self.chip // 2

    def sibling(self):
        return (self.dp, self.ctx + 1 - 2 * self.core)

    def in_ctx(self, chip, core):
        return (self.dp, chip * 2 + core)

    def side(self):
        return (self.dp, self.ctx + 2 - 4 * self.xl)

    def along_z(self, step):
        return (self.dp, (self.ctx + 4 * step) % 32)

    def cross(self):
        return ((1 - self.xh) * 4 + self.y, self.ctx + 2 - 4 * self.xl)

    def ring(self, step):
        return (self.xh * 4 + (self.y + step) % 4, self.ctx)


def rdma(src, dst, send, recv, device):
    return pltpu.make_async_remote_copy(
        src_ref=src, dst_ref=dst, send_sem=send, recv_sem=recv, device_id=device,
        device_id_type=MESH,
    )


def signal_peers(devices):
    barrier = pltpu.get_barrier_semaphore()
    for device in devices:
        pl.semaphore_signal(barrier, inc=1, device_id=device, device_id_type=MESH)
    return barrier


def dg(a, b, dims):
    return lax.dot_general(a, b, dims, preferred_element_type=jnp.float32)


def mm(a, b):
    return jnp.dot(a, b, preferred_element_type=jnp.float32)


SCALE = 1.0 / float(NOPE + ROPE) ** 0.5


PLAN = (
    ("along_y", 0), ("along_z", 1, 1), ("cross", 0, 0), ("unit", 0, 0, 0), ("down", 0),
    ("cross", 0, 3), ("up", 0), ("along_z", 1, 2), ("cross", 0, 1), ("relay", 0, 0),
    ("unit", 0, 0, 3), ("relay", 0, 3), ("cross", 0, 2), ("unit", 0, 0, 2), ("relay", 0, 1),
    ("along_z", 1, 3), ("unit", 0, 0, 1), ("relay", 0, 2), ("unit", 0, 1, 3), ("unit", 0, 1, 1),
    ("add_x", 0, 3), ("along_z", 1, 4), ("unit", 0, 1, 2), ("add_x", 0, 2), ("unit", 0, 1, 0),
    ("add_cross", 0, 3), ("add_x", 0, 1), ("add_x", 0, 0), ("unit", 1, 1, 2), ("add_x", 1, 2),
    ("add_cross", 0, 2), ("unit", 1, 1, 1), ("add_cross", 0, 1), ("add_x", 1, 1),
    ("unit", 1, 0, 2), ("add_y2", 0), ("add_cross", 0, 0), ("add_y1_far", 0, 1),
    ("unit", 1, 1, 3), ("add_x", 1, 3), ("add_cross", 1, 2), ("add_y1_far", 0, 0),
    ("unit", 1, 1, 0), ("add_y1", 0, 0), ("add_cross", 1, 1), ("add_y1", 0, 1), ("unit", 1, 0, 1),
    ("add_cross", 1, 3), ("add_x", 1, 0), ("unit", 1, 0, 3), ("add_y2", 1), ("add_z", 0),
    ("add_y1_far", 1, 0), ("add_y1_far", 1, 1), ("unit", 1, 0, 0), ("add_cross", 1, 0),
    ("add_y1", 1, 0), ("add_y1", 1, 1), ("add_z", 1), ("add_side", 0), ("finish", 0),
    ("add_side", 1), ("finish", 1),
)
UNITS = [op[1:] for op in PLAN if op[0] == "unit"]
SLOT = {u: i for i, u in enumerate(UNITS)}
WIDE = SLAB // 2
LONG = HALF // 2


class Sems:
    def __init__(self):
        self.at = {}
        self.count = 0

    def __call__(self, name, size=1):
        if name not in self.at:
            self.at[name] = self.count
            self.count += size
        return self.at[name]


ARRIVALS = 132
SENDS = 48


def fused_kernel(
    selected, offered, qn, qr, go, lt, own_t, upw,
    out_n, out_r, out_l, out_w,
    own, box, qn2, qr2, go2, lt2, c, bias2, w, in_slab, in_long, stage,
    gqn, gqr, cg, cgl, got, own2, rope_a, rope_b, ct, lat, rope_acc,
    acc, xsend, xrecv, csend, crecv, y2s, y2r, y1s, y1r, zbuf, part, side_in, low, low_in, fin,
    ss, rs, ls,
):
    bf, f32 = jnp.bfloat16, jnp.float32
    me = Place()
    core, chip = me.core, me.chip
    sib = me.sibling()
    chip_at = [(chip + o) % 16 for o in range(16)]
    y_at = [(me.y + o) % 4 for o in range(4)]
    z_at = [(me.z + o) % 8 for o in range(8)]
    peers = [(me.dp, (me.ctx + o) % 32) for o in (1, 2, 3, 4, 28, 29, 30, 31)]
    peers += [me.in_ctx(chip_at[o], core) for o in range(3, 14)]
    peers += [((me.dp + o) % 8, chip * 2 + k) for o in range(1, 8) for k in range(2)]
    peers += [me.cross()]
    barrier = signal_peers(peers)

    sem = Sems()
    sends = []
    local = []
    seen = set()

    def send(src, dst, name, device):
        if len(sends) < SENDS:
            at = len(sends)
        else:
            old, at = sends.pop(0)
            rdma(old(), old(), ss.at[at], rs.at[0], sib).wait_send()
        rdma(src(), dst(), ss.at[at], rs.at[sem(name)], device).start()
        sends.append((src, at))

    def got_it(ref, name):
        if name not in seen:
            seen.add(name)
            at = sem(name)
            rdma(ref, ref, ss.at[0], rs.at[at], sib).wait_recv()

    def copy(src, dst):
        cp = pltpu.make_async_copy(src, dst, ls.at[len(local)])
        cp.start()
        local.append(cp)

    def rows_at(start, size, unit=8):
        return pl.ds(pl.multiple_of(start, unit), size)

    def col(k, width):
        return pl.ds(pl.multiple_of(k * width, width), width)

    def cols_of(f, side, step):
        xh = me.xh if side == 0 else 1 - me.xh
        return col(f * 8 + xh * 4 + y_at[step], WIDE)

    def rows_of(k):
        return rows_at(k * TOK, TOK, TOK)

    def crows_of(k, size):
        return rows_at(k * CAND, size, TOK)

    qrow, crow = rows_of(core), crows_of(core, TOK)
    pairs = [
        (lambda k: qn.at[:, col(k, 4096)], lambda k: qn2.at[rows_of(k), :]),
        (lambda k: qr.at[:, col(k, 2048)], lambda k: qr2.at[rows_of(k), :]),
        (lambda k: go.at[:, col(k, 4096)], lambda k: go2.at[rows_of(k), :]),
        (lambda k: lt.at[col(k, 32), :], lambda k: lt2.at[k]),
    ]
    for src, dst in pairs:
        copy(src(core), dst(core))

    group = me.ctx
    latent = own_t[...].astype(f32).T
    own[...] = latent.astype(bf)
    c[crow, :] = latent.astype(bf)
    offer = [offered[m, group] for m in range(4)]
    for m in range(4):
        box[m] = jnp.where(offer[m] == 0, latent[:BLOCK], latent[BLOCK:]).astype(bf)
    ids = [group * 2, group * 2 + 1]
    for m, o in enumerate(offsets):
        source = group - o
        sender = jnp.maximum(source, 0)
        ids.append(jnp.where(source >= 0, sender * 2 + offered[m, sender], -1))
    lane64 = lax.broadcasted_iota(jnp.int32, (BLOCK, TOK), 1)
    inner = lax.broadcasted_iota(jnp.int32, (BLOCK, TOK), 0)
    for k in range(6):
        cols = []
        for q in range(2):
            hit = (selected[q, 0] == ids[k]) | (selected[q, 1] == ids[k]) | (selected[q, 2] == ids[k])
            off = jnp.where(hit & (ids[k] >= 0), 0.0, -1e30).astype(f32)
            if k == q:
                place = lane64 - q * BLOCK
                cols.append(jnp.where(place >= inner, 0.0, jnp.broadcast_to(off, (BLOCK, TOK))))
            else:
                cols.append(jnp.broadcast_to(off, (BLOCK, TOK)))
        bias2[rows_at(core * CAND + k * BLOCK, BLOCK, 64), :] = jnp.where(
            lane64 < BLOCK, cols[0], cols[1]).astype(bf)
    pl.semaphore_wait(barrier, len(peers))

    near = [sib, me.side(), (me.dp, me.ctx + 2 - 4 * me.xl + 1 - 2 * core)]
    near_core = [1 - core, core, 1 - core]
    near_at = [me.xl * 2 + 1 - core, (1 - me.xl) * 2 + core, (1 - me.xl) * 2 + 1 - core]

    def slab_in(k):
        return upw.at[:, col(k * 16 + me.dp, WIDE)]

    def long_in(k):
        return upw.at[:, col(k * 2 + 1, LONG)]

    for i in range(3):
        send(lambda i=i: slab_in(near_core[i]), lambda i=i: in_slab.at[i], ("slab", i), near[i])
    for i in range(3):
        send(lambda i=i: long_in(near_core[i]), lambda i=i: in_long.at[i], ("long", i), near[i])

    for m, o in enumerate(offsets):
        to = (me.ctx + o) % 32
        place = rows_at((to % 2) * CAND + TOK + m * BLOCK, BLOCK, 64)
        send(lambda m=m: box.at[m], lambda place=place: c.at[place, :], ("offer", m), (me.dp, to))
    shared = [(lambda k: own, lambda k: c.at[crows_of(k, TOK), :]),
              (lambda k: bias2.at[crows_of(1 - k, CAND), :], lambda k: bias2.at[crows_of(k, CAND), :])]
    for i, (src, dst) in enumerate(pairs + shared):
        send(lambda src=src: src(1 - core), lambda dst=dst: dst(core), ("sib", i), sib)

    def offered_rows(k):
        return c.at[rows_at(k * CAND + TOK, 4 * BLOCK, TOK), :]

    my_rows = rows_at(me.z * 32, 32, 32)
    zrows = lambda o: rows_at(z_at[o % 8] * 32, 32, 32)
    at_z = lambda o: (me.dp, (z_at[o % 8] * 2 + me.xl) * 2 + core)

    def assemble(arrived, mine, width, name):
        stage[rows_at((me.xl * 2 + core) * 8, 8), 0:width] = mine.astype(f32)
        for i in range(3):
            got_it(arrived.at[i], (name, i))
            stage[rows_at(near_at[i] * 8, 8), 0:width] = arrived[i].astype(f32)
        return stage[:, 0:width].astype(bf)

    w[my_rows, cols_of(0, 0, 0)] = assemble(
        in_slab, upw[:, col(core * 16 + me.dp, WIDE)], WIDE, "slab")
    for o in range(1, 8):
        ref = lambda: w.at[my_rows, cols_of(0, 0, 0)]
        send(ref, ref, ("z", o), at_z(o))
    w[my_rows, LONG:] = assemble(in_long, upw[:, col(core * 2 + 1, LONG)], LONG, "long")

    lo, hi, whole = pl.ds(0, 128), pl.ds(128, 128), pl.ds(0, 256)
    sent_half = rows_at(me.xl * 128, 128, 128)
    got_half = rows_at((1 - me.xl) * 128, 128, 128)
    full_long = pl.ds(LONG, LONG)
    quarters = [pl.ds(LONG, LONG // 2), pl.ds(LONG + LONG // 2, LONG // 2)]

    def ring_ref(n, way):
        rows = zrows(8 - (n - 1) if way == 0 else n - 1)
        return w.at[rows, full_long if n < 4 else quarters[way]]

    def ring_in(n, way):
        rows = zrows(8 - n if way == 0 else n)
        return w.at[rows, full_long if n < 4 else quarters[way]]

    def along_z(f, n):
        if n == 1:
            need_block(0, 0, 0)
        for way in range(2):
            if n > 1:
                got_it(ring_in(n - 1, way), ("ring", n - 1, way))
            ref = lambda way=way: ring_ref(n, way)
            send(ref, ref, ("ring", n, way), at_z(1 if way == 0 else 7))

    for m in range(4):
        got_it(c.at[rows_at(core * CAND + TOK + m * BLOCK, BLOCK, 64), :], ("offer", m))
    send(lambda: offered_rows(core), lambda: offered_rows(core), "offer_on", sib)

    def weight_part(rows, side, step, name):
        got_it(w.at[rows, cols_of(0, side, step)], name)

    def need_block(f, side, step):
        if f == 1:
            for n in range(1, 5):
                for way in range(2):
                    got_it(ring_in(n, way), ("ring", n, way))
        elif side == 1:
            weight_part(got_half, 1, step, ("cross", step))
            weight_part(sent_half, 1, step, ("side", step))
        elif step == 0:
            for o in range(1, 8):
                got_it(w.at[zrows(8 - o), cols_of(0, 0, 0)], ("z", o))
        elif step == 2:
            weight_part(lo, 0, 2, "up2")
            weight_part(hi, 0, 2, "down2")
        else:
            weight_part(whole, 0, step, "up" if step == 3 else "down")

    def pass_on(rows, side, step, name, device):
        ref = lambda: w.at[rows, cols_of(0, side, step)]
        send(ref, ref, name, device)

    def along_y(f):
        need_block(0, 0, 0)
        pass_on(whole, 0, 0, "up", me.ring(1))
        pass_on(whole, 0, 0, "down", me.ring(3))

    def cross(f, step):
        need_block(0, 0, step)
        pass_on(sent_half, 0, step, ("cross", step), me.cross())

    def up(f):
        need_block(0, 0, 3)
        pass_on(lo, 0, 3, "up2", me.ring(1))

    def down(f):
        need_block(0, 0, 1)
        pass_on(hi, 0, 1, "down2", me.ring(3))

    def relay(f, step):
        weight_part(got_half, 1, step, ("cross", step))
        pass_on(got_half, 1, step, ("side", step), me.side())

    def add_x(f, step):
        at = f * 4 + step
        xsend[at] = acc[SLOT[f, 1, step], sent_half, :].astype(bf)
        send(lambda: xsend.at[at], lambda: xrecv.at[at], ("rx", at), me.side())

    def add_cross(f, step):
        at = f * 4 + step
        got_it(xrecv.at[at], ("rx", at))
        csend[at] = (acc[SLOT[f, 1, step], got_half, :] + xrecv[at].astype(f32)).astype(bf)
        send(lambda: csend.at[at], lambda: crecv.at[at], ("rc", at), me.cross())

    def crossed(f, step):
        at = f * 4 + step
        got_it(crecv.at[at], ("rc", at))
        acc[SLOT[f, 0, step], sent_half, :] += crecv[at].astype(f32)

    def add_y2(f):
        crossed(f, 2)
        for i, step in enumerate((1, 3)):
            at = f * 2 + i
            y2s[at] = acc[SLOT[f, 0, 2], i * 128:(i + 1) * 128, :].astype(bf)
            send(lambda at=at: y2s.at[at], lambda at=at: y2r.at[at], ("ry2", at), me.ring(step))

    def add_y1_far(f, i):
        step = (1, 3)[i]
        crossed(f, step)
        at = f * 4 + i * 2
        far = slice((1 - i) * 128, (2 - i) * 128)
        y1s[at] = acc[SLOT[f, 0, step], far, :].astype(bf)
        send(lambda: y1s.at[at], lambda: y1r.at[at], ("ry1", at), me.ring(step))

    def add_y1(f, i):
        step = (1, 3)[i]
        got_it(y2r.at[f * 2 + i], ("ry2", f * 2 + i))
        at = f * 4 + i * 2 + 1
        near_half = slice(i * 128, (i + 1) * 128)
        y1s[at] = (acc[SLOT[f, 0, step], near_half, :] + y2r[f * 2 + i].astype(f32)).astype(bf)
        send(lambda: y1s.at[at], lambda: y1r.at[at], ("ry1", at), me.ring(step))

    def add_z(f):
        slot = SLOT[f, 0, 0]
        crossed(f, 0)
        for at in range(f * 4, f * 4 + 4):
            got_it(y1r.at[at], ("ry1", at))
        for i in range(2):
            rows = slice(i * 128, (i + 1) * 128)
            near_in, far_in = f * 4 + i * 2 + 1, f * 4 + (1 - i) * 2
            acc[slot, rows, :] += y1r[near_in].astype(f32) + y1r[far_in].astype(f32)
        if f == 1:
            low[...] = acc[slot].astype(bf)
            for o in range(1, 16):
                send(lambda o=o: low.at[rows_at(chip_at[o] * 16, 16, 16), :], lambda o=o: low_in.at[o],
                     ("rz", f, o), me.in_ctx(chip_at[o], core))
            return
        for o in range(1, 8):
            send(lambda o=o: acc.at[slot, zrows(o), :], lambda o=o: zbuf.at[o], ("rz", f, o), at_z(o))

    def add_side(f):
        if f == 1:
            total = acc[SLOT[f, 0, 0], rows_at(chip * 16, 16, 16), :]
            for o in range(1, 16):
                got_it(low_in.at[o], ("rz", f, o))
                total = total + low_in[o].astype(f32)
            fin[f] = total
            return
        total = acc[SLOT[f, 0, 0], my_rows, :]
        for o in range(1, 8):
            got_it(zbuf.at[o], ("rz", f, o))
            total = total + zbuf[o]
        part[...] = total
        send(lambda: part.at[rows_at((1 - me.xl) * 16, 16, 16), :], lambda: side_in, "pair", me.side())

    def finish(f):
        if f == 0:
            got_it(side_in, "pair")
            fin[f] = part[rows_at(me.xl * 16, 16, 16), :] + side_in[...]
        for o in range(8):
            for k in range(2):
                if o == 0 and k == 0:
                    continue
                to = core if k == 0 else 1 - core
                send(lambda to=to: fin.at[f, rows_at(to * 8, 8), :], lambda: out_cols(f, core, me.dp),
                     ("w", f, o, k), ((me.dp + o) % 8, chip * 2 + to))

    def out_cols(f, k, r):
        return out_w.at[:, col(k * 16 + f * 8 + r, WIDE)]

    actions = dict(
        along_y=along_y, along_z=along_z, cross=cross, up=up, down=down, relay=relay, add_x=add_x,
        add_cross=add_cross, add_y2=add_y2, add_y1=add_y1,
        add_y1_far=add_y1_far, add_z=add_z, add_side=add_side,
        finish=finish, unit=need_block)
    before, events = [], []
    for op in PLAN:
        events.append(op)
        if op[0] == "unit":
            before.append(events)
            events = []
    after = events

    def act(ops):
        for name, *where in ops:
            actions[name](*where)

    for cp in local:
        cp.wait()
    for i, (_, dst) in enumerate(pairs + shared):
        got_it(dst(1 - core), ("sib", i))
    got_it(offered_rows(1 - core), "offer_on")
    zero = jnp.zeros((2 * CAND, ROPE), bf)
    rp = c[:, LAT:]
    rope_a[...] = jnp.concatenate([rp, zero], axis=1)
    rope_b[...] = jnp.concatenate([zero, rp], axis=1)
    ct[...] = c[:, :LAT].T
    lat[...] = jnp.zeros_like(lat)
    rope_acc[...] = jnp.zeros_like(rope_acc)
    lane = lax.broadcasted_iota(jnp.int32, (CAND, 128), 1)
    z128 = jnp.zeros((TOK, 128), bf)

    @pl.loop(0, 16)
    def _(s):
        for k, ops in enumerate(before):
            @pl.when(s == k)
            def _(ops=ops):
                act(ops)
        half, side, step = [
            sum((s == k).astype(jnp.int32) * u[i] for k, u in enumerate(UNITS) if u[i])
            for i in range(3)]
        xh = me.xh + side - 2 * me.xh * side
        p = half * 8 + xh * 4 + (me.y + step) % 4

        rcol = col(p, 128)
        pair = col(p, 512)
        hcol = [col(p * 2 + e, 128) for e in range(2)]
        keys = [slice(g * CAND, (g + 1) * CAND) for g in range(2)]
        qs = [slice(g * TOK, (g + 1) * TOK) for g in range(2)]
        expanded = mm(c[:, :LAT], w[:, pair]).astype(bf)
        kvs = [expanded[:, :256], expanded[:, 256:]]

        def kcat(g, e):
            rope = rope_a if e == 0 else rope_b
            return jnp.concatenate([kvs[e][keys[g], :128], rope[keys[g], :]], axis=1)

        def qcat(g, e):
            return jnp.concatenate([qn2[qs[g], hcol[e]], qr2[qs[g], rcol]], axis=1)

        both = []
        for g in range(2):
            gos = [go2[qs[g], hcol[e]] for e in range(2)]
            both.append(jnp.concatenate(
                [jnp.concatenate([gos[0], z128], axis=1),
                 jnp.concatenate([z128, gos[1]], axis=1)], axis=0))
        sg, low_p = {}, {}
        for g in range(2):
            vals = jnp.concatenate([kvs[0][keys[g], 128:], kvs[1][keys[g], 128:]], axis=1)
            dp_t = dg(vals, both[g], NT)
            scores = [dg(kcat(g, e), qcat(g, e), NT) for e in range(2)]
            for e in range(2):
                shift = bias2[keys[g], :].astype(f32) - lt2[g, pl.ds(p * 2 + e, 1), :]
                p_t = jnp.exp(scores[e] * SCALE + shift)
                d = dp_t[:, e * 128:(e + 1) * 128]
                rd = jnp.sum(p_t * d, axis=0, keepdims=True)
                sg[g, e] = (p_t * (d - rd)).astype(bf)
                low_p[g, e] = p_t.astype(bf)
        kgs = [[None, None], [None, None]]
        for g in range(2):
            vg = mm(jnp.concatenate([low_p[g, 0], low_p[g, 1]], axis=1), both[g]).astype(bf)
            rk = []
            for e in range(2):
                kg = mm(sg[g, e], qcat(g, e)) * SCALE
                rk.append(kg[:, 128:])
                kgs[e][g] = jnp.concatenate(
                    [kg[:, :128].astype(bf), vg[:, e * 128:(e + 1) * 128]], axis=1)
            rope_acc[keys[g], :] += jnp.where(lane < ROPE, rk[0], rk[1])
            turned = jnp.concatenate([sg[g, 0], sg[g, 1]], axis=1).T
            gr = None
            for e in range(2):
                gq = mm(turned[e * 128:(e + 1) * 128], kcat(g, e)) * SCALE
                gqn[qs[g], hcol[e]] = gq[:, :128].astype(bf)
                gr = gq[:, 128:] if gr is None else gr + gq[:, 128:]
            gqr[qs[g], rcol] = gr.astype(bf)
        kga = jnp.concatenate([jnp.concatenate(kgs[e], axis=0) for e in range(2)], axis=1)
        acc[s] = mm(ct[...], kga)
        for g in range(2):
            lat[keys[g], :] += dg(kga[keys[g]], w[:, pair], NT)

    last = after.index(("add_z", 1)) + 1
    act(after[:last])
    late = [op for op in after[last:] if op[1] == 1]
    ra = rope_acc[...]
    cg[...] = jnp.concatenate([lat[...], ra[:, :ROPE] + ra[:, ROPE:]], axis=1)
    send(lambda: cg.at[crows_of(1 - core, CAND), :], lambda: own2, "back_o", sib)
    act(op for op in after[last:] if op[1] == 0)

    got_it(own2, "back_o")
    mine = cg[crows_of(core, CAND), :] + own2[...]
    for m in range(4):
        cgl[m] = mine[TOK + m * BLOCK:TOK + (m + 1) * BLOCK].astype(bf)

    ncol = lambda k: out_n.at[:, col(k, 4096)]
    rcol_ = lambda k: out_r.at[:, col(k, 2048)]
    send(lambda: gqn.at[rows_of(1 - core), :], lambda: ncol(core), "back_n", sib)
    send(lambda: gqr.at[rows_of(1 - core), :], lambda: rcol_(core), "back_r", sib)
    first_late = len(local)
    copy(gqn.at[qrow, :], ncol(core))
    copy(gqr.at[qrow, :], rcol_(core))

    act(late)
    for m, o in enumerate(offsets):
        send(lambda m=m: cgl.at[m], lambda m=m: got.at[m], ("back", m), (me.dp, (me.ctx + 32 - o) % 32))

    first, second = mine[:BLOCK], mine[BLOCK:TOK]
    for m in range(4):
        got_it(got.at[m], ("back", m))
        rows = got[m].astype(f32)
        nil = jnp.zeros_like(rows)
        first = first + jnp.where(offer[m] == 0, rows, nil)
        second = second + jnp.where(offer[m] == 0, nil, rows)
    out_l[...] = jnp.concatenate([first, second], axis=0).T
    for f in range(2):
        copy(fin.at[f, rows_at(core * 8, 8), :], out_cols(f, core, me.dp))
    got_it(ncol(1 - core), "back_n")
    got_it(rcol_(1 - core), "back_r")
    for f in range(2):
        for o in range(8):
            for k in range(2):
                if o == 0 and k == 0:
                    continue
                who = core if k == 0 else 1 - core
                got_it(out_cols(f, who, (me.dp + 8 - o) % 8), ("w", f, o, k))
    for cp in local[first_late:]:
        cp.wait()
    for src, at in sends:
        rdma(src(), src(), ss.at[at], rs.at[0], sib).wait_send()
    assert sem.count == ARRIVALS, sem.count


def fused_call(selected, offered, qn, qr, go, lt, own_t, upw):
    bf, f32 = jnp.bfloat16, jnp.float32
    dma = pltpu.SemaphoreType.DMA
    v = pltpu.VMEM
    smem = pl.BlockSpec(memory_space=pltpu.SMEM)
    return pl.pallas_call(
        fused_kernel,
        out_shape=(
            jax.ShapeDtypeStruct((TOK, HEADS * NOPE), bf),
            jax.ShapeDtypeStruct((TOK, HEADS * ROPE), bf),
            jax.ShapeDtypeStruct((LAT + ROPE, TOK), f32),
            jax.ShapeDtypeStruct((8, 2 * HALF), f32),
        ),
        in_specs=[smem, smem] + [ANY] * 4 + [VMEM, VMEM],
        out_specs=(ANY, ANY, VMEM, ANY),
        scratch_shapes=[
            v((TOK, LAT + ROPE), bf), v((4, BLOCK, LAT + ROPE), bf),
            v((2 * TOK, 4096), bf), v((2 * TOK, 2048), bf), v((2 * TOK, 4096), bf),
            v((2, HALF_HEADS, TOK), f32), v((2 * CAND, LAT + ROPE), bf), v((2 * CAND, TOK), bf),
            v((LAT, HALF), bf), v((3, 8, WIDE), bf), v((3, 8, LONG), bf), v((32, LONG), f32),
            v((2 * TOK, 4096), bf), v((2 * TOK, 2048), bf),
            v((2 * CAND, LAT + ROPE), f32), v((4, BLOCK, LAT + ROPE), bf),
            v((4, BLOCK, LAT + ROPE), bf), v((CAND, LAT + ROPE), f32),
            v((2 * CAND, 128), bf), v((2 * CAND, 128), bf), v((LAT, 2 * CAND), bf),
            v((2 * CAND, LAT), f32), v((2 * CAND, 128), f32),
            v((16, LAT, WIDE), f32),
            v((8, 128, WIDE), bf), v((8, 128, WIDE), bf), v((8, 128, WIDE), bf),
            v((8, 128, WIDE), bf),
            v((4, 128, WIDE), bf), v((4, 128, WIDE), bf),
            v((8, 128, WIDE), bf), v((8, 128, WIDE), bf),
            v((8, 32, WIDE), f32), v((32, WIDE), f32), v((16, WIDE), f32),
            v((LAT, WIDE), bf), v((16, 16, WIDE), bf), v((2, 16, WIDE), f32),
            dma((SENDS,)), dma((ARRIVALS,)), dma((8,)),
        ],
        compiler_params=pltpu.CompilerParams(
            collective_id=0, has_side_effects=True, vmem_limit_bytes=56 << 20),
        name="fused_backward",
    )(selected, offered, qn, qr, go, lt, own_t, upw)


def hand_over_kernel(*refs):
    count = (len(refs) - 2) // 3
    sources, results, held = refs[:count], refs[count:2 * count], refs[2 * count:3 * count]
    sem_in, sem_out = refs[3 * count:]
    parts = []
    for src, dst, buf in zip(sources, results, held):
        pieces = src.shape[0] // 32 if src.shape[0] == TOK else 1
        size = src.shape[0] // pieces
        for i in range(pieces):
            rows = pl.ds(i * size, size)
            at = len(parts)
            parts.append((
                pltpu.make_async_copy(src.at[rows, :], buf.at[rows, :], sem_in.at[at]),
                pltpu.make_async_copy(buf.at[rows, :], dst.at[rows, :], sem_out.at[at])))
    for into, _ in parts:
        into.start()
    for into, out in parts:
        into.wait()
        out.start()
    for _, out in parts:
        out.wait()


def hand_over(*arrays):
    dma = pltpu.SemaphoreType.DMA
    return pl.pallas_call(
        hand_over_kernel,
        out_shape=tuple(jax.ShapeDtypeStruct(a.shape, a.dtype) for a in arrays),
        in_specs=[ANY] * len(arrays),
        out_specs=(ANY,) * len(arrays),
        scratch_shapes=[pltpu.VMEM(a.shape, a.dtype) for a in arrays] + [dma((10,)), dma((10,))],
        compiler_params=pltpu.CompilerParams(vmem_limit_bytes=60 << 20),
        name="hand_over",
    )(*arrays)


def shards(q_nope, q_rope, grad_out, log_total, kv_latent, up_weight, selected, offered):
    out_n, out_r, out_l, out_w = hand_over(*fused_call(
        selected[0], offered[0].T, q_nope[0], q_rope[0], grad_out[0], log_total[0], kv_latent[0].T,
        up_weight))
    return (out_n[None], out_r[None], out_l.T[None], out_w)


def solution(mesh):
    in_specs = (
        P("dp", "ctx", None),
        P("dp", "ctx", None),
        P("dp", "ctx", None),
        P("dp", None, "ctx"),
        P("dp", "ctx", None),
        P("ctx", None),
        P("dp", "ctx", None),
        P("dp", None, None),
    )
    out_specs = (P("dp", "ctx", None), P("dp", "ctx", None), P("dp", "ctx", None), P("ctx", None))
    return jax.shard_map(shards, mesh=mesh, in_specs=in_specs, out_specs=out_specs, check_vma=False)
```
